32 devices in a mesh: grp: 4 (over y, x), seq: 8 (over z, core).
Axes of the slice: x: 2, y: 2, z: 4, core: 2. Of those that a mesh axis runs over, the one named last changes fastest.
Arguments:
- layer_input: bfloat16 [8192, 1024], P(('grp', 'seq')), may hold values from -6 to 6
- segments: int32 [4, 2048], P('grp', 'seq'), may hold values from 0 to 2, never falling along the last dimension, each value on 1 to 2000 neighbouring positions
- ln_gain: bfloat16 [1024], P('seq'), may hold values from 0.5 to 1.5
- ln_bias: bfloat16 [1024], P('seq'), may hold values from -1.75 to 1.75
- w_value: bfloat16 [3072, 1024], P('seq'), may hold values from -0.1875 to 0.1875
- b_value: bfloat16 [3072], P('seq'), may hold values from -1.25 to 1.25
- w_reduce: bfloat16 [512, 1024], P('seq'), may hold values from -0.1875 to 0.1875
- b_reduce: bfloat16 [512], P('seq'), may hold values from -1.25 to 1.25
- lam_log: bfloat16 [512], P('seq'), may hold values from -2 to 0.5
- lam_freq: bfloat16 [512], P('seq'), may hold values from 0 to 50
- dss_w: bfloat16 [2, 512, 512], P(None, 'seq'), may hold values from -1.75 to 1.75
- log_step: bfloat16 [512], P('seq'), may hold values from -6.875 to -2.296875
- w_up: bfloat16 [3072, 512], P('seq'), may hold values from -0.5 to 0.5
- b_up: bfloat16 [3072], P('seq'), may hold values from -1.25 to 1.25
- w_out: bfloat16 [1024, 3072], P('seq'), may hold values from -0.21875 to 0.21875
- b_out: bfloat16 [1024], P('seq'), may hold values from -1.25 to 1.25
- out_cotangent: bfloat16 [8192, 1024], P(('grp', 'seq')), may hold values from -6 to 6
Outputs:
- layer_output: bfloat16 [8192, 1024], P(('grp', 'seq'))
- grad_input: float32 [8192, 1024], P(('grp', 'seq'))
- grad_ln_gain: float32 [1024], P('seq')
- grad_ln_bias: float32 [1024], P('seq')
- grad_w_value: float32 [3072, 1024], P('seq')
- grad_b_value: float32 [3072], P('seq')
- grad_w_reduce: float32 [512, 1024], P('seq')
- grad_b_reduce: float32 [512], P('seq')
- grad_lam_log: float32 [512], P('seq')
- grad_lam_freq: float32 [512], P('seq')
- grad_dss_w: float32 [2, 512, 512], P(None, 'seq')
- grad_log_step: float32 [512], P('seq')
- grad_w_up: float32 [3072, 512], P('seq')
- grad_b_up: float32 [3072], P('seq')
- grad_w_out: float32 [1024, 3072], P('seq')
- grad_b_out: float32 [1024], P('seq')
The draws below stay inside these ranges and needn't reach their ends.
Inputs may be any that keep to these rules, and one draw needn't show every extreme that they name: `segments`: along each sequence the segment numbers never fall; every segment covers at most 2000 consecutive positions and one covers exactly 2000.
All inputs are finite; a program needn't handle non-finite values.
Results may differ from the reference program's by a relative error of at most 0.0077.
Values may be sent and summed in bfloat16 or wider, within the bound.
No kernel may reach another device: no remote copies, remote signals or barrier semaphores. Data moves between devices by JAX's collectives and lax.ppermute only.
A program may use at most 320 MiB of HBM per device.

```python
import math
import jax
import jax.numpy as jnp
import numpy as np
from jax import lax

D = 1024
F = 3072
H = 512
STATE = 512
MOST = 2000
LEN = 2048
DOCS = 3
TOKENS = 8192
N_GRP = 4


def shard_levels(own_key, extent, split, smallest, high):
    def one(dim, parts):
        draws = jax.random.uniform(jax.random.fold_in(jax.random.fold_in(own_key, 6), dim), (parts,), jnp.float32, smallest / len(split), high / len(split))
        return jnp.repeat(jnp.exp(draws), extent[dim] // parts).reshape((-1,) + (1,) * (len(extent) - dim - 1))

    factor_of = one(*split[0])
    for cut in split[1:]:
        factor_of = factor_of * one(*cut)
    return factor_of


def length_profile(amount, total, reach, skew):
    portions = [(1 << 20) // math.isqrt(rank ** skew) + 1 for rank in range(2, amount + 1)]
    spare, given = total - reach - (amount - 1), [1] * (amount - 1)
    while spare > 0:
        candidates = [i for i in range(amount - 1) if given[i] < reach]
        mass, remaining = sum([portions[i] for i in candidates]), spare
        for i in candidates:
            addition = min(reach - given[i], max(1, remaining * portions[i] // mass), spare)
            given[i] = given[i] + addition
            spare = spare - addition
    return np.array([reach] + given)


def ragged_sizes(own_key, amount, total, limit, lean):
    if amount == 2:
        one = jax.random.randint(own_key, (), max(1, total - limit), min(limit, total - 1) + 1)
        return jnp.stack([one, total - one])
    tallies = jnp.asarray(length_profile(amount, total, limit, lean), jnp.int32)
    twos = (amount - 1) // 2
    donor, taker = tallies[1:1 + 2 * twos:2], tallies[2:2 + 2 * twos:2]
    slack = jnp.minimum(donor - 1, limit - taker)
    moved = jax.random.randint(jax.random.fold_in(own_key, 1), (twos,), 0, 1 << 20) % (slack + 1)
    tallies = tallies.at[1:1 + 2 * twos:2].set(donor - moved).at[2:2 + 2 * twos:2].set(taker + moved)
    return tallies[jax.random.permutation(jax.random.fold_in(own_key, 2), amount)]


def bell_draw(rng, extent, width, most, cuts=(), held_as=jnp.bfloat16):
    gain = shard_levels(rng, extent, cuts, -0.22, 0.18) if cuts else 1.0
    drawn = jax.random.normal(rng, extent, jnp.float32) * width * gain
    return jnp.minimum(jnp.maximum(drawn, -most), most).astype(held_as)


def setup_inputs(seed: int = 0) -> dict:
    keys = jax.random.split(jax.random.key(seed), 18)
    layer_input = bell_draw(keys[0], (TOKENS, D), 1.0, 6.0, ((0, 32),))
    segments = jax.vmap(lambda own: jnp.searchsorted(jnp.cumsum(ragged_sizes(own, DOCS, LEN, MOST, 0)), jnp.arange(LEN), side="right"))(jax.random.split(keys[1], N_GRP)).reshape((N_GRP, LEN)).astype(jnp.int32)
    ln_gain = jnp.clip(1.0 + 0.1 * jax.random.normal(keys[2], (D,), jnp.float32), 0.5, 1.5).astype(jnp.bfloat16)
    ln_bias = bell_draw(keys[3], (D,), 0.3, 1.75, ((0, 8),))
    w_value = bell_draw(keys[4], (F, D), D ** -0.5, 0.1875, ((0, 8),))
    b_value = bell_draw(keys[5], (F,), 0.2, 1.25, ((0, 8),))
    w_reduce = bell_draw(keys[6], (H, D), D ** -0.5, 0.1875, ((0, 8),))
    b_reduce = bell_draw(keys[7], (H,), 0.2, 1.25, ((0, 8),))
    lam_log = jnp.clip(-2.0 + 2.5 * jax.random.uniform(keys[8], (STATE,), jnp.float32) ** shard_levels(keys[8], (STATE,), ((0, 8),), -0.2, 0.2), -2.0, 0.5).astype(jnp.bfloat16)
    lam_freq = jnp.clip(50.0 * jax.random.uniform(keys[9], (STATE,), jnp.float32) ** shard_levels(keys[9], (STATE,), ((0, 8),), -0.2, 0.2), 0.0, 50.0).astype(jnp.bfloat16)
    dss_w = bell_draw(keys[10], (2, H, STATE), 0.3, 1.75, ((1, 8),))
    log_step = jnp.clip(-6.875 + 4.578125 * jax.random.uniform(keys[11], (H,), jnp.float32) ** shard_levels(keys[11], (H,), ((0, 8),), -0.2, 0.2), -6.875, -2.296875).astype(jnp.bfloat16)
    w_up = bell_draw(keys[12], (F, H), (H // 4) ** -0.5, 0.5, ((0, 8),))
    b_up = bell_draw(keys[13], (F,), 0.2, 1.25, ((0, 8),))
    w_out = bell_draw(keys[14], (D, F), (F // 4) ** -0.5, 0.21875, ((0, 8),))
    b_out = bell_draw(keys[15], (D,), 0.2, 1.25, ((0, 8),))
    out_cotangent = bell_draw(keys[16], (TOKENS, D), 1.0, 6.0, ((0, 32),))
    return {"layer_input": layer_input, "segments": segments, "ln_gain": ln_gain, "ln_bias": ln_bias, "w_value": w_value, "b_value": b_value, "w_reduce": w_reduce, "b_reduce": b_reduce, "lam_log": lam_log, "lam_freq": lam_freq, "dss_w": dss_w, "log_step": log_step, "w_up": w_up, "b_up": b_up, "w_out": w_out, "b_out": b_out, "out_cotangent": out_cotangent}


@jax.custom_vjp
def low(v):
    return lax.optimization_barrier(v.astype(jnp.bfloat16)).astype(jnp.float32)

@jax.custom_vjp
def low_back(v):
    return v

def low_keep(v):
    return (low(v), None)

def low_pass(kept, grad):
    return (grad,)

def back_keep(v):
    return (v, None)

def back_low(kept, grad):
    return (low(grad),)
low.defvjp(low_keep, low_pass)
low_back.defvjp(back_keep, back_low)
epsilon = 1e-05
highest = lax.Precision.HIGHEST

def make_taps(lam_log, lam_freq, dss_w, log_step):
    lag_steps = jnp.arange(MOST).astype(jnp.float32)
    lam_real = -jnp.exp(lam_log)
    lam_imag = lam_freq
    modulus = lam_real * lam_real + lam_imag * lam_imag
    groups = H // 16

    def group_taps(pieces):
        weight_re, weight_im, step_log = pieces
        delta = jnp.exp(step_log)[:, None]
        decay_re = delta * lam_real[None, :]
        decay_im = delta * lam_imag[None, :]
        growth = jnp.exp(decay_re)
        shift_re = growth * jnp.cos(decay_im) - 1.0
        shift_im = growth * jnp.sin(decay_im)
        ratio_re = (shift_re * lam_real + shift_im * lam_imag) / modulus
        ratio_im = (shift_im * lam_real - shift_re * lam_imag) / modulus
        coeff_re = weight_re * ratio_re - weight_im * ratio_im
        coeff_im = weight_re * ratio_im + weight_im * ratio_re
        magnitude = jnp.exp(decay_re[:, :, None] * lag_steps)
        phase = decay_im[:, :, None] * lag_steps
        return lax.optimization_barrier(jnp.sum(magnitude * (coeff_re[:, :, None] * jnp.cos(phase) - coeff_im[:, :, None] * jnp.sin(phase)), axis=1))
    filter_taps = lax.map(jax.checkpoint(group_taps), (dss_w[0].reshape(groups, 16, STATE), dss_w[1].reshape(groups, 16, STATE), log_step.reshape(groups, 16)))
    return filter_taps.reshape(H, MOST)

def doc_conv(reduced_t, segment_row, filter_taps):
    doc_numbers = jnp.arange(DOCS).astype(jnp.int32)
    starts = lax.optimization_barrier(jnp.sum((segment_row[None, :] < doc_numbers[:, None]).astype(jnp.int32), axis=1))
    counts = lax.optimization_barrier(jnp.sum((segment_row[None, :] == doc_numbers[:, None]).astype(jnp.int32), axis=1))
    offsets = jnp.arange(MOST).astype(jnp.int32)
    inside = offsets[None, :] < counts[:, None]
    source = jnp.minimum(starts[:, None] + offsets[None, :], LEN - 1)
    per_doc = jnp.where(inside[None, :, :], reduced_t[:, source], 0.0)
    length = 2 * MOST
    spectrum = jnp.fft.rfft(per_doc, n=length, axis=-1) * jnp.fft.rfft(filter_taps, n=length, axis=-1)[:, None, :]
    convolved = jnp.fft.irfft(spectrum, n=length, axis=-1)[:, :, :MOST]
    places = jnp.arange(LEN).astype(jnp.int32)
    target = segment_row * MOST + places - starts[segment_row]
    return convolved.reshape(H, DOCS * MOST)[:, target]

def block_layer(x_row, segment_row, params, filter_taps):
    ln_gain, ln_bias, w_value, b_value, w_reduce, b_reduce, w_up, b_up, w_out, b_out = params
    center = x_row - lax.optimization_barrier(jnp.mean(x_row, axis=-1, keepdims=True))
    spread = lax.optimization_barrier(jnp.mean(center * center, axis=-1, keepdims=True))
    normed = low(center * lax.rsqrt(spread + epsilon) * ln_gain + ln_bias)
    pre_value = low_back(jnp.dot(normed, w_value.T, precision=highest) + b_value)
    activated = jax.nn.gelu(pre_value)
    pre_reduce = low_back(jnp.dot(normed, w_reduce.T, precision=highest) + b_reduce)
    reduced = low_back(low(jax.nn.gelu(pre_reduce)))
    mixed = low_back(low(doc_conv(reduced.T, segment_row, filter_taps).T))
    pre_up = low_back(jnp.dot(mixed, w_up.T, precision=highest) + b_up)
    gated = low(activated * pre_up)
    return x_row + jnp.dot(gated, w_out.T, precision=highest) + b_out

def reference(layer_input, segments, ln_gain, ln_bias, w_value, b_value, w_reduce, b_reduce, lam_log, lam_freq, dss_w, log_step, w_up, b_up, w_out, b_out, out_cotangent):

    def widen(array):
        return array.astype(jnp.float32)
    params = (widen(ln_gain), widen(ln_bias), widen(w_value), widen(b_value), widen(w_reduce), widen(b_reduce), widen(w_up), widen(b_up), widen(w_out), widen(b_out))

    def forward(x_full, layer_params, decay_log, frequency, weights, step_log):
        filter_taps = make_taps(decay_log, frequency, weights, step_log)

        def one_sequence(operands):
            return block_layer(operands[0], operands[1], layer_params, filter_taps)
        results = lax.map(jax.checkpoint(one_sequence), (x_full.reshape(N_GRP, LEN, D), segments))
        return results.reshape(N_GRP * LEN, D)
    output, pullback = jax.vjp(forward, widen(layer_input), params, widen(lam_log), widen(lam_freq), widen(dss_w), widen(log_step))
    grad_input, grad_params, grad_lam_log, grad_lam_freq, grad_dss_w, grad_log_step = pullback(widen(out_cotangent))
    g_gain, g_bias, g_w_value, g_b_value, g_w_reduce, g_b_reduce, g_w_up, g_b_up, g_w_out, g_b_out = grad_params
    return (output.astype(jnp.bfloat16), grad_input, g_gain, g_bias, g_w_value, g_b_value, g_w_reduce, g_b_reduce, grad_lam_log, grad_lam_freq, grad_dss_w, grad_log_step, g_w_up, g_b_up, g_w_out, g_b_out)
```

```python
import functools

import jax
import jax.numpy as jnp
from jax import lax
from jax.experimental import pallas as pl
from jax.experimental.pallas import tpu as pltpu
from jax.sharding import PartitionSpec as P

f32, bf16 = jnp.float32, jnp.bfloat16
TILE = 128
MOST = 2000
LAGS = 2048
ROWS = 8
NT = (((1,), (1,)), ((), ()))
TN = (((0,), (0,)), ((), ()))


def params(mb=56):
    return pltpu.CompilerParams(vmem_limit_bytes=mb << 20)


def lag_blocks(length):
    return min(length // TILE, (MOST + TILE - 2) // TILE + 1)


def doc_count(length):
    return length // 1024 + 1


def cmul(a, b):
    return (a[0] * b[0] - a[1] * b[1], a[0] * b[1] + a[1] * b[0])


def mode_rates(lam_log_ref, lam_freq_ref, step_ref):
    lam_re = -jnp.exp(lam_log_ref[...])
    lam_im = lam_freq_ref[...]
    delta = jnp.exp(step_ref[...])
    return lam_re, lam_im, delta


def first_power(lam_re, lam_im, delta):
    growth = jnp.exp(delta * lam_re)
    phase = delta * lam_im
    return growth * jnp.cos(phase), growth * jnp.sin(phase)


def store_squares(one, sq_ref):
    cur = one
    for k in range(11):
        sq_ref[0, k], sq_ref[1, k] = cur
        if k < 10:
            cur = cmul(cur, cur)


def power_tiles(sq_ref, c, first, count):
    def sq(k):
        return sq_ref[0, k, pl.ds(c, 1), :], sq_ref[1, k, pl.ds(c, 1), :]

    width = sq_ref.shape[-1]
    row = lax.broadcasted_iota(jnp.int32, (8, width), 0)
    tile = None
    for k in range(3):
        re, im = sq(first + k)
        on = (row & (1 << k)) != 0
        term = jnp.where(on, re, 1.0), jnp.where(on, im, 0.0)
        tile = term if tile is None else cmul(tile, term)
    tiles, k = [tile], 3
    while len(tiles) < count:
        step = sq(first + k)
        tiles = tiles + [cmul(t, step) for t in tiles]
        k += 1
    return tiles


def split(x):
    hi = x.astype(bf16)
    return hi, (x - hi.astype(f32)).astype(bf16)


def store_fine(sq_ref, c, qh_ref, ql_ref):
    width = sq_ref.shape[-1]
    for t, pair in enumerate(power_tiles(sq_ref, c, 0, TILE // 8)):
        if t % 2 == 0:
            held = pair
            continue
        for part in range(2):
            hi, lo = split(jnp.concatenate([held[part], pair[part]], axis=0))
            qh_ref[8 * t - 8 : 8 * t + 8, part * width : (part + 1) * width] = hi
            ql_ref[8 * t - 8 : 8 * t + 8, part * width : (part + 1) * width] = lo


def taps_kernel(lam_log_ref, lam_freq_ref, w_ref, step_ref, tt_ref, sq_ref, cf_ref, qh_ref, ql_ref, p_ref):
    lam_re, lam_im, delta = mode_rates(lam_log_ref, lam_freq_ref, step_ref)
    one = first_power(lam_re, lam_im, delta)
    store_squares(one, sq_ref)
    modulus = lam_re * lam_re + lam_im * lam_im
    shift_re, shift_im = one[0] - 1.0, one[1]
    ratio = (
        (shift_re * lam_re + shift_im * lam_im) / modulus,
        (shift_im * lam_re - shift_re * lam_im) / modulus,
    )
    cf_ref[0], cf_ref[1] = cmul((w_ref[0], w_ref[1]), ratio)
    width = sq_ref.shape[-1]
    deep = tt_ref.shape[1]
    coarse = LAGS // TILE

    def channel(c, _):
        store_fine(sq_ref, c, qh_ref, ql_ref)
        coeff = cf_ref[0, pl.ds(c, 1), :], cf_ref[1, pl.ds(c, 1), :]
        tiles = [cmul(t, coeff) for t in power_tiles(sq_ref, c, 7, coarse // 8)]
        for part, sign in ((0, 1.0), (1, -1.0)):
            hi, lo = split(sign * jnp.concatenate([t[part] for t in tiles], axis=0))
            p_ref[:coarse, part * width : (part + 1) * width] = hi
            p_ref[coarse:, part * width : (part + 1) * width] = lo
        both = lax.dot_general(p_ref[...], qh_ref[...], NT, preferred_element_type=f32)
        low = lax.dot_general(p_ref[:coarse], ql_ref[...], NT, preferred_element_type=f32)
        taps = both[:coarse] + both[coarse:] + low
        empty = jnp.zeros((TILE, TILE), f32)
        pieces = [empty] + [
            jnp.broadcast_to(taps[d : d + 1], (TILE, TILE)) if d < coarse else empty for d in range(deep)
        ]
        skew = pltpu.roll(jnp.concatenate(pieces, axis=1), 0, 1, stride=1, stride_axis=0)
        for d in range(deep):
            tt_ref[c, d] = skew[:, (d + 1) * TILE : (d + 2) * TILE].astype(bf16)
        return 0

    lax.fori_loop(0, ROWS, channel, 0)


def make_toeplitz(lam_log, lam_freq, weights, log_step, deep):
    channels, modes = weights.shape[1:]
    return pl.pallas_call(
        taps_kernel,
        grid=(channels // ROWS,),
        in_specs=[
            pl.BlockSpec((1, modes), lambda i: (0, 0)),
            pl.BlockSpec((1, modes), lambda i: (0, 0)),
            pl.BlockSpec((2, ROWS, modes), lambda i: (0, i, 0)),
            pl.BlockSpec((ROWS, 1), lambda i: (i, 0)),
        ],
        out_specs=pl.BlockSpec((ROWS, deep, TILE, TILE), lambda i: (i, 0, 0, 0)),
        out_shape=jax.ShapeDtypeStruct((channels, deep, TILE, TILE), bf16),
        scratch_shapes=[
            pltpu.VMEM((2, 11, ROWS, modes), f32),
            pltpu.VMEM((2, ROWS, modes), f32),
            pltpu.VMEM((TILE, 2 * modes), bf16),
            pltpu.VMEM((TILE, 2 * modes), bf16),
            pltpu.VMEM((2 * LAGS // TILE, 2 * modes), bf16),
        ],
        compiler_params=params(),
    )(lam_log[None], lam_freq[None], weights, log_step[:, None])


def conv_kernel(docs, seg_ref, x_ref, tt_ref, y_ref, xs_ref, xw_ref):
    blocks, deep = x_ref.shape[1], tt_ref.shape[1]
    lead = deep - 1
    seg = seg_ref[...]
    for u in range(xs_ref.shape[0]):
        for k in range(docs):
            xs_ref[u, k, :lead, :] = jnp.zeros((lead, TILE), f32)

    def one(c, u):
        x = x_ref[c].astype(f32)
        for k in range(docs):
            xs_ref[u, k, lead:, :] = jnp.where(seg == k, x, 0.0)
        for k in range(docs):
            for d in range(deep):
                xw_ref[u, k * blocks : (k + 1) * blocks, d * TILE : (d + 1) * TILE] = xs_ref[
                    u, k, lead - d : lead - d + blocks, :
                ].astype(bf16)
        y = jnp.dot(xw_ref[u], tt_ref[c].reshape(deep * TILE, TILE), preferred_element_type=f32)
        out = jnp.zeros((blocks, TILE), f32)
        for k in range(docs):
            out = jnp.where(seg == k, y[k * blocks : (k + 1) * blocks], out)
        y_ref[c] = out.astype(bf16)

    def pair(i, _):
        for u in range(xs_ref.shape[0]):
            one(i * xs_ref.shape[0] + u, u)
        return 0

    lax.fori_loop(0, ROWS // xs_ref.shape[0], pair, 0)


def conv(seg, x, tt, unroll=2):
    channels, blocks, _ = x.shape
    deep = tt.shape[1]
    docs = doc_count(blocks * TILE)
    return pl.pallas_call(
        functools.partial(conv_kernel, docs),
        grid=(channels // ROWS,),
        in_specs=[
            pl.BlockSpec((blocks, TILE), lambda i: (0, 0)),
            pl.BlockSpec((ROWS, blocks, TILE), lambda i: (i, 0, 0)),
            pl.BlockSpec((ROWS, deep, TILE, TILE), lambda i: (i, 0, 0, 0)),
        ],
        out_specs=pl.BlockSpec((ROWS, blocks, TILE), lambda i: (i, 0, 0)),
        out_shape=jax.ShapeDtypeStruct(x.shape, bf16),
        scratch_shapes=[
            pltpu.VMEM((unroll, docs, blocks + deep - 1, TILE), f32),
            pltpu.VMEM((unroll, docs * blocks, deep * TILE), bf16),
        ],
        compiler_params=params(),
    )(seg, x, tt)


def back_kernel(docs, seg_ref, flip_ref, x_ref, g_ref, tt_ref, gx_ref, dt_ref, gs_ref, gw_ref, xst_ref):
    blocks, deep = x_ref.shape[1], tt_ref.shape[1]
    lead = deep - 1
    seg = seg_ref[...]
    for u in range(gs_ref.shape[0]):
        for k in range(docs):
            gs_ref[u, k, blocks:, :] = jnp.zeros((lead, TILE), f32)

    def one(c, u):
        g = g_ref[c].astype(f32)
        x = x_ref[c].astype(f32)
        for k in range(docs):
            gs_ref[u, k, :blocks, :] = jnp.where(seg == k, g, 0.0)
            xst_ref[u, k * blocks : (k + 1) * blocks, :] = jnp.where(seg == k, x, 0.0).astype(bf16)
        for k in range(docs):
            for d in range(deep):
                gw_ref[u, k * blocks : (k + 1) * blocks, d * TILE : (d + 1) * TILE] = gs_ref[
                    u, k, d : d + blocks, :
                ].astype(bf16)
        gx = jnp.zeros((docs * blocks, TILE), f32)
        for d in range(deep):
            gx += lax.dot_general(
                gw_ref[u, :, d * TILE : (d + 1) * TILE], tt_ref[c, d], NT, preferred_element_type=f32
            )
        out = jnp.zeros((blocks, TILE), f32)
        for k in range(docs):
            out = jnp.where(seg == k, gx[k * blocks : (k + 1) * blocks], out)
        gx_ref[c] = out.astype(bf16)
        xr = jnp.dot(xst_ref[u], flip_ref[...], preferred_element_type=f32).astype(bf16)
        wide = lax.dot_general(xr, gw_ref[u], TN, preferred_element_type=f32)
        wide = jnp.concatenate([wide, jnp.zeros((TILE, TILE), f32)], axis=1)
        flat = pltpu.roll(wide, wide.shape[1] - (TILE - 1), 1, stride=1, stride_axis=0)
        dt_ref[pl.ds(c, 1), :] = jnp.sum(flat[:, : LAGS], axis=0, keepdims=True)

    def pair(i, _):
        for u in range(gs_ref.shape[0]):
            one(i * gs_ref.shape[0] + u, u)
        return 0

    lax.fori_loop(0, ROWS // gs_ref.shape[0], pair, 0)


def conv_back(seg, x, g, tt, unroll=2):
    channels, blocks, _ = x.shape
    deep = tt.shape[1]
    docs = doc_count(blocks * TILE)
    flip = jnp.eye(TILE, dtype=bf16)[::-1]
    rows = pl.BlockSpec((ROWS, blocks, TILE), lambda i: (i, 0, 0))
    return pl.pallas_call(
        functools.partial(back_kernel, docs),
        grid=(channels // ROWS,),
        in_specs=[
            pl.BlockSpec((blocks, TILE), lambda i: (0, 0)),
            pl.BlockSpec((TILE, TILE), lambda i: (0, 0)),
            rows,
            rows,
            pl.BlockSpec((ROWS, deep, TILE, TILE), lambda i: (i, 0, 0, 0)),
        ],
        out_specs=[rows, pl.BlockSpec((ROWS, LAGS), lambda i: (i, 0))],
        out_shape=[jax.ShapeDtypeStruct(x.shape, bf16), jax.ShapeDtypeStruct((channels, LAGS), f32)],
        scratch_shapes=[
            pltpu.VMEM((unroll, docs, blocks + deep - 1, TILE), f32),
            pltpu.VMEM((unroll, docs * blocks, deep * TILE), bf16),
            pltpu.VMEM((unroll, docs * blocks, TILE), bf16),
        ],
        compiler_params=params(),
    )(seg, flip, x, g, tt)


def mode_grad_kernel(
    lam_log_ref, lam_freq_ref, w_ref, step_ref, dt_ref, gw_ref, gstep_ref, glam_ref, sq_ref, qh_ref, ql_ref, l_ref, s_ref
):
    lam_re, lam_im, delta = mode_rates(lam_log_ref, lam_freq_ref, step_ref)
    one = first_power(lam_re, lam_im, delta)
    store_squares(one, sq_ref)
    width = sq_ref.shape[-1]
    coarse = LAGS // TILE

    def channel(c, _):
        store_fine(sq_ref, c, qh_ref, ql_ref)
        dt = dt_ref[c]
        lane = lax.broadcasted_iota(jnp.int32, (coarse, TILE), 1).astype(f32)
        hi, lo = split(jnp.concatenate([dt, dt * lane], axis=0))
        l_ref[: 2 * coarse] = hi
        l_ref[2 * coarse :] = lo
        both = jnp.dot(l_ref[...], qh_ref[...], preferred_element_type=f32)
        low = jnp.dot(l_ref[: 2 * coarse], ql_ref[...], preferred_element_type=f32)
        v = both[: 2 * coarse] + both[2 * coarse :] + low
        tiles = power_tiles(sq_ref, c, 7, coarse // 8)
        power = tuple(jnp.concatenate([t[part] for t in tiles], axis=0) for part in range(2))
        v0 = v[:coarse, :width], v[:coarse, width:]
        row = lax.broadcasted_iota(jnp.int32, (coarse, width), 0).astype(f32) * float(TILE)
        v1 = tuple(row * v0[part] + v[coarse:, part * width : (part + 1) * width] for part in range(2))
        for n, pair in enumerate((v0, v1)):
            prod = cmul(power, pair)
            for part in range(2):
                s_ref[2 * n + part, pl.ds(c, 1), :] = jnp.sum(prod[part], axis=0, keepdims=True)
        return 0

    lax.fori_loop(0, ROWS, channel, 0)
    modulus = lam_re * lam_re + lam_im * lam_im
    inv = lam_re / modulus, -lam_im / modulus
    shift = one[0] - 1.0, one[1]
    ratio = cmul(shift, inv)
    w = w_ref[0], w_ref[1]
    s0 = s_ref[0], s_ref[1]
    s1 = s_ref[2], s_ref[3]
    coeff = cmul(w, ratio)
    gw = cmul(s0, ratio)
    gw_ref[0], gw_ref[1] = gw[0], -gw[1]
    near = cmul(s0, cmul(w, cmul(one, inv)))
    far = cmul(coeff, s1)
    z = near[0] + far[0], near[1] + far[1]
    back = cmul(s0, cmul(coeff, inv))
    big = delta * z[0] - back[0], delta * z[1] - back[1]
    step = jnp.sum((z[0] * lam_re - z[1] * lam_im) * delta, axis=1, keepdims=True)
    gstep_ref[...] = jnp.broadcast_to(step, gstep_ref.shape)

    @pl.when(pl.program_id(0) == 0)
    def _():
        glam_ref[...] = jnp.zeros(glam_ref.shape, f32)

    glam_ref[0] += big[0] * lam_re
    glam_ref[1] -= big[1]


def mode_grads(lam_log, lam_freq, weights, log_step, dt):
    channels, modes = weights.shape[1:]
    coarse = LAGS // TILE
    gw, gstep, glam = pl.pallas_call(
        mode_grad_kernel,
        grid=(channels // ROWS,),
        in_specs=[
            pl.BlockSpec((1, modes), lambda i: (0, 0)),
            pl.BlockSpec((1, modes), lambda i: (0, 0)),
            pl.BlockSpec((2, ROWS, modes), lambda i: (0, i, 0)),
            pl.BlockSpec((ROWS, 1), lambda i: (i, 0)),
            pl.BlockSpec((ROWS, coarse, TILE), lambda i: (i, 0, 0)),
        ],
        out_specs=[
            pl.BlockSpec((2, ROWS, modes), lambda i: (0, i, 0)),
            pl.BlockSpec((ROWS, TILE), lambda i: (i, 0)),
            pl.BlockSpec((2, ROWS, modes), lambda i: (0, 0, 0)),
        ],
        out_shape=[
            jax.ShapeDtypeStruct((2, channels, modes), f32),
            jax.ShapeDtypeStruct((channels, TILE), f32),
            jax.ShapeDtypeStruct((2, ROWS, modes), f32),
        ],
        scratch_shapes=[
            pltpu.VMEM((2, 11, ROWS, modes), f32),
            pltpu.VMEM((TILE, 2 * modes), bf16),
            pltpu.VMEM((TILE, 2 * modes), bf16),
            pltpu.VMEM((4 * coarse, TILE), bf16),
            pltpu.VMEM((4, ROWS, modes), f32),
        ],
        compiler_params=params(),
    )(lam_log[None], lam_freq[None], weights, log_step[:, None], dt.reshape(channels, coarse, TILE))
    return gw, gstep[:, 0], jnp.sum(glam, axis=1)


epsilon = 1e-05
contract_last = (((1,), (1,)), ((), ()))
contract_first = (((0,), (0,)), ((), ()))


def swap(x, k, n_grp):
    return x if k == 0 else lax.ppermute(x, "grp", [(i, i ^ k) for i in range(n_grp)])


def gather_grp(x, n_grp):
    return [swap(x, k, n_grp) for k in range(n_grp)]


def sum_scatter_grp(pieces, n_grp):
    total = pieces[0].astype(f32)
    for k in range(1, n_grp):
        total = total + swap(pieces[k].astype(bf16), k, n_grp).astype(f32)
    return total


def place_grp(x, n_grp, me, axis):
    held = jnp.stack(gather_grp(x, n_grp))
    order = jnp.arange(n_grp, dtype=jnp.int32) ^ me
    rows = [lax.dynamic_index_in_dim(held, order[j], 0, keepdims=False) for j in range(n_grp)]
    return jnp.stack(rows, axis=axis)


def body(
    n_grp,
    n_seq,
    layer_input,
    segments,
    ln_gain,
    ln_bias,
    w_value,
    b_value,
    w_reduce,
    b_reduce,
    lam_log,
    lam_freq,
    dss_w,
    log_step,
    w_up,
    b_up,
    w_out,
    b_out,
    out_cotangent,
):
    me = lax.axis_index("grp")
    tokens, wide = layer_input.shape
    part = w_value.shape[0] // n_grp
    quarter = n_seq * part
    reduced_width = w_reduce.shape[0] * n_seq

    small = (ln_gain, ln_bias, b_value, b_reduce, lam_log, lam_freq, b_up, b_out, segments[0].astype(bf16))
    packed = lax.all_gather(jnp.concatenate(small), "seq", axis=0)
    spots, fulls = 0, []
    for array in small:
        fulls.append(packed[:, spots : spots + array.shape[0]])
        spots += array.shape[0]
    gain_full, bias_full, value_bias, reduce_bias, decay_full, freq_full, up_bias, out_bias, doc_row = fulls
    gain_wide = gain_full.reshape(-1).astype(f32)
    bias_wide = bias_full.reshape(-1).astype(f32)
    value_bias = lax.dynamic_slice_in_dim(value_bias, me * part, part, 1).reshape(-1).astype(f32)
    up_bias = lax.dynamic_slice_in_dim(up_bias, me * part, part, 1).reshape(-1).astype(f32)

    reduce_full = lax.all_gather(w_reduce, "seq", axis=0, tiled=True)
    up_part = lax.all_gather(lax.dynamic_slice_in_dim(w_up, me * part, part, 0), "seq", axis=0, tiled=True)
    value_part = lax.all_gather(lax.dynamic_slice_in_dim(w_value, me * part, part, 0), "seq", axis=0, tiled=True)
    out_cols = lax.dynamic_index_in_dim(w_out.reshape(-1, n_seq, n_grp, part), me, 2, keepdims=False)
    out_part = lax.all_gather(out_cols.reshape(-1, quarter), "seq", axis=0, tiled=True)

    modes = (
        decay_full.reshape(-1).astype(f32),
        freq_full.reshape(-1).astype(f32),
        dss_w.astype(f32),
        log_step.astype(f32),
    )
    length = tokens * n_seq
    blocks = length // TILE
    toeplitz = make_toeplitz(*modes, lag_blocks(length))

    x_wide = layer_input.astype(f32)
    center = x_wide - jnp.mean(x_wide, axis=1, keepdims=True)
    inverse = lax.rsqrt(jnp.mean(center * center, axis=1, keepdims=True) + epsilon)
    unit = center * inverse
    normed = (unit * gain_wide + bias_wide).astype(bf16)

    normed_all = jnp.concatenate(gather_grp(normed, n_grp), axis=0)
    cot_all = jnp.concatenate(gather_grp(out_cotangent, n_grp), axis=0)

    pre_reduce = (
        lax.dot_general(reduce_full, normed, contract_last, preferred_element_type=f32)
        + reduce_bias.reshape(-1).astype(f32)[:, None]
    )
    reduced, reduce_pull = jax.vjp(jax.nn.gelu, pre_reduce)
    channel_in = lax.all_to_all(reduced.astype(bf16), "seq", split_axis=0, concat_axis=1, tiled=True)
    seg = doc_row.astype(jnp.int32).reshape(blocks, TILE)
    signal = channel_in.reshape(-1, blocks, TILE)
    channel_out = conv(seg, signal, toeplitz).reshape(-1, length)
    mixed = lax.all_to_all(channel_out, "seq", split_axis=1, concat_axis=0, tiled=True)
    mixed_all = jnp.concatenate(gather_grp(mixed, n_grp), axis=1)

    pre_value = lax.dot_general(normed_all, value_part, contract_last, preferred_element_type=f32) + value_bias
    activated, value_pull = jax.vjp(jax.nn.gelu, pre_value)
    g_gated = jnp.dot(cot_all, out_part, preferred_element_type=f32)
    pre_up = lax.dot_general(mixed_all, up_part, (((0,), (1,)), ((), ())), preferred_element_type=f32) + up_bias
    gated = (activated * pre_up).astype(bf16)
    g_activated = g_gated * pre_up
    g_pre_up = (g_gated * activated).astype(bf16)
    g_pre_value = value_pull(g_activated)[0].astype(bf16)

    g_mixed = lax.dot_general(up_part, g_pre_up, (((0,), (1,)), ((), ())), preferred_element_type=f32)
    g_mixed = sum_scatter_grp([g_mixed[:, k * tokens : (k + 1) * tokens] for k in range(n_grp)], n_grp)
    g_channel = lax.all_to_all(g_mixed.astype(bf16), "seq", split_axis=0, concat_axis=1, tiled=True)
    g_signal, g_taps = conv_back(seg, signal, g_channel.reshape(-1, blocks, TILE), toeplitz)
    g_reduced = lax.all_to_all(g_signal.reshape(-1, length), "seq", split_axis=1, concat_axis=0, tiled=True)
    g_weights, g_step, g_lam = mode_grads(*modes, g_taps)

    added = lax.dot_general(gated, out_part, contract_last, preferred_element_type=f32)
    added = sum_scatter_grp([added[k * tokens : (k + 1) * tokens] for k in range(n_grp)], n_grp)
    output = (x_wide + added + out_bias.reshape(-1).astype(f32)).astype(bf16)

    g_normed = jnp.dot(g_pre_value, value_part, preferred_element_type=f32)
    g_normed = sum_scatter_grp([g_normed[k * tokens : (k + 1) * tokens] for k in range(n_grp)], n_grp)

    def over_seq(x):
        return lax.psum_scatter(x.astype(bf16), "seq", scatter_dimension=0, tiled=True)

    g_out = over_seq(lax.dot_general(cot_all, gated, contract_first, preferred_element_type=f32))
    g_up = over_seq(lax.dot_general(g_pre_up, mixed_all, (((0,), (1,)), ((), ())), preferred_element_type=f32))
    g_value = over_seq(lax.dot_general(g_pre_value, normed_all, contract_first, preferred_element_type=f32))
    g_out = place_grp(g_out.reshape(-1, n_seq, part), n_grp, me, 2).reshape(w_out.shape).astype(f32)
    g_up = place_grp(g_up, n_grp, me, 0).reshape(w_up.shape).astype(f32)
    g_value = place_grp(g_value, n_grp, me, 0).reshape(w_value.shape).astype(f32)

    g_pre_reduce = reduce_pull(g_reduced.astype(f32))[0].astype(bf16)
    g_reduce = jnp.dot(g_pre_reduce, normed, preferred_element_type=f32)
    g_normed = g_normed + lax.dot_general(g_pre_reduce, reduce_full, contract_first, preferred_element_type=f32)
    g_unit = g_normed * gain_wide
    g_input = inverse * (
        g_unit
        - jnp.mean(g_unit, axis=1, keepdims=True)
        - unit * jnp.mean(g_unit * unit, axis=1, keepdims=True)
    ) + out_cotangent.astype(f32)

    def spread(x):
        return lax.dynamic_update_slice_in_dim(
            jnp.zeros((n_seq, n_grp, part), f32), x.reshape(n_seq, 1, part), me, 1
        ).reshape(n_seq, -1)

    vectors = (
        jnp.sum(g_normed * unit, axis=0).reshape(n_seq, -1),
        jnp.sum(g_normed, axis=0).reshape(n_seq, -1),
        spread(jnp.sum(g_pre_value.astype(f32), axis=0)),
        jnp.sum(g_pre_reduce.astype(f32), axis=1).reshape(n_seq, -1),
        g_lam[0].reshape(n_seq, -1),
        g_lam[1].reshape(n_seq, -1),
        spread(jnp.sum(g_pre_up.astype(f32), axis=0)),
        jnp.sum(out_cotangent.astype(f32), axis=0).reshape(n_seq, -1),
    )
    shard = lax.psum_scatter(jnp.concatenate(vectors, axis=1), "seq", scatter_dimension=0, tiled=False)
    g_reduce = lax.psum_scatter(g_reduce.astype(bf16), "seq", scatter_dimension=0, tiled=True)
    shard, g_step, g_weights, g_reduce = lax.psum(
        (shard, g_step, g_weights, g_reduce.astype(f32)), "grp"
    )
    sums, spots = [], 0
    for array in vectors:
        sums.append(shard[spots : spots + array.shape[1]])
        spots += array.shape[1]
    g_gain, g_bias, g_value_bias, g_reduce_bias, g_decay, g_freq, g_up_bias, g_out_bias = sums
    return (
        output,
        g_input,
        g_gain,
        g_bias,
        g_value,
        g_value_bias,
        g_reduce,
        g_reduce_bias,
        g_decay,
        g_freq,
        g_weights,
        g_step,
        g_up,
        g_up_bias,
        g_out,
        g_out_bias,
    )


def solution(mesh):
    by_token = P(("grp", "seq"), None)
    row, matrix, cube = P("seq"), P("seq", None), P(None, "seq", None)
    layer = (row, row, matrix, row, matrix, row, row, row, cube, row, matrix, row, matrix, row)
    return jax.shard_map(
        functools.partial(body, mesh.shape["grp"], mesh.shape["seq"]),
        mesh=mesh,
        in_specs=(by_token, P("grp", "seq"), *layer, by_token),
        out_specs=(by_token, by_token, *layer),
        check_vma=False,
    )
```

```python
import functools

import jax
import jax.numpy as jnp
from jax import lax
from jax.experimental import pallas as pl
from jax.experimental.pallas import tpu as pltpu
from jax.sharding import PartitionSpec as P

f32, bf16 = jnp.float32, jnp.bfloat16
TILE = 128
MOST = 2000
LAGS = 2048
FINE = 64
PART = 64
ROWS = 8
NT = (((1,), (1,)), ((), ()))
TN = (((0,), (0,)), ((), ()))


def params(mb=56):
    return pltpu.CompilerParams(vmem_limit_bytes=mb << 20)


def cost(us):
    return pl.CostEstimate(flops=us * 10**9, bytes_accessed=us * 10**6, transcendentals=0)


def lag_blocks(length):
    return min(length // TILE, (MOST + TILE - 2) // TILE + 1)


def doc_count(length):
    return length // 1024 + 1


def over_channels(step, unroll):
    def some(i, _):
        for u in range(unroll):
            step(i * unroll + u, u)
        return 0

    lax.fori_loop(0, ROWS // unroll, some, 0)


def cmul(a, b):
    return (a[0] * b[0] - a[1] * b[1], a[0] * b[1] + a[1] * b[0])


def mode_rates(lam_log_ref, lam_freq_ref, step_ref):
    lam_re = -jnp.exp(lam_log_ref[...])
    lam_im = lam_freq_ref[...]
    delta = jnp.exp(step_ref[...])
    return lam_re, lam_im, delta


def first_power(lam_re, lam_im, delta):
    growth = jnp.exp(delta * lam_re)
    phase = delta * lam_im
    return growth * jnp.cos(phase), growth * jnp.sin(phase)


def store_squares(one, sq_ref):
    cur = one
    for k in range(11):
        sq_ref[0, k], sq_ref[1, k] = cur
        if k < 10:
            cur = cmul(cur, cur)


def power_tiles(sq_ref, c, first, count):
    def sq(k):
        return sq_ref[0, k, pl.ds(c, 1), :], sq_ref[1, k, pl.ds(c, 1), :]

    width = sq_ref.shape[-1]
    row = lax.broadcasted_iota(jnp.int32, (8, width), 0)
    tile = None
    for k in range(3):
        re, im = sq(first + k)
        on = (row & (1 << k)) != 0
        term = jnp.where(on, re, 1.0), jnp.where(on, im, 0.0)
        tile = term if tile is None else cmul(tile, term)
    tiles, k = [tile], 3
    while len(tiles) < count:
        step = sq(first + k)
        tiles = tiles + [cmul(t, step) for t in tiles]
        k += 1
    return tiles


def split(x):
    hi = x.astype(bf16)
    return hi, (x - hi.astype(f32)).astype(bf16)


def coarse_tiles(sq_ref, c):
    even = power_tiles(sq_ref, c, 7, LAGS // TILE // 8)
    half = sq_ref[0, 6, pl.ds(c, 1), :], sq_ref[1, 6, pl.ds(c, 1), :]
    return even + [cmul(t, half) for t in even]


def taps_kernel(
    lam_log_ref, lam_freq_ref, w_ref, step_ref, tt_ref, qh_ref, ql_ref, sq_ref, cf_ref, p_ref
):
    lam_re, lam_im, delta = mode_rates(lam_log_ref, lam_freq_ref, step_ref)
    one = first_power(lam_re, lam_im, delta)
    store_squares(one, sq_ref)
    modulus = lam_re * lam_re + lam_im * lam_im
    shift_re, shift_im = one[0] - 1.0, one[1]
    ratio = (
        (shift_re * lam_re + shift_im * lam_im) / modulus,
        (shift_im * lam_re - shift_re * lam_im) / modulus,
    )
    cf_ref[0], cf_ref[1] = cmul((w_ref[0], w_ref[1]), ratio)
    width = sq_ref.shape[-1]
    deep = tt_ref.shape[1]
    coarse = LAGS // FINE

    def channel(c, u):
        for t, pair in enumerate(power_tiles(sq_ref, c, 0, FINE // 8)):
            if t % 2 == 0:
                held = pair
                continue
            for part in range(2):
                hi, lo = split(jnp.concatenate([held[part], pair[part]], axis=0))
                qh_ref[c, 8 * t - 8 : 8 * t + 8, part * width : (part + 1) * width] = hi
                ql_ref[c, 8 * t - 8 : 8 * t + 8, part * width : (part + 1) * width] = lo
        coeff = cf_ref[0, pl.ds(c, 1), :], cf_ref[1, pl.ds(c, 1), :]
        tiles = [cmul(t, coeff) for t in coarse_tiles(sq_ref, c)]
        for part, sign in ((0, 1.0), (1, -1.0)):
            hi, lo = split(sign * jnp.concatenate([t[part] for t in tiles], axis=0))
            p_ref[u, :coarse, part * width : (part + 1) * width] = hi
            p_ref[u, coarse:, part * width : (part + 1) * width] = lo
        both = lax.dot_general(qh_ref[c], p_ref[u], NT, preferred_element_type=f32)
        low = lax.dot_general(ql_ref[c], p_ref[u, :coarse], NT, preferred_element_type=f32)
        taps = (both[:, :coarse] + both[:, coarse:] + low).T
        taps = jnp.concatenate([taps[: coarse // 2], taps[coarse // 2 :]], axis=1)
        empty = jnp.zeros((TILE, TILE), f32)
        pieces = [empty] + [
            jnp.broadcast_to(taps[d : d + 1], (TILE, TILE)) if d < LAGS // TILE else empty for d in range(deep)
        ]
        skew = pltpu.roll(jnp.concatenate(pieces, axis=1), 0, 1, stride=1, stride_axis=0)
        for d in range(deep):
            tt_ref[c, d] = skew[:, (d + 1) * TILE : (d + 2) * TILE].astype(bf16)

    over_channels(channel, p_ref.shape[0])


def make_toeplitz(lam_log, lam_freq, weights, log_step, deep):
    channels, modes = weights.shape[1:]
    table = pl.BlockSpec((ROWS, FINE, 2 * modes), lambda i: (i, 0, 0))
    return pl.pallas_call(
        taps_kernel,
        grid=(channels // ROWS,),
        in_specs=[
            pl.BlockSpec((1, modes), lambda i: (0, 0)),
            pl.BlockSpec((1, modes), lambda i: (0, 0)),
            pl.BlockSpec((2, ROWS, modes), lambda i: (0, i, 0)),
            pl.BlockSpec((ROWS, 1), lambda i: (i, 0)),
        ],
        out_specs=[pl.BlockSpec((ROWS, deep, TILE, TILE), lambda i: (i, 0, 0, 0)), table, table],
        out_shape=[
            jax.ShapeDtypeStruct((channels, deep, TILE, TILE), bf16),
            jax.ShapeDtypeStruct((channels, FINE, 2 * modes), bf16),
            jax.ShapeDtypeStruct((channels, FINE, 2 * modes), bf16),
        ],
        scratch_shapes=[
            pltpu.VMEM((2, 11, ROWS, modes), f32),
            pltpu.VMEM((2, ROWS, modes), f32),
            pltpu.VMEM((4, 2 * LAGS // FINE, 2 * modes), bf16),
        ],
        compiler_params=params(),
        cost_estimate=cost(25),
    )(lam_log[None], lam_freq[None], weights, log_step[:, None])


def conv_kernel(docs, seg_ref, x_ref, tt_ref, y_ref, xs_ref, xw_ref):
    blocks, deep = x_ref.shape[1], tt_ref.shape[1]
    lead = deep - 1
    seg = seg_ref[...]
    for u in range(xs_ref.shape[0]):
        for k in range(docs):
            xs_ref[u, k, :lead, :] = jnp.zeros((lead, TILE), f32)

    def one(c, u):
        x = x_ref[c].astype(f32)
        for k in range(docs):
            xs_ref[u, k, lead:, :] = jnp.where(seg == k, x, 0.0)
        for k in range(docs):
            for d in range(deep):
                xw_ref[u, k * blocks : (k + 1) * blocks, d * TILE : (d + 1) * TILE] = xs_ref[
                    u, k, lead - d : lead - d + blocks, :
                ].astype(bf16)
        y = jnp.dot(xw_ref[u], tt_ref[c].reshape(deep * TILE, TILE), preferred_element_type=f32)
        out = jnp.zeros((blocks, TILE), f32)
        for k in range(docs):
            out = jnp.where(seg == k, y[k * blocks : (k + 1) * blocks], out)
        y_ref[c] = out.astype(bf16)

    def pair(i, _):
        for u in range(xs_ref.shape[0]):
            one(i * xs_ref.shape[0] + u, u)
        return 0

    lax.fori_loop(0, ROWS // xs_ref.shape[0], pair, 0)


def conv(seg, x, tt, unroll=4):
    channels, blocks, _ = x.shape
    deep = tt.shape[1]
    docs = doc_count(blocks * TILE)
    return pl.pallas_call(
        functools.partial(conv_kernel, docs),
        grid=(channels // ROWS,),
        in_specs=[
            pl.BlockSpec((blocks, TILE), lambda i: (0, 0)),
            pl.BlockSpec((ROWS, blocks, TILE), lambda i: (i, 0, 0)),
            pl.BlockSpec((ROWS, deep, TILE, TILE), lambda i: (i, 0, 0, 0)),
        ],
        out_specs=pl.BlockSpec((ROWS, blocks, TILE), lambda i: (i, 0, 0)),
        out_shape=jax.ShapeDtypeStruct(x.shape, bf16),
        scratch_shapes=[
            pltpu.VMEM((unroll, docs, blocks + deep - 1, TILE), f32),
            pltpu.VMEM((unroll, docs * blocks, deep * TILE), bf16),
        ],
        compiler_params=params(),
        cost_estimate=cost(17),
    )(seg, x, tt)


def back_kernel(docs, seg_ref, flip_ref, g_ref, tt_ref, gx_ref, gs_ref, gw_ref, gr_ref):
    blocks, deep = g_ref.shape[1], tt_ref.shape[1]
    lead = deep - 1
    flip = flip_ref[...]
    seg = jnp.dot(seg_ref[...].astype(bf16), flip, preferred_element_type=f32)
    flat = g_ref[...].reshape(ROWS * blocks, TILE)
    gr_ref[...] = jnp.dot(flat, flip, preferred_element_type=f32).reshape(gr_ref.shape)
    for u in range(gs_ref.shape[0]):
        for k in range(docs):
            gs_ref[u, k, blocks:, :] = jnp.zeros((lead, TILE), f32)

    def one(c, u):
        g = gr_ref[c]
        for k in range(docs):
            gs_ref[u, k, :blocks, :] = jnp.where(seg == k, g, 0.0)
        for k in range(docs):
            for d in range(deep):
                gw_ref[u, k * blocks : (k + 1) * blocks, d * TILE : (d + 1) * TILE] = gs_ref[
                    u, k, d : d + blocks, :
                ].astype(bf16)
        gx = jnp.dot(gw_ref[u], tt_ref[c].reshape(deep * TILE, TILE), preferred_element_type=f32)
        out = jnp.zeros((blocks, TILE), f32)
        for k in range(docs):
            out = jnp.where(seg == k, gx[k * blocks : (k + 1) * blocks], out)
        gr_ref[c] = out

    def pair(i, _):
        for u in range(gs_ref.shape[0]):
            one(i * gs_ref.shape[0] + u, u)
        return 0

    lax.fori_loop(0, ROWS // gs_ref.shape[0], pair, 0)
    flat = gr_ref[...].astype(bf16).reshape(ROWS * blocks, TILE)
    gx_ref[...] = jnp.dot(flat, flip, preferred_element_type=f32).astype(bf16).reshape(gx_ref.shape)


def conv_back(seg, g, tt, unroll=4):
    channels, blocks, _ = g.shape
    deep = tt.shape[1]
    docs = doc_count(blocks * TILE)
    flip = jnp.eye(TILE, dtype=bf16)[::-1]
    rows = pl.BlockSpec((ROWS, blocks, TILE), lambda i: (i, 0, 0))
    return pl.pallas_call(
        functools.partial(back_kernel, docs),
        grid=(channels // ROWS,),
        in_specs=[
            pl.BlockSpec((blocks, TILE), lambda i: (0, 0)),
            pl.BlockSpec((TILE, TILE), lambda i: (0, 0)),
            rows,
            pl.BlockSpec((ROWS, deep, TILE, TILE), lambda i: (i, 0, 0, 0)),
        ],
        out_specs=rows,
        out_shape=jax.ShapeDtypeStruct(g.shape, bf16),
        scratch_shapes=[
            pltpu.VMEM((unroll, docs, blocks + deep - 1, TILE), f32),
            pltpu.VMEM((unroll, docs * blocks, deep * TILE), bf16),
            pltpu.VMEM((ROWS, blocks, TILE), f32),
        ],
        compiler_params=params(),
        cost_estimate=cost(15),
    )(seg, flip, g, tt)


def taps_grad_kernel(docs, seg_ref, flip_ref, x_ref, g_ref, dt_ref, gs_ref, gw_ref, xst_ref):
    blocks = x_ref.shape[1]
    deep = gw_ref.shape[2] // TILE
    lead = deep - 1
    cuts = TILE // PART
    seg = seg_ref[...]
    lane = lax.broadcasted_iota(jnp.int32, (blocks, TILE), 1)
    for u in range(gs_ref.shape[0]):
        for k in range(docs * cuts):
            gs_ref[u, k, blocks:, :] = jnp.zeros((lead, TILE), f32)

    def one(c, u):
        g = g_ref[c].astype(f32)
        x = x_ref[c].astype(f32)
        for k in range(docs):
            own = jnp.where(seg == k, g, 0.0)
            gs_ref[u, k * cuts, :blocks, :] = own
            after = jnp.concatenate([own[1:], jnp.zeros((1, TILE), f32)], axis=0)
            for p in range(1, cuts):
                gs_ref[u, k * cuts + p, :blocks, :] = pltpu.roll(
                    jnp.where(lane < p * PART, after, own), TILE - p * PART, 1
                )
            mine = jnp.where(seg == k, x, 0.0).astype(bf16)
            mine = jnp.dot(mine, flip_ref[...], preferred_element_type=f32).astype(bf16)
            for p in range(cuts):
                at = (k * cuts + p) * blocks
                xst_ref[u, at : at + blocks, :] = mine[:, p * PART : (p + 1) * PART]
        for k in range(docs * cuts):
            for d in range(deep):
                gw_ref[u, k * blocks : (k + 1) * blocks, d * TILE : (d + 1) * TILE] = gs_ref[
                    u, k, d : d + blocks, :
                ].astype(bf16)
        wide = lax.dot_general(xst_ref[u], gw_ref[u], TN, preferred_element_type=f32)
        wide = jnp.concatenate([wide, jnp.zeros((PART, TILE), f32)], axis=1)
        flat = pltpu.roll(wide, wide.shape[1] - (PART - 1), 1, stride=1, stride_axis=0)
        dt_ref[pl.ds(c, 1), :] = jnp.sum(flat[:, :LAGS], axis=0, keepdims=True)

    def pair(i, _):
        for u in range(gs_ref.shape[0]):
            one(i * gs_ref.shape[0] + u, u)
        return 0

    lax.fori_loop(0, ROWS // gs_ref.shape[0], pair, 0)


def taps_grad(seg, x, g, unroll=4):
    channels, blocks, _ = x.shape
    deep = lag_blocks(blocks * TILE)
    docs = doc_count(blocks * TILE)
    cuts = TILE // PART
    place = jnp.arange(TILE)
    flip = (place[:, None] == (place // PART * PART + PART - 1 - place % PART)[None, :]).astype(bf16)
    rows = pl.BlockSpec((ROWS, blocks, TILE), lambda i: (i, 0, 0))
    return pl.pallas_call(
        functools.partial(taps_grad_kernel, docs),
        grid=(channels // ROWS,),
        in_specs=[
            pl.BlockSpec((blocks, TILE), lambda i: (0, 0)),
            pl.BlockSpec((TILE, TILE), lambda i: (0, 0)),
            rows,
            rows,
        ],
        out_specs=pl.BlockSpec((ROWS, LAGS), lambda i: (i, 0)),
        out_shape=jax.ShapeDtypeStruct((channels, LAGS), f32),
        scratch_shapes=[
            pltpu.VMEM((unroll, docs * cuts, blocks + deep - 1, TILE), f32),
            pltpu.VMEM((unroll, docs * cuts * blocks, deep * TILE), bf16),
            pltpu.VMEM((unroll, docs * cuts * blocks, PART), bf16),
        ],
        compiler_params=params(),
        cost_estimate=cost(20),
    )(seg, flip, x, g)


def mode_grad_kernel(
    lam_log_ref, lam_freq_ref, w_ref, step_ref, dt_ref, qh_ref, ql_ref, gw_ref, gstep_ref, glam_ref, sq_ref, s_ref
):
    lam_re, lam_im, delta = mode_rates(lam_log_ref, lam_freq_ref, step_ref)
    one = first_power(lam_re, lam_im, delta)
    store_squares(one, sq_ref)
    width = sq_ref.shape[-1]
    coarse = LAGS // FINE

    def channel(c, u):
        dt = dt_ref[c]
        dt = jnp.concatenate([dt[:, :FINE], dt[:, FINE:]], axis=0)
        lane = lax.broadcasted_iota(jnp.int32, (coarse, FINE), 1).astype(f32)
        hi, lo = split(jnp.concatenate([dt, dt * lane], axis=0))
        both = jnp.dot(jnp.concatenate([hi, lo], axis=0), qh_ref[c], preferred_element_type=f32)
        low = jnp.dot(hi, ql_ref[c], preferred_element_type=f32)
        v = both[: 2 * coarse] + both[2 * coarse :] + low
        tiles = coarse_tiles(sq_ref, c)
        power = tuple(jnp.concatenate([t[part] for t in tiles], axis=0) for part in range(2))
        v0 = v[:coarse, :width], v[:coarse, width:]
        row = lax.broadcasted_iota(jnp.int32, (coarse, width), 0)
        far = (row % (coarse // 2)) * (2 * FINE) + (row // (coarse // 2)) * FINE
        far = far.astype(f32)
        v1 = tuple(far * v0[part] + v[coarse:, part * width : (part + 1) * width] for part in range(2))
        for n, pair in enumerate((v0, v1)):
            prod = cmul(power, pair)
            for part in range(2):
                s_ref[2 * n + part, pl.ds(c, 1), :] = jnp.sum(prod[part], axis=0, keepdims=True)

    over_channels(channel, 4)
    modulus = lam_re * lam_re + lam_im * lam_im
    inv = lam_re / modulus, -lam_im / modulus
    shift = one[0] - 1.0, one[1]
    ratio = cmul(shift, inv)
    w = w_ref[0], w_ref[1]
    s0 = s_ref[0], s_ref[1]
    s1 = s_ref[2], s_ref[3]
    coeff = cmul(w, ratio)
    gw = cmul(s0, ratio)
    gw_ref[0], gw_ref[1] = gw[0], -gw[1]
    near = cmul(s0, cmul(w, cmul(one, inv)))
    far = cmul(coeff, s1)
    z = near[0] + far[0], near[1] + far[1]
    back = cmul(s0, cmul(coeff, inv))
    big = delta * z[0] - back[0], delta * z[1] - back[1]
    step = jnp.sum((z[0] * lam_re - z[1] * lam_im) * delta, axis=1, keepdims=True)
    gstep_ref[...] = jnp.broadcast_to(step, gstep_ref.shape)

    @pl.when(pl.program_id(0) == 0)
    def _():
        glam_ref[...] = jnp.zeros(glam_ref.shape, f32)

    glam_ref[0] += big[0] * lam_re
    glam_ref[1] -= big[1]


def mode_grads(lam_log, lam_freq, weights, log_step, dt, fine_high, fine_low):
    channels, modes = weights.shape[1:]
    rows = LAGS // TILE
    table = pl.BlockSpec((ROWS, FINE, 2 * modes), lambda i: (i, 0, 0))
    gw, gstep, glam = pl.pallas_call(
        mode_grad_kernel,
        grid=(channels // ROWS,),
        in_specs=[
            pl.BlockSpec((1, modes), lambda i: (0, 0)),
            pl.BlockSpec((1, modes), lambda i: (0, 0)),
            pl.BlockSpec((2, ROWS, modes), lambda i: (0, i, 0)),
            pl.BlockSpec((ROWS, 1), lambda i: (i, 0)),
            pl.BlockSpec((ROWS, rows, TILE), lambda i: (i, 0, 0)),
            table,
            table,
        ],
        out_specs=[
            pl.BlockSpec((2, ROWS, modes), lambda i: (0, i, 0)),
            pl.BlockSpec((ROWS, TILE), lambda i: (i, 0)),
            pl.BlockSpec((2, ROWS, modes), lambda i: (0, 0, 0)),
        ],
        out_shape=[
            jax.ShapeDtypeStruct((2, channels, modes), f32),
            jax.ShapeDtypeStruct((channels, TILE), f32),
            jax.ShapeDtypeStruct((2, ROWS, modes), f32),
        ],
        scratch_shapes=[
            pltpu.VMEM((2, 11, ROWS, modes), f32),
            pltpu.VMEM((4, ROWS, modes), f32),
        ],
        compiler_params=params(),
        cost_estimate=cost(12),
    )(lam_log[None], lam_freq[None], weights, log_step[:, None], dt.reshape(channels, rows, TILE), fine_high, fine_low)
    return gw, gstep[:, 0], jnp.sum(glam, axis=1)


epsilon = 1e-05
contract_last = (((1,), (1,)), ((), ()))
contract_first = (((0,), (0,)), ((), ()))


def swap(x, k, n_grp):
    return x if k == 0 else lax.ppermute(x, "grp", [(i, i ^ k) for i in range(n_grp)])


def gather_grp(x, n_grp):
    return [swap(x, k, n_grp) for k in range(n_grp)]


def sum_scatter_grp(pieces, n_grp):
    total = pieces[0].astype(f32)
    for k in range(1, n_grp):
        total = total + swap(pieces[k].astype(bf16), k, n_grp).astype(f32)
    return total


def tree_sum(terms):
    while len(terms) > 1:
        terms = [terms[i] + terms[i + 1] for i in range(0, len(terms), 2)]
    return terms[0]


def sum_grp(x, n_grp):
    return tree_sum([y.astype(f32) for y in gather_grp(x.astype(bf16), n_grp)])


def place_grp(x, n_grp, me, axis):
    held = jnp.stack(gather_grp(x, n_grp))
    order = jnp.arange(n_grp, dtype=jnp.int32) ^ me
    rows = [lax.dynamic_index_in_dim(held, order[j], 0, keepdims=False) for j in range(n_grp)]
    return jnp.stack(rows, axis=axis)


def body(
    n_grp,
    n_seq,
    layer_input,
    segments,
    ln_gain,
    ln_bias,
    w_value,
    b_value,
    w_reduce,
    b_reduce,
    lam_log,
    lam_freq,
    dss_w,
    log_step,
    w_up,
    b_up,
    w_out,
    b_out,
    out_cotangent,
):
    me = lax.axis_index("grp")
    tokens, wide = layer_input.shape
    part = w_value.shape[0] // n_grp
    quarter = n_seq * part
    reduced_width = w_reduce.shape[0] * n_seq

    small = (ln_gain, ln_bias, b_value, b_reduce, lam_log, lam_freq, b_up, b_out, segments[0].astype(bf16))
    packed = jnp.concatenate(small)
    packed = jnp.pad(packed, (0, -packed.shape[0] % 2048)).reshape(-1, 128)
    packed = lax.all_gather(packed, "seq", axis=0, tiled=True).reshape(n_seq, -1)
    spots, fulls = 0, []
    for array in small:
        fulls.append(packed[:, spots : spots + array.shape[0]])
        spots += array.shape[0]
    gain_full, bias_full, value_bias, reduce_bias, decay_full, freq_full, up_bias, out_bias, doc_row = fulls
    gain_wide = gain_full.reshape(-1).astype(f32)
    bias_wide = bias_full.reshape(-1).astype(f32)
    value_bias = lax.dynamic_slice_in_dim(value_bias, me * part, part, 1).reshape(-1).astype(f32)
    up_bias = lax.dynamic_slice_in_dim(up_bias, me * part, part, 1).reshape(-1).astype(f32)

    reduce_full = lax.all_gather(w_reduce, "seq", axis=0, tiled=True)
    pieces = [lax.dynamic_slice_in_dim(w, me * part, part, 0) for w in (w_value, w_up)]
    both_part = lax.all_gather(jnp.concatenate(pieces, axis=1), "seq", axis=0, tiled=True)
    value_part, up_part = both_part[:, :wide], both_part[:, wide:]
    out_cols = lax.dynamic_index_in_dim(w_out.reshape(-1, n_seq, n_grp, part), me, 2, keepdims=False)
    out_part = lax.all_gather(out_cols.reshape(-1, quarter), "seq", axis=0, tiled=True)

    modes = (
        decay_full.reshape(-1).astype(f32),
        freq_full.reshape(-1).astype(f32),
        dss_w.astype(f32),
        log_step.astype(f32),
    )
    length = tokens * n_seq
    blocks = length // TILE
    toeplitz, fine_high, fine_low = make_toeplitz(*modes, lag_blocks(length))

    x_wide = layer_input.astype(f32)
    center = x_wide - jnp.mean(x_wide, axis=1, keepdims=True)
    inverse = lax.rsqrt(jnp.mean(center * center, axis=1, keepdims=True) + epsilon)
    unit = center * inverse
    normed = (unit * gain_wide + bias_wide).astype(bf16)

    normed_all = jnp.concatenate(gather_grp(normed, n_grp), axis=0)
    cot_all = jnp.concatenate(gather_grp(out_cotangent, n_grp), axis=0)

    pre_reduce = (
        lax.dot_general(reduce_full, normed, contract_last, preferred_element_type=f32)
        + reduce_bias.reshape(-1).astype(f32)[:, None]
    )
    reduced, reduce_pull = jax.vjp(jax.nn.gelu, pre_reduce)
    channel_in = lax.all_to_all(reduced.astype(bf16), "seq", split_axis=0, concat_axis=1, tiled=True)
    seg = doc_row.astype(jnp.int32).reshape(blocks, TILE)
    signal = channel_in.reshape(-1, blocks, TILE)
    channel_out = conv(seg, signal, toeplitz).reshape(-1, length)
    mixed = lax.all_to_all(channel_out, "seq", split_axis=1, concat_axis=0, tiled=True)
    mixed_all = jnp.concatenate(gather_grp(mixed, n_grp), axis=1)

    pre_value = lax.dot_general(normed_all, value_part, contract_last, preferred_element_type=f32) + value_bias
    activated, value_pull = jax.vjp(jax.nn.gelu, pre_value)
    g_gated = jnp.dot(cot_all, out_part, preferred_element_type=f32)
    pre_up = lax.dot_general(mixed_all, up_part, (((0,), (1,)), ((), ())), preferred_element_type=f32) + up_bias
    gated = (activated * pre_up).astype(bf16)
    g_activated = g_gated * pre_up
    g_pre_up = (g_gated * activated).astype(bf16)
    g_pre_value = value_pull(g_activated)[0].astype(bf16)

    g_mixed = lax.dot_general(up_part, g_pre_up, (((0,), (1,)), ((), ())), preferred_element_type=f32)
    g_mixed = sum_scatter_grp([g_mixed[:, k * tokens : (k + 1) * tokens] for k in range(n_grp)], n_grp)
    g_channel = lax.all_to_all(g_mixed.astype(bf16), "seq", split_axis=0, concat_axis=1, tiled=True)
    g_channel = g_channel.reshape(-1, blocks, TILE)
    g_signal = conv_back(seg, g_channel, toeplitz)
    g_reduced = lax.all_to_all(g_signal.reshape(-1, length), "seq", split_axis=1, concat_axis=0, tiled=True)
    g_taps = taps_grad(seg, signal, g_channel)
    g_weights, g_step, g_lam = mode_grads(*modes, g_taps, fine_high, fine_low)
    channels, states = g_weights.shape[1:]
    own = jnp.concatenate([g_weights.reshape(-1), jnp.pad(g_step, (0, -channels % states))])
    own = sum_grp(own.reshape(-1, states), n_grp)
    g_weights, g_step = own[: 2 * channels].reshape(g_weights.shape), own[2 * channels :].reshape(-1)[:channels]

    added = lax.dot_general(gated, out_part, contract_last, preferred_element_type=f32)
    added = sum_scatter_grp([added[k * tokens : (k + 1) * tokens] for k in range(n_grp)], n_grp)
    output = (x_wide + added + out_bias.reshape(-1).astype(f32)).astype(bf16)

    g_normed = jnp.dot(g_pre_value, value_part, preferred_element_type=f32)
    g_normed = sum_scatter_grp([g_normed[k * tokens : (k + 1) * tokens] for k in range(n_grp)], n_grp)

    def over_seq(x):
        return lax.psum_scatter(x.astype(bf16), "seq", scatter_dimension=0, tiled=True)

    g_out = over_seq(lax.dot_general(cot_all, gated, contract_first, preferred_element_type=f32))
    g_up = lax.dot_general(g_pre_up, mixed_all, (((0,), (1,)), ((), ())), preferred_element_type=f32)
    g_value = lax.dot_general(g_pre_value, normed_all, contract_first, preferred_element_type=f32)
    g_both = over_seq(jnp.concatenate([g_value.astype(bf16), g_up.astype(bf16)], axis=1))
    g_out = place_grp(g_out.reshape(-1, n_seq, part), n_grp, me, 2).reshape(w_out.shape).astype(f32)
    g_both = place_grp(g_both, n_grp, me, 0).reshape(-1, g_both.shape[1]).astype(f32)
    g_value, g_up = g_both[:, :wide], g_both[:, wide:]

    g_pre_reduce = reduce_pull(g_reduced.astype(f32))[0].astype(bf16)
    g_reduce = jnp.dot(g_pre_reduce, normed, preferred_element_type=f32)
    g_normed = g_normed + lax.dot_general(g_pre_reduce, reduce_full, contract_first, preferred_element_type=f32)
    g_unit = g_normed * gain_wide
    g_input = inverse * (
        g_unit
        - jnp.mean(g_unit, axis=1, keepdims=True)
        - unit * jnp.mean(g_unit * unit, axis=1, keepdims=True)
    ) + out_cotangent.astype(f32)

    def spread(x):
        return lax.dynamic_update_slice_in_dim(
            jnp.zeros((n_seq, n_grp, part), f32), x.reshape(n_seq, 1, part), me, 1
        ).reshape(n_seq, -1)

    vectors = (
        jnp.sum(g_normed * unit, axis=0).reshape(n_seq, -1),
        jnp.sum(g_normed, axis=0).reshape(n_seq, -1),
        spread(jnp.sum(g_pre_value.astype(f32), axis=0)),
        jnp.sum(g_pre_reduce.astype(f32), axis=1).reshape(n_seq, -1),
        g_lam[0].reshape(n_seq, -1),
        g_lam[1].reshape(n_seq, -1),
        spread(jnp.sum(g_pre_up.astype(f32), axis=0)),
        jnp.sum(out_cotangent.astype(f32), axis=0).reshape(n_seq, -1),
    )
    flat = jnp.concatenate(vectors, axis=1)
    flat = jnp.pad(flat, ((0, 0), (0, -flat.shape[1] % wide))).reshape(n_seq, -1, wide)
    own = jnp.concatenate([g_reduce.reshape(n_seq, -1, wide).astype(bf16), flat.astype(bf16)], axis=1)
    own = sum_grp(lax.psum_scatter(own, "seq", scatter_dimension=0, tiled=False), n_grp)
    g_reduce, shard = own[: w_reduce.shape[0]], own[w_reduce.shape[0] :].reshape(-1)
    sums, spots = [], 0
    for array in vectors:
        sums.append(shard[spots : spots + array.shape[1]])
        spots += array.shape[1]
    g_gain, g_bias, g_value_bias, g_reduce_bias, g_decay, g_freq, g_up_bias, g_out_bias = sums
    return (
        output,
        g_input,
        g_gain,
        g_bias,
        g_value,
        g_value_bias,
        g_reduce,
        g_reduce_bias,
        g_decay,
        g_freq,
        g_weights,
        g_step,
        g_up,
        g_up_bias,
        g_out,
        g_out_bias,
    )


def solution(mesh):
    by_token = P(("grp", "seq"), None)
    row, matrix, cube = P("seq"), P("seq", None), P(None, "seq", None)
    layer = (row, row, matrix, row, matrix, row, row, row, cube, row, matrix, row, matrix, row)
    return jax.shard_map(
        functools.partial(body, mesh.shape["grp"], mesh.shape["seq"]),
        mesh=mesh,
        in_specs=(by_token, P("grp", "seq"), *layer, by_token),
        out_specs=(by_token, by_token, *layer),
        check_vma=False,
    )
```

```python
import functools

import jax
import jax.numpy as jnp
from jax import lax
from jax.experimental import pallas as pl
from jax.experimental.pallas import tpu as pltpu
from jax.sharding import PartitionSpec as P

f32, bf16 = jnp.float32, jnp.bfloat16
TILE = 128
MOST = 2000
LAGS = 2048
FINE = 64
EXTRA = 16
PART = 64
ROWS = 8
NT = (((1,), (1,)), ((), ()))
TN = (((0,), (0,)), ((), ()))


def params(mb=48):
    return pltpu.CompilerParams(vmem_limit_bytes=mb << 20)


def cost(us):
    return pl.CostEstimate(flops=us * 10**9, bytes_accessed=us * 10**6, transcendentals=0)


def lag_blocks(length):
    return min(length // TILE, (MOST + TILE - 2) // TILE + 1)


def doc_count(length):
    return length // 1024 + 1


def over_channels(step, unroll):
    def some(i, _):
        for u in range(unroll):
            step(i * unroll + u, u)
        return 0

    lax.fori_loop(0, ROWS // unroll, some, 0)


def cmul(a, b):
    return (a[0] * b[0] - a[1] * b[1], a[0] * b[1] + a[1] * b[0])


def mode_rates(lam_log_ref, lam_freq_ref, step_ref):
    lam_re = -jnp.exp(lam_log_ref[...])
    lam_im = lam_freq_ref[...]
    delta = jnp.exp(step_ref[...])
    return lam_re, lam_im, delta


def first_power(lam_re, lam_im, delta):
    growth = jnp.exp(delta * lam_re)
    phase = delta * lam_im
    return growth * jnp.cos(phase), growth * jnp.sin(phase)


def store_squares(one, sq_ref):
    cur = one
    for k in range(11):
        sq_ref[0, k], sq_ref[1, k] = cur
        if k < 10:
            cur = cmul(cur, cur)


def power_tiles(sq_ref, c, first, count):
    def sq(k):
        return sq_ref[0, k, pl.ds(c, 1), :], sq_ref[1, k, pl.ds(c, 1), :]

    width = sq_ref.shape[-1]
    row = lax.broadcasted_iota(jnp.int32, (8, width), 0)
    tile = None
    for k in range(3):
        re, im = sq(first + k)
        on = (row & (1 << k)) != 0
        term = jnp.where(on, re, 1.0), jnp.where(on, im, 0.0)
        tile = term if tile is None else cmul(tile, term)
    tiles, k = [tile], 3
    while len(tiles) < count:
        step = sq(first + k)
        tiles = tiles + [cmul(t, step) for t in tiles]
        k += 1
    return tiles


def split(x):
    hi = x.astype(bf16)
    return hi, (x - hi.astype(f32)).astype(bf16)


def coarse_tiles(sq_ref, c):
    even = power_tiles(sq_ref, c, 7, LAGS // TILE // 8)
    half = sq_ref[0, 6, pl.ds(c, 1), :], sq_ref[1, 6, pl.ds(c, 1), :]
    return even + [cmul(t, half) for t in even]


def taps_kernel(
    lam_log_ref, lam_freq_ref, w_ref, step_ref, tt_ref, qh_ref, sq_ref, cf_ref, p_ref, ql_ref
):
    lam_re, lam_im, delta = mode_rates(lam_log_ref, lam_freq_ref, step_ref)
    one = first_power(lam_re, lam_im, delta)
    store_squares(one, sq_ref)
    modulus = lam_re * lam_re + lam_im * lam_im
    shift_re, shift_im = one[0] - 1.0, one[1]
    ratio = (
        (shift_re * lam_re + shift_im * lam_im) / modulus,
        (shift_im * lam_re - shift_re * lam_im) / modulus,
    )
    cf_ref[0], cf_ref[1] = cmul((w_ref[0], w_ref[1]), ratio)
    width = sq_ref.shape[-1]
    deep = tt_ref.shape[2] // TILE
    coarse = LAGS // FINE

    def channel(c, u):
        for t, pair in enumerate(power_tiles(sq_ref, c, 0, FINE // 8)):
            if t % 2 == 0:
                held = pair
                continue
            for part in range(2):
                hi, lo = split(jnp.concatenate([held[part], pair[part]], axis=0))
                qh_ref[c, 8 * t - 8 : 8 * t + 8, part * width : (part + 1) * width] = hi
                ql_ref[u, 8 * t - 8 : 8 * t + 8, part * width : (part + 1) * width] = lo
        coeff = cf_ref[0, pl.ds(c, 1), :], cf_ref[1, pl.ds(c, 1), :]
        tiles = [cmul(t, coeff) for t in coarse_tiles(sq_ref, c)]
        for part, sign in ((0, 1.0), (1, -1.0)):
            hi, lo = split(sign * jnp.concatenate([t[part] for t in tiles], axis=0))
            p_ref[u, :coarse, part * width : (part + 1) * width] = hi
            p_ref[u, coarse:, part * width : (part + 1) * width] = lo
        both = lax.dot_general(qh_ref[c], p_ref[u], NT, preferred_element_type=f32)
        low = lax.dot_general(ql_ref[u], p_ref[u, :coarse], NT, preferred_element_type=f32)
        taps = (both[:, :coarse] + both[:, coarse:] + low).T
        taps = jnp.concatenate([taps[: coarse // 2], taps[coarse // 2 :]], axis=1)
        rows = [jnp.broadcast_to(taps[d : d + 1], (8, TILE)) for d in range(min(deep, LAGS // TILE))]
        gap = jnp.zeros((8, TILE), f32)
        source = jnp.concatenate([gap] + rows + [gap] * (deep - len(rows)), axis=1)
        for r in range(PART // 16):
            pair = [pltpu.roll(source, 16 * r + s, 1, stride=1, stride_axis=0)[:, TILE:] for s in (0, 8)]
            tt_ref[c, 16 * r : 16 * r + 16, :] = jnp.concatenate(pair, axis=0).astype(bf16)

    over_channels(channel, p_ref.shape[0])


def make_toeplitz(lam_log, lam_freq, weights, log_step, deep):
    channels, modes = weights.shape[1:]
    table = pl.BlockSpec((ROWS, FINE, 2 * modes), lambda i: (i, 0, 0))
    return pl.pallas_call(
        taps_kernel,
        grid=(channels // ROWS,),
        in_specs=[
            pl.BlockSpec((1, modes), lambda i: (0, 0)),
            pl.BlockSpec((1, modes), lambda i: (0, 0)),
            pl.BlockSpec((2, ROWS, modes), lambda i: (0, i, 0)),
            pl.BlockSpec((ROWS, 1), lambda i: (i, 0)),
        ],
        out_specs=[pl.BlockSpec((ROWS, PART, deep * TILE), lambda i: (i, 0, 0)), table],
        out_shape=[
            jax.ShapeDtypeStruct((channels, PART, deep * TILE), bf16),
            jax.ShapeDtypeStruct((channels, FINE, 2 * modes), bf16),
        ],
        scratch_shapes=[
            pltpu.VMEM((2, 11, ROWS, modes), f32),
            pltpu.VMEM((2, ROWS, modes), f32),
            pltpu.VMEM((4, 2 * LAGS // FINE, 2 * modes), bf16),
            pltpu.VMEM((4, FINE, 2 * modes), bf16),
        ],
        compiler_params=params(),
        cost_estimate=cost(3),
    )(lam_log[None], lam_freq[None], weights, log_step[:, None])


def doc_windows(z, seg, docs, zs_ref, zw_ref, u, deep):
    blocks = z.shape[0]
    lane = lax.broadcasted_iota(jnp.int32, z.shape, 1)
    for k in range(docs):
        own = jnp.where(seg == k, z, 0.0)
        after = jnp.concatenate([own[1:], jnp.zeros((1, TILE), f32)], axis=0)
        zs_ref[u, 2 * k, :blocks, :] = own
        zs_ref[u, 2 * k + 1, :blocks, :] = pltpu.roll(jnp.where(lane < PART, after, own), TILE - PART, 1)
    for k in range(2 * docs):
        for d in range(deep):
            zw_ref[u, k * blocks : (k + 1) * blocks, d * TILE : (d + 1) * TILE] = zs_ref[
                u, k, d : d + blocks, :
            ].astype(bf16)


def conv_kernel(docs, back, seg_ref, rows_ref, lanes_ref, x_ref, tt_ref, y_ref, zs_ref, zw_ref, xr_ref):
    blocks, deep = x_ref.shape[1], tt_ref.shape[2] // TILE
    zs_ref[...] = jnp.zeros(zs_ref.shape, f32)
    seg = seg_ref[...].astype(f32)
    if not back:
        rows, lanes = rows_ref[...], lanes_ref[...]
        seg = turn(seg.astype(bf16), rows[:blocks, :blocks], lanes)
        xr_ref[...] = turn(x_ref[...].reshape(ROWS * blocks, TILE), rows, lanes).reshape(xr_ref.shape)

    def channel(c, u):
        z = x_ref[c].astype(f32) if back else xr_ref[c]
        doc_windows(z, seg, docs, zs_ref, zw_ref, u, deep)
        y = lax.dot_general(zw_ref[u], tt_ref[c], NT, preferred_element_type=f32)
        out = jnp.zeros((blocks, TILE), f32)
        for k in range(docs):
            at = 2 * k * blocks
            mine = jnp.concatenate([y[at : at + blocks], y[at + blocks : at + 2 * blocks]], axis=1)
            out = jnp.where(seg == k, mine, out)
        if back:
            y_ref[c] = out.astype(bf16)
        else:
            xr_ref[c] = out

    over_channels(channel, zw_ref.shape[0])
    if not back:
        y = turn(xr_ref[...].astype(bf16).reshape(ROWS * blocks, TILE), rows, lanes)
        y_ref[...] = y.astype(bf16).reshape(y_ref.shape)


def any_conv(seg, x, tt, back, unroll=2):
    channels, blocks, _ = x.shape
    deep = tt.shape[2] // TILE
    docs = doc_count(blocks * TILE)
    rows, lanes = reverse_maps(blocks)
    cut = pl.BlockSpec((ROWS, blocks, TILE), lambda i: (i, 0, 0))
    return pl.pallas_call(
        functools.partial(conv_kernel, docs, back),
        grid=(channels // ROWS,),
        in_specs=[
            whole(seg),
            whole(rows),
            whole(lanes),
            cut,
            pl.BlockSpec((ROWS, PART, deep * TILE), lambda i: (i, 0, 0)),
        ],
        out_specs=cut,
        out_shape=jax.ShapeDtypeStruct(x.shape, bf16),
        scratch_shapes=[
            pltpu.VMEM((unroll, 2 * docs, blocks + deep - 1, TILE), f32),
            pltpu.VMEM((unroll, 2 * docs * blocks, deep * TILE), bf16),
            pltpu.VMEM((ROWS, blocks, TILE), f32),
        ],
        compiler_params=params(),
        cost_estimate=cost(3),
    )(seg, rows, lanes, x, tt)


def taps_grad_kernel(docs, seg_ref, flip_ref, x_ref, g_ref, dt_ref, gs_ref, gw_ref, xst_ref, wide_ref):
    wide_ref[...] = jnp.zeros(wide_ref.shape, f32)
    blocks = x_ref.shape[1]
    deep = gw_ref.shape[2] // TILE
    lead = deep - 1
    cuts = TILE // PART
    seg = seg_ref[...]
    lane = lax.broadcasted_iota(jnp.int32, (blocks, TILE), 1)
    for u in range(gs_ref.shape[0]):
        for k in range(docs * cuts):
            gs_ref[u, k, blocks:, :] = jnp.zeros((lead, TILE), f32)

    def one(c, u):
        g = g_ref[c].astype(f32)
        x = x_ref[c].astype(f32)
        for k in range(docs):
            own = jnp.where(seg == k, g, 0.0)
            gs_ref[u, k * cuts, :blocks, :] = own
            after = jnp.concatenate([own[1:], jnp.zeros((1, TILE), f32)], axis=0)
            for p in range(1, cuts):
                gs_ref[u, k * cuts + p, :blocks, :] = pltpu.roll(
                    jnp.where(lane < p * PART, after, own), TILE - p * PART, 1
                )
            mine = jnp.where(seg == k, x, 0.0).astype(bf16)
            mine = jnp.dot(mine, flip_ref[...], preferred_element_type=f32).astype(bf16)
            for p in range(cuts):
                at = (k * cuts + p) * blocks
                xst_ref[u, at : at + blocks, :] = mine[:, p * PART : (p + 1) * PART]
        for k in range(docs * cuts):
            for d in range(deep):
                gw_ref[u, k * blocks : (k + 1) * blocks, d * TILE : (d + 1) * TILE] = gs_ref[
                    u, k, d : d + blocks, :
                ].astype(bf16)
        wide_ref[u, :, : deep * TILE] = lax.dot_general(xst_ref[u], gw_ref[u], TN, preferred_element_type=f32)
        total = jnp.zeros((8, LAGS), f32)
        for r in range(0, PART, 8):
            rows = wide_ref[u, r : r + 8, :]
            total += pltpu.roll(rows, rows.shape[1] - (PART - 1) + r, 1, stride=1, stride_axis=0)[:, :LAGS]
        dt_ref[pl.ds(c, 1), :] = jnp.sum(total, axis=0, keepdims=True)

    def pair(i, _):
        for u in range(gs_ref.shape[0]):
            one(i * gs_ref.shape[0] + u, u)
        return 0

    lax.fori_loop(0, ROWS // gs_ref.shape[0], pair, 0)


def taps_grad(seg, x, g, unroll=4):
    channels, blocks, _ = x.shape
    deep = lag_blocks(blocks * TILE)
    docs = doc_count(blocks * TILE)
    cuts = TILE // PART
    place = jnp.arange(TILE)
    flip = (place[:, None] == (place // PART * PART + PART - 1 - place % PART)[None, :]).astype(bf16)
    rows = pl.BlockSpec((ROWS, blocks, TILE), lambda i: (i, 0, 0))
    return pl.pallas_call(
        functools.partial(taps_grad_kernel, docs),
        grid=(channels // ROWS,),
        in_specs=[
            pl.BlockSpec((blocks, TILE), lambda i: (0, 0)),
            pl.BlockSpec((TILE, TILE), lambda i: (0, 0)),
            rows,
            rows,
        ],
        out_specs=pl.BlockSpec((ROWS, LAGS), lambda i: (i, 0)),
        out_shape=jax.ShapeDtypeStruct((channels, LAGS), f32),
        scratch_shapes=[
            pltpu.VMEM((unroll, docs * cuts, blocks + deep - 1, TILE), f32),
            pltpu.VMEM((unroll, docs * cuts * blocks, deep * TILE), bf16),
            pltpu.VMEM((unroll, docs * cuts * blocks, PART), bf16),
            pltpu.VMEM((unroll, PART, (deep + 1) * TILE), f32),
        ],
        compiler_params=params(),
        cost_estimate=cost(4),
    )(seg, flip, x, g)


def lone(length):
    return MOST < length <= MOST + PART and 2 * doc_count(length) <= EXTRA


def lone_masks(seg, docs):
    blocks = seg.shape[0]
    long = jnp.zeros(seg.shape, f32)
    row = lax.broadcasted_iota(jnp.int32, (EXTRA, PART), 0)
    ends = jnp.where(row % 2 == 0, seg[:1, :PART], seg[blocks - 1 :, TILE - PART :])
    extra = jnp.zeros((EXTRA, PART), f32)
    for k in range(docs):
        here = (seg == k).astype(f32)
        count = jnp.sum(jnp.sum(here, axis=0, keepdims=True), axis=1, keepdims=True)
        long += jnp.where(count >= MOST, here, 0.0)
        extra += jnp.where((row // 2 == k) & (ends == k) & (count[:, :1] < MOST), 1.0, 0.0)
    return long, extra


def end_rows(z, extra):
    even = lax.broadcasted_iota(jnp.int32, extra.shape, 0) % 2 == 0
    return jnp.where(even, z[:1, :PART], z[z.shape[0] - 1 :, TILE - PART :]) * extra


def store_windows(z, long, extra, zs_ref, zw_ref, u, deep):
    blocks = z.shape[0]
    own = z * long
    after = jnp.concatenate([own[1:], jnp.zeros((1, TILE), f32)], axis=0)
    lane = lax.broadcasted_iota(jnp.int32, own.shape, 1)
    zs_ref[u, 0, :blocks, :] = own
    zs_ref[u, 1, :blocks, :] = pltpu.roll(jnp.where(lane < PART, after, own), TILE - PART, 1)
    for p in range(2):
        for d in range(deep):
            zw_ref[u, p * blocks : (p + 1) * blocks, d * TILE : (d + 1) * TILE] = zs_ref[
                u, p, d : d + blocks, :
            ].astype(bf16)
    ends = end_rows(z, extra)
    zw_ref[u, 2 * blocks :, :TILE] = jnp.concatenate([ends, jnp.zeros_like(ends)], axis=1).astype(bf16)


def turn(x, rows, lanes):
    x = jnp.dot(rows, x, preferred_element_type=f32).astype(bf16)
    return jnp.dot(x, lanes, preferred_element_type=f32)


def lone_conv_kernel(docs, back, seg_ref, rows_ref, lanes_ref, x_ref, tt_ref, y_ref, zs_ref, zw_ref, xr_ref):
    blocks, deep = x_ref.shape[1], tt_ref.shape[2] // TILE
    zw_ref[...] = jnp.zeros(zw_ref.shape, bf16)
    zs_ref[...] = jnp.zeros(zs_ref.shape, f32)
    seg = seg_ref[...].astype(f32)
    if not back:
        rows, lanes = rows_ref[...], lanes_ref[...]
        seg = turn(seg.astype(bf16), rows[:blocks, :blocks], lanes)
        xr_ref[...] = turn(x_ref[...].reshape(ROWS * blocks, TILE), rows, lanes).reshape(xr_ref.shape)
    long, extra = lone_masks(seg, docs)
    even = lax.broadcasted_iota(jnp.int32, extra.shape, 0) % 2 == 0
    place = lax.broadcasted_iota(jnp.int32, (blocks, PART), 0)

    def channel(c, u):
        z = x_ref[c].astype(f32) if back else xr_ref[c]
        store_windows(z, long, extra, zs_ref, zw_ref, u, deep)
        y = lax.dot_general(zw_ref[u], tt_ref[c], NT, preferred_element_type=f32)
        ends = y[2 * blocks :] * extra
        first = jnp.sum(jnp.where(even, ends, 0.0), axis=0, keepdims=True)
        last = jnp.sum(jnp.where(even, 0.0, ends), axis=0, keepdims=True)
        ends = jnp.concatenate([jnp.where(place == 0, first, 0.0), jnp.where(place == blocks - 1, last, 0.0)], axis=1)
        y = jnp.concatenate([y[:blocks], y[blocks : 2 * blocks]], axis=1) * long + ends
        if back:
            y_ref[c] = y.astype(bf16)
        else:
            xr_ref[c] = y

    over_channels(channel, zw_ref.shape[0])
    if not back:
        y = turn(xr_ref[...].astype(bf16).reshape(ROWS * blocks, TILE), rows, lanes)
        y_ref[...] = y.astype(bf16).reshape(y_ref.shape)


def reverse_maps(blocks):
    row = jnp.arange(ROWS * blocks)
    lane = jnp.arange(TILE)
    rows = row[:, None] == (row // blocks * blocks + blocks - 1 - row % blocks)[None, :]
    return rows.astype(bf16), (lane[:, None] == TILE - 1 - lane[None, :]).astype(bf16)


def whole(a):
    return pl.BlockSpec(a.shape, lambda i: (0,) * a.ndim)


def lone_conv(seg, x, tt, back, unroll=4):
    channels, blocks, _ = x.shape
    deep = tt.shape[2] // TILE
    rows, lanes = reverse_maps(blocks)
    cut = pl.BlockSpec((ROWS, blocks, TILE), lambda i: (i, 0, 0))
    return pl.pallas_call(
        functools.partial(lone_conv_kernel, doc_count(blocks * TILE), back),
        grid=(channels // ROWS,),
        in_specs=[
            whole(seg),
            whole(rows),
            whole(lanes),
            cut,
            pl.BlockSpec((ROWS, PART, deep * TILE), lambda i: (i, 0, 0)),
        ],
        out_specs=cut,
        out_shape=jax.ShapeDtypeStruct(x.shape, bf16),
        scratch_shapes=[
            pltpu.VMEM((unroll, 2, blocks + deep - 1, TILE), f32),
            pltpu.VMEM((unroll, 2 * blocks + EXTRA, deep * TILE), bf16),
            pltpu.VMEM((ROWS, blocks, TILE), f32),
        ],
        compiler_params=params(),
        cost_estimate=cost(3),
    )(seg, rows, lanes, x, tt)


def lone_taps_kernel(docs, seg_ref, lanes_ref, x_ref, g_ref, dt_ref, zs_ref, zw_ref, xs_ref, xr_ref):
    blocks = x_ref.shape[1]
    deep = zw_ref.shape[2] // TILE
    zw_ref[...] = jnp.zeros(zw_ref.shape, bf16)
    zs_ref[...] = jnp.zeros(zs_ref.shape, f32)
    lanes = lanes_ref[...]
    seg = seg_ref[...].astype(f32)
    long, extra = lone_masks(seg, docs)
    turned_long, turned_extra = lone_masks(jnp.dot(seg.astype(bf16), lanes, preferred_element_type=f32), docs)
    flat = x_ref[...].reshape(ROWS * blocks, TILE)
    xr_ref[...] = jnp.dot(flat, lanes, preferred_element_type=f32).reshape(xr_ref.shape)

    def channel(c, u):
        store_windows(g_ref[c].astype(f32), long, extra, zs_ref, zw_ref, u, deep)
        x = xr_ref[c]
        own = (x * turned_long).astype(bf16)
        for p in range(2):
            xs_ref[u, p * blocks : (p + 1) * blocks, :] = own[:, p * PART : (p + 1) * PART]
        xs_ref[u, 2 * blocks :, :] = end_rows(x, turned_extra).astype(bf16)
        wide = lax.dot_general(xs_ref[u], zw_ref[u], TN, preferred_element_type=f32)
        wide = jnp.concatenate([wide, jnp.zeros((PART, TILE), f32)], axis=1)
        total = jnp.zeros((8, LAGS), f32)
        for r in range(0, PART, 8):
            total += pltpu.roll(
                wide[r : r + 8], wide.shape[1] - (PART - 1) + r, 1, stride=1, stride_axis=0
            )[:, :LAGS]
        dt_ref[pl.ds(c, 1), :] = jnp.sum(total, axis=0, keepdims=True)

    over_channels(channel, zw_ref.shape[0])


def lone_taps(seg, x, g, unroll=4):
    channels, blocks, _ = x.shape
    deep = lag_blocks(blocks * TILE)
    place = jnp.arange(TILE)
    lanes = (place[:, None] == (place // PART * PART + PART - 1 - place % PART)[None, :]).astype(bf16)
    cut = pl.BlockSpec((ROWS, blocks, TILE), lambda i: (i, 0, 0))
    return pl.pallas_call(
        functools.partial(lone_taps_kernel, doc_count(blocks * TILE)),
        grid=(channels // ROWS,),
        in_specs=[whole(seg), whole(lanes), cut, cut],
        out_specs=pl.BlockSpec((ROWS, LAGS), lambda i: (i, 0)),
        out_shape=jax.ShapeDtypeStruct((channels, LAGS), f32),
        scratch_shapes=[
            pltpu.VMEM((unroll, 2, blocks + deep - 1, TILE), f32),
            pltpu.VMEM((unroll, 2 * blocks + EXTRA, deep * TILE), bf16),
            pltpu.VMEM((unroll, 2 * blocks + EXTRA, PART), bf16),
            pltpu.VMEM((ROWS, blocks, TILE), f32),
        ],
        compiler_params=params(),
        cost_estimate=cost(4),
    )(seg, lanes, x, g)


def mode_grad_kernel(
    lam_log_ref, lam_freq_ref, w_ref, step_ref, dt_ref, qh_ref, gw_ref, gstep_ref, glam_ref, sq_ref, s_ref
):
    lam_re, lam_im, delta = mode_rates(lam_log_ref, lam_freq_ref, step_ref)
    one = first_power(lam_re, lam_im, delta)
    store_squares(one, sq_ref)
    width = sq_ref.shape[-1]
    coarse = LAGS // FINE

    def channel(c, u):
        dt = dt_ref[c]
        dt = jnp.concatenate([dt[:, :FINE], dt[:, FINE:]], axis=0)
        lane = lax.broadcasted_iota(jnp.int32, (coarse, FINE), 1).astype(f32)
        hi, lo = split(jnp.concatenate([dt, dt * lane], axis=0))
        both = jnp.dot(jnp.concatenate([hi, lo], axis=0), qh_ref[c], preferred_element_type=f32)
        v = both[: 2 * coarse] + both[2 * coarse :]
        tiles = coarse_tiles(sq_ref, c)
        power = tuple(jnp.concatenate([t[part] for t in tiles], axis=0) for part in range(2))
        v0 = v[:coarse, :width], v[:coarse, width:]
        row = lax.broadcasted_iota(jnp.int32, (coarse, width), 0)
        far = (row % (coarse // 2)) * (2 * FINE) + (row // (coarse // 2)) * FINE
        far = far.astype(f32)
        v1 = tuple(far * v0[part] + v[coarse:, part * width : (part + 1) * width] for part in range(2))
        for n, pair in enumerate((v0, v1)):
            prod = cmul(power, pair)
            for part in range(2):
                s_ref[2 * n + part, pl.ds(c, 1), :] = jnp.sum(prod[part], axis=0, keepdims=True)

    over_channels(channel, 4)
    modulus = lam_re * lam_re + lam_im * lam_im
    inv = lam_re / modulus, -lam_im / modulus
    shift = one[0] - 1.0, one[1]
    ratio = cmul(shift, inv)
    w = w_ref[0], w_ref[1]
    s0 = s_ref[0], s_ref[1]
    s1 = s_ref[2], s_ref[3]
    coeff = cmul(w, ratio)
    gw = cmul(s0, ratio)
    gw_ref[0], gw_ref[1] = gw[0], -gw[1]
    near = cmul(s0, cmul(w, cmul(one, inv)))
    far = cmul(coeff, s1)
    z = near[0] + far[0], near[1] + far[1]
    back = cmul(s0, cmul(coeff, inv))
    big = delta * z[0] - back[0], delta * z[1] - back[1]
    step = jnp.sum((z[0] * lam_re - z[1] * lam_im) * delta, axis=1, keepdims=True)
    gstep_ref[...] = jnp.broadcast_to(step, gstep_ref.shape)

    @pl.when(pl.program_id(0) == 0)
    def _():
        glam_ref[...] = jnp.zeros(glam_ref.shape, f32)

    glam_ref[0] += big[0] * lam_re
    glam_ref[1] -= big[1]


def mode_grads(lam_log, lam_freq, weights, log_step, dt, fine):
    channels, modes = weights.shape[1:]
    rows = LAGS // TILE
    table = pl.BlockSpec((ROWS, FINE, 2 * modes), lambda i: (i, 0, 0))
    gw, gstep, glam = pl.pallas_call(
        mode_grad_kernel,
        grid=(channels // ROWS,),
        in_specs=[
            pl.BlockSpec((1, modes), lambda i: (0, 0)),
            pl.BlockSpec((1, modes), lambda i: (0, 0)),
            pl.BlockSpec((2, ROWS, modes), lambda i: (0, i, 0)),
            pl.BlockSpec((ROWS, 1), lambda i: (i, 0)),
            pl.BlockSpec((ROWS, rows, TILE), lambda i: (i, 0, 0)),
            table,
        ],
        out_specs=[
            pl.BlockSpec((2, ROWS, modes), lambda i: (0, i, 0)),
            pl.BlockSpec((ROWS, TILE), lambda i: (i, 0)),
            pl.BlockSpec((2, ROWS, modes), lambda i: (0, 0, 0)),
        ],
        out_shape=[
            jax.ShapeDtypeStruct((2, channels, modes), f32),
            jax.ShapeDtypeStruct((channels, TILE), f32),
            jax.ShapeDtypeStruct((2, ROWS, modes), f32),
        ],
        scratch_shapes=[
            pltpu.VMEM((2, 11, ROWS, modes), f32),
            pltpu.VMEM((4, ROWS, modes), f32),
        ],
        compiler_params=params(),
        cost_estimate=cost(2),
    )(lam_log[None], lam_freq[None], weights, log_step[:, None], dt.reshape(channels, rows, TILE), fine)
    return gw, gstep[:, 0], jnp.sum(glam, axis=1)


epsilon = 1e-05
contract_last = (((1,), (1,)), ((), ()))
contract_first = (((0,), (0,)), ((), ()))


def swap(x, k, n_grp):
    return x if k == 0 else lax.ppermute(x, "grp", [(i, i ^ k) for i in range(n_grp)])


def gather_small(x, n_seq):
    held = lax.dynamic_update_index_in_dim(jnp.zeros((n_seq, *x.shape), x.dtype), x, lax.axis_index("seq"), 0)
    for k in range(n_seq.bit_length() - 1):
        held = held + lax.ppermute(held, "seq", [(i, i ^ (1 << k)) for i in range(n_seq)])
    return held


def gelu_parts(v):
    t = jnp.tanh(0.7978845608028654 * (v + 0.044715 * (v * v * v)))
    half = 0.5 * (1.0 + t)
    return v * half, half + 0.5 * v * (1.0 - t * t) * 0.7978845608028654 * (1.0 + 0.134145 * (v * v))


def gather_grp(x, n_grp):
    return [swap(x, k, n_grp) for k in range(n_grp)]


def sum_scatter_grp(pieces, n_grp):
    total = pieces[0].astype(f32)
    for k in range(1, n_grp):
        total = total + swap(pieces[k].astype(bf16), k, n_grp).astype(f32)
    return total


def tree_sum(terms):
    while len(terms) > 1:
        terms = [terms[i] + terms[i + 1] for i in range(0, len(terms), 2)]
    return terms[0]


def sum_grp(x, n_grp):
    return tree_sum([y.astype(f32) for y in gather_grp(x.astype(bf16), n_grp)])


def place_grp(x, n_grp, me, axis):
    held = jnp.stack(gather_grp(x, n_grp))
    rows = [lax.dynamic_index_in_dim(held, (me ^ j).astype(jnp.uint32), 0, keepdims=False) for j in range(n_grp)]
    return jnp.stack(rows, axis=axis)


def body(
    n_grp,
    n_seq,
    layer_input,
    segments,
    ln_gain,
    ln_bias,
    w_value,
    b_value,
    w_reduce,
    b_reduce,
    lam_log,
    lam_freq,
    dss_w,
    log_step,
    w_up,
    b_up,
    w_out,
    b_out,
    out_cotangent,
):
    me = lax.axis_index("grp")
    tokens, wide = layer_input.shape
    part = w_value.shape[0] // n_grp
    quarter = n_seq * part
    reduced_width = w_reduce.shape[0] * n_seq

    small = (ln_gain, ln_bias, b_value, b_reduce, lam_log, lam_freq, b_up, b_out, segments[0].astype(bf16))
    packed = jnp.concatenate([jnp.pad(v, (0, -v.shape[0] % 128)).reshape(-1, 128) for v in small], axis=0)
    packed = jnp.pad(packed, ((0, -packed.shape[0] % 16), (0, 0)))
    packed = gather_small(packed, n_seq)
    spots, fulls = 0, []
    for array in small:
        deep = -(-array.shape[0] // 128)
        fulls.append(packed[:, spots : spots + deep].reshape(n_seq, -1)[:, : array.shape[0]])
        spots += deep
    gain_full, bias_full, value_bias, reduce_bias, decay_full, freq_full, up_bias, out_bias, doc_row = fulls
    gain_wide = gain_full.reshape(-1).astype(f32)
    bias_wide = bias_full.reshape(-1).astype(f32)
    value_bias = lax.dynamic_slice_in_dim(value_bias, me * part, part, 1).reshape(-1).astype(f32)
    up_bias = lax.dynamic_slice_in_dim(up_bias, me * part, part, 1).reshape(-1).astype(f32)

    reduce_full = lax.all_gather(w_reduce, "seq", axis=0, tiled=True)
    pieces = [lax.dynamic_slice_in_dim(w, me * part, part, 0) for w in (w_value, w_up)]
    both_part = lax.all_gather(jnp.concatenate(pieces, axis=1), "seq", axis=0, tiled=True)
    value_part, up_part = both_part[:, :wide], both_part[:, wide:]
    out_cols = lax.dynamic_index_in_dim(w_out.reshape(-1, n_seq, n_grp, part), me, 2, keepdims=False)
    out_part = lax.all_gather(out_cols.reshape(-1, quarter), "seq", axis=0, tiled=True)

    length = tokens * n_seq
    blocks = length // TILE
    deep = lag_blocks(length)
    decay = decay_full.reshape(-1).astype(f32)
    freq = freq_full.reshape(-1).astype(f32)
    weights = dss_w.astype(f32)
    steps = log_step.astype(f32)
    half = steps.shape[0] // 2
    modes = [
        (decay, freq, weights[:, :half], steps[:half]),
        (decay, freq, weights[:, half:], steps[half:]),
    ]
    tables = [make_toeplitz(*modes[0], deep)]
    fine, cot_own = lax.optimization_barrier((tables[0][1], out_cotangent))
    tables = [(tables[0][0], fine)]
    cot_parts = gather_grp(cot_own, n_grp)

    x_wide = layer_input.astype(f32)
    center = x_wide - jnp.mean(x_wide, axis=1, keepdims=True)
    inverse = lax.rsqrt(jnp.mean(center * center, axis=1, keepdims=True) + epsilon)
    unit = center * inverse
    normed = (unit * gain_wide + bias_wide).astype(bf16)

    pre_reduce = (
        lax.dot_general(reduce_full, normed, contract_last, preferred_element_type=f32)
        + reduce_bias.reshape(-1).astype(f32)[:, None]
    )
    reduced, reduce_slope = gelu_parts(pre_reduce)
    reduced = reduced.astype(bf16)
    reduced, later, normed_own, last = lax.optimization_barrier((reduced, modes[1][0], normed, tables[0]))
    cot_parts, _ = lax.optimization_barrier((cot_parts, reduced))
    cot_all = jnp.concatenate(cot_parts, axis=0)
    tables[0] = last
    tables.append(make_toeplitz(later, *modes[1][1:], deep))
    normed_all = jnp.concatenate(gather_grp(normed_own, n_grp), axis=0)
    channel_in = lax.all_to_all(reduced, "seq", split_axis=0, concat_axis=1, tiled=True)
    seg = doc_row.astype(jnp.int32).reshape(blocks, TILE)
    signal = channel_in.reshape(-1, blocks, TILE)
    halves = [slice(0, half), slice(half, 2 * half)]
    convolve, sum_lags = (lone_conv, lone_taps) if lone(length) else (any_conv, taps_grad)
    channel_out = jnp.concatenate(
        [convolve(seg, signal[h], t[0], False) for h, t in zip(halves, tables)], axis=0
    ).reshape(-1, length)
    mixed = lax.all_to_all(channel_out, "seq", split_axis=1, concat_axis=0, tiled=True)
    mixed_all = jnp.concatenate(gather_grp(mixed, n_grp), axis=1)

    pre_value = lax.dot_general(normed_all, value_part, contract_last, preferred_element_type=f32) + value_bias
    activated, slope = lax.optimization_barrier(gelu_parts(pre_value))
    g_gated = jnp.dot(cot_all, out_part, preferred_element_type=f32)
    pre_up = lax.dot_general(mixed_all, up_part, (((0,), (1,)), ((), ())), preferred_element_type=f32) + up_bias
    gated = (activated * pre_up).astype(bf16)
    g_activated = g_gated * pre_up
    g_pre_up = (g_gated * activated).astype(bf16)
    g_pre_value = (g_activated * slope).astype(bf16)

    g_mixed = lax.dot_general(up_part, g_pre_up, (((0,), (1,)), ((), ())), preferred_element_type=f32)
    g_mixed = sum_scatter_grp([g_mixed[:, k * tokens : (k + 1) * tokens] for k in range(n_grp)], n_grp)
    added = lax.dot_general(gated, out_part, contract_last, preferred_element_type=f32)
    g_normed = jnp.dot(g_pre_value, value_part, preferred_element_type=f32)
    both = jnp.concatenate([added.astype(bf16), g_normed.astype(bf16)], axis=1)
    g_mixed, gated, g_pre_up, g_pre_value, both = lax.optimization_barrier(
        (g_mixed.astype(bf16), gated, g_pre_up, g_pre_value, both)
    )
    g_channel = lax.all_to_all(g_mixed, "seq", split_axis=0, concat_axis=1, tiled=True)
    g_channel = g_channel.reshape(-1, blocks, TILE)
    g_out = lax.dot_general(cot_all, gated, contract_first, preferred_element_type=f32).astype(bf16)
    g_up = lax.dot_general(g_pre_up, mixed_all, (((0,), (1,)), ((), ())), preferred_element_type=f32)
    g_value = lax.dot_general(g_pre_value, normed_all, contract_first, preferred_element_type=f32)
    left = (jnp.arange(TILE) < TILE // 2).astype(bf16)
    ones = [jnp.broadcast_to(m, (g_pre_value.shape[0], TILE)) for m in (left, 1 - left)]
    g_biases = lax.dot_general(g_pre_value, ones[0], contract_first, preferred_element_type=f32)
    g_biases += lax.dot_general(g_pre_up, ones[1], contract_first, preferred_element_type=f32)
    g_both = jnp.concatenate([y.astype(bf16) for y in (g_value, g_up, g_biases)], axis=1)
    g_channel, g_out, g_both, both = lax.optimization_barrier((g_channel, g_out, g_both, both))
    g_out = lax.psum_scatter(g_out, "seq", scatter_dimension=0, tiled=True)
    g_both = lax.psum_scatter(g_both, "seq", scatter_dimension=0, tiled=True)
    g_signal = jnp.concatenate([convolve(seg, g_channel[h], t[0], True) for h, t in zip(halves, tables)], axis=0)
    g_signal, g_channel = lax.optimization_barrier((g_signal, g_channel))
    g_reduced = lax.all_to_all(g_signal.reshape(-1, length), "seq", split_axis=1, concat_axis=0, tiled=True)
    g_taps = sum_lags(seg, signal, g_channel)
    g_taps, g_reduced = lax.optimization_barrier((g_taps, g_reduced))
    found = [mode_grads(*m, g_taps[h], *t[1:]) for h, m, t in zip(halves, modes, tables)]
    g_lam = found[0][2] + found[1][2]
    states = g_lam.shape[1]
    both = sum_scatter_grp([both[k * tokens : (k + 1) * tokens] for k in range(n_grp)], n_grp)
    added, g_normed = both[:, :wide], both[:, wide:]
    output = (x_wide + added + out_bias.reshape(-1).astype(f32)).astype(bf16)

    g_pre_reduce = (g_reduced.astype(f32) * reduce_slope).astype(bf16)
    g_reduce = jnp.dot(g_pre_reduce, normed, preferred_element_type=f32)
    g_normed = g_normed + lax.dot_general(g_pre_reduce, reduce_full, contract_first, preferred_element_type=f32)
    g_unit = g_normed * gain_wide
    g_input = inverse * (
        g_unit
        - jnp.mean(g_unit, axis=1, keepdims=True)
        - unit * jnp.mean(g_unit * unit, axis=1, keepdims=True)
    ) + out_cotangent.astype(f32)

    vectors = (
        jnp.sum(g_normed * unit, axis=0).reshape(n_seq, -1),
        jnp.sum(g_normed, axis=0).reshape(n_seq, -1),
        jnp.sum(g_pre_reduce.astype(f32), axis=1).reshape(n_seq, -1),
        g_lam[0].reshape(n_seq, -1),
        g_lam[1].reshape(n_seq, -1),
        jnp.sum(out_cotangent.astype(f32), axis=0).reshape(n_seq, -1),
    )
    flat = jnp.concatenate(vectors, axis=1)
    flat = jnp.pad(flat, ((0, 0), (0, -flat.shape[1] % wide))).reshape(n_seq, -1, wide)
    own = jnp.concatenate([g_reduce.reshape(n_seq, -1, wide).astype(bf16), flat.astype(bf16)], axis=1)
    own, g_out, g_both = lax.optimization_barrier((own, g_out, g_both))
    own = lax.psum_scatter(own, "seq", scatter_dimension=0, tiled=False)
    packed = [f[0][i].reshape(-1) for i in range(2) for f in found] + [f[1] for f in found]
    packed.append(jnp.zeros((-2 * half % wide,), f32))
    packed = jnp.concatenate(packed).reshape(-1, wide).astype(bf16)
    packed = sum_grp(packed, n_grp)
    own = sum_grp(own, n_grp)
    g_reduce, shard = own[: w_reduce.shape[0]], own[w_reduce.shape[0] :].reshape(-1)
    g_weights = packed[:-1].reshape(2, -1, states)
    g_step = packed[-1][: 2 * half]
    placed = place_grp(g_out, n_grp, me, 0)
    g_out = placed.reshape(n_grp, -1, n_seq, part).transpose(1, 2, 0, 3).reshape(w_out.shape).astype(f32)
    placed = place_grp(g_both, n_grp, me, 0).reshape(w_value.shape[0], -1).astype(f32)
    g_value, g_up = placed[:, :wide], placed[:, wide : wide + w_up.shape[1]]
    g_value_bias, g_up_bias = placed[:, wide + w_up.shape[1]], placed[:, -1]
    sums, spots = [], 0
    for array in vectors:
        sums.append(shard[spots : spots + array.shape[1]])
        spots += array.shape[1]
    g_gain, g_bias, g_reduce_bias, g_decay, g_freq, g_out_bias = sums
    return (
        output,
        g_input,
        g_gain,
        g_bias,
        g_value,
        g_value_bias,
        g_reduce,
        g_reduce_bias,
        g_decay,
        g_freq,
        g_weights,
        g_step,
        g_up,
        g_up_bias,
        g_out,
        g_out_bias,
    )


def solution(mesh):
    by_token = P(("grp", "seq"), None)
    row, matrix, cube = P("seq"), P("seq", None), P(None, "seq", None)
    layer = (row, row, matrix, row, matrix, row, row, row, cube, row, matrix, row, matrix, row)
    return jax.shard_map(
        functools.partial(body, mesh.shape["grp"], mesh.shape["seq"]),
        mesh=mesh,
        in_specs=(by_token, P("grp", "seq"), *layer, by_token),
        out_specs=(by_token, by_token, *layer),
        check_vma=False,
    )
```

```python
import functools

import jax
import jax.numpy as jnp
from jax import lax
from jax.experimental import pallas as pl
from jax.experimental.pallas import tpu as pltpu
from jax.sharding import PartitionSpec as P

f32, bf16 = jnp.float32, jnp.bfloat16
TILE = 128
MOST = 2000
LAGS = 2048
FINE = 64
EXTRA = 16
PART = 64
ROWS = 8
NT = (((1,), (1,)), ((), ()))
TN = (((0,), (0,)), ((), ()))


def params(mb=48):
    return pltpu.CompilerParams(vmem_limit_bytes=mb << 20)


def cost(us):
    return pl.CostEstimate(flops=us * 10**9, bytes_accessed=us * 10**6, transcendentals=0)


def lag_blocks(length):
    return min(length // TILE, (MOST + TILE - 2) // TILE + 1)


def doc_count(length):
    return length // 1024 + 1


def over_channels(step, unroll):
    def some(i, _):
        for u in range(unroll):
            step(i * unroll + u, u)
        return 0

    lax.fori_loop(0, ROWS // unroll, some, 0)


def cmul(a, b):
    return (a[0] * b[0] - a[1] * b[1], a[0] * b[1] + a[1] * b[0])


def mode_rates(lam_log_ref, lam_freq_ref, step_ref):
    lam_re = -jnp.exp(lam_log_ref[...])
    lam_im = lam_freq_ref[...]
    delta = jnp.exp(step_ref[...])
    return lam_re, lam_im, delta


def first_power(lam_re, lam_im, delta):
    growth = jnp.exp(delta * lam_re)
    phase = delta * lam_im
    return growth * jnp.cos(phase), growth * jnp.sin(phase)


def store_squares(one, sq_ref):
    cur = one
    for k in range(11):
        sq_ref[0, k], sq_ref[1, k] = cur
        if k < 10:
            cur = cmul(cur, cur)


def power_tiles(sq_ref, c, first, count):
    def sq(k):
        return sq_ref[0, k, pl.ds(c, 1), :], sq_ref[1, k, pl.ds(c, 1), :]

    width = sq_ref.shape[-1]
    row = lax.broadcasted_iota(jnp.int32, (8, width), 0)
    tile = None
    for k in range(3):
        re, im = sq(first + k)
        on = (row & (1 << k)) != 0
        term = jnp.where(on, re, 1.0), jnp.where(on, im, 0.0)
        tile = term if tile is None else cmul(tile, term)
    tiles, k = [tile], 3
    while len(tiles) < count:
        step = sq(first + k)
        tiles = tiles + [cmul(t, step) for t in tiles]
        k += 1
    return tiles


def split(x):
    hi = x.astype(bf16)
    return hi, (x - hi.astype(f32)).astype(bf16)


def coarse_tiles(sq_ref, c):
    even = power_tiles(sq_ref, c, 7, LAGS // TILE // 8)
    half = sq_ref[0, 6, pl.ds(c, 1), :], sq_ref[1, 6, pl.ds(c, 1), :]
    return even + [cmul(t, half) for t in even]


def taps_kernel(
    lam_log_ref, lam_freq_ref, w_ref, step_ref, tt_ref, qh_ref, sq_ref, cf_ref, p_ref, ql_ref
):
    lam_re, lam_im, delta = mode_rates(lam_log_ref, lam_freq_ref, step_ref)
    one = first_power(lam_re, lam_im, delta)
    store_squares(one, sq_ref)
    modulus = lam_re * lam_re + lam_im * lam_im
    shift_re, shift_im = one[0] - 1.0, one[1]
    ratio = (
        (shift_re * lam_re + shift_im * lam_im) / modulus,
        (shift_im * lam_re - shift_re * lam_im) / modulus,
    )
    cf_ref[0], cf_ref[1] = cmul((w_ref[0], w_ref[1]), ratio)
    width = sq_ref.shape[-1]
    deep = tt_ref.shape[2] // TILE
    coarse = LAGS // FINE

    def channel(c, u):
        for t, pair in enumerate(power_tiles(sq_ref, c, 0, FINE // 8)):
            if t % 2 == 0:
                held = pair
                continue
            for part in range(2):
                hi, lo = split(jnp.concatenate([held[part], pair[part]], axis=0))
                qh_ref[c, 8 * t - 8 : 8 * t + 8, part * width : (part + 1) * width] = hi
                ql_ref[u, 8 * t - 8 : 8 * t + 8, part * width : (part + 1) * width] = lo
        coeff = cf_ref[0, pl.ds(c, 1), :], cf_ref[1, pl.ds(c, 1), :]
        tiles = [cmul(t, coeff) for t in coarse_tiles(sq_ref, c)]
        for part, sign in ((0, 1.0), (1, -1.0)):
            hi, lo = split(sign * jnp.concatenate([t[part] for t in tiles], axis=0))
            p_ref[u, :coarse, part * width : (part + 1) * width] = hi
            p_ref[u, coarse:, part * width : (part + 1) * width] = lo
        both = lax.dot_general(qh_ref[c], p_ref[u], NT, preferred_element_type=f32)
        low = lax.dot_general(ql_ref[u], p_ref[u, :coarse], NT, preferred_element_type=f32)
        taps = (both[:, :coarse] + both[:, coarse:] + low).T
        taps = jnp.concatenate([taps[: coarse // 2], taps[coarse // 2 :]], axis=1)
        rows = [jnp.broadcast_to(taps[d : d + 1], (8, TILE)) for d in range(min(deep, LAGS // TILE))]
        gap = jnp.zeros((8, TILE), f32)
        source = jnp.concatenate([gap] + rows + [gap] * (deep - len(rows)), axis=1)
        for r in range(PART // 16):
            pair = [pltpu.roll(source, 16 * r + s, 1, stride=1, stride_axis=0)[:, TILE:] for s in (0, 8)]
            tt_ref[c, 16 * r : 16 * r + 16, :] = jnp.concatenate(pair, axis=0).astype(bf16)

    over_channels(channel, p_ref.shape[0])


def make_toeplitz(lam_log, lam_freq, weights, log_step, deep):
    channels, modes = weights.shape[1:]
    table = pl.BlockSpec((ROWS, FINE, 2 * modes), lambda i: (i, 0, 0))
    return pl.pallas_call(
        taps_kernel,
        grid=(channels // ROWS,),
        in_specs=[
            pl.BlockSpec((1, modes), lambda i: (0, 0)),
            pl.BlockSpec((1, modes), lambda i: (0, 0)),
            pl.BlockSpec((2, ROWS, modes), lambda i: (0, i, 0)),
            pl.BlockSpec((ROWS, 1), lambda i: (i, 0)),
        ],
        out_specs=[pl.BlockSpec((ROWS, PART, deep * TILE), lambda i: (i, 0, 0)), table],
        out_shape=[
            jax.ShapeDtypeStruct((channels, PART, deep * TILE), bf16),
            jax.ShapeDtypeStruct((channels, FINE, 2 * modes), bf16),
        ],
        scratch_shapes=[
            pltpu.VMEM((2, 11, ROWS, modes), f32),
            pltpu.VMEM((2, ROWS, modes), f32),
            pltpu.VMEM((4, 2 * LAGS // FINE, 2 * modes), bf16),
            pltpu.VMEM((4, FINE, 2 * modes), bf16),
        ],
        compiler_params=params(),
        cost_estimate=cost(3),
    )(lam_log[None], lam_freq[None], weights, log_step[:, None])


def doc_windows(z, seg, docs, zs_ref, zw_ref, u, deep):
    blocks = z.shape[0]
    lane = lax.broadcasted_iota(jnp.int32, z.shape, 1)
    for k in range(docs):
        own = jnp.where(seg == k, z, 0.0)
        after = jnp.concatenate([own[1:], jnp.zeros((1, TILE), f32)], axis=0)
        zs_ref[u, 2 * k, :blocks, :] = own
        zs_ref[u, 2 * k + 1, :blocks, :] = pltpu.roll(jnp.where(lane < PART, after, own), TILE - PART, 1)
    for k in range(2 * docs):
        for d in range(deep):
            zw_ref[u, k * blocks : (k + 1) * blocks, d * TILE : (d + 1) * TILE] = zs_ref[
                u, k, d : d + blocks, :
            ].astype(bf16)


def conv_kernel(docs, back, seg_ref, rows_ref, lanes_ref, x_ref, tt_ref, y_ref, zs_ref, zw_ref, xr_ref):
    blocks, deep = x_ref.shape[1], tt_ref.shape[2] // TILE
    zs_ref[...] = jnp.zeros(zs_ref.shape, f32)
    seg = seg_ref[...].astype(f32)
    if not back:
        rows, lanes = rows_ref[...], lanes_ref[...]
        seg = turn(seg.astype(bf16), rows[:blocks, :blocks], lanes)
        xr_ref[...] = turn(x_ref[...].reshape(ROWS * blocks, TILE), rows, lanes).reshape(xr_ref.shape)

    def channel(c, u):
        z = x_ref[c].astype(f32) if back else xr_ref[c]
        doc_windows(z, seg, docs, zs_ref, zw_ref, u, deep)
        y = lax.dot_general(zw_ref[u], tt_ref[c], NT, preferred_element_type=f32)
        out = jnp.zeros((blocks, TILE), f32)
        for k in range(docs):
            at = 2 * k * blocks
            mine = jnp.concatenate([y[at : at + blocks], y[at + blocks : at + 2 * blocks]], axis=1)
            out = jnp.where(seg == k, mine, out)
        if back:
            y_ref[c] = out.astype(bf16)
        else:
            xr_ref[c] = out

    over_channels(channel, zw_ref.shape[0])
    if not back:
        y = turn(xr_ref[...].astype(bf16).reshape(ROWS * blocks, TILE), rows, lanes)
        y_ref[...] = y.astype(bf16).reshape(y_ref.shape)


def any_conv(seg, x, tt, back, unroll=2):
    channels, blocks, _ = x.shape
    deep = tt.shape[2] // TILE
    docs = doc_count(blocks * TILE)
    rows, lanes = reverse_maps(blocks)
    cut = pl.BlockSpec((ROWS, blocks, TILE), lambda i: (i, 0, 0))
    return pl.pallas_call(
        functools.partial(conv_kernel, docs, back),
        grid=(channels // ROWS,),
        in_specs=[
            whole(seg),
            whole(rows),
            whole(lanes),
            cut,
            pl.BlockSpec((ROWS, PART, deep * TILE), lambda i: (i, 0, 0)),
        ],
        out_specs=cut,
        out_shape=jax.ShapeDtypeStruct(x.shape, bf16),
        scratch_shapes=[
            pltpu.VMEM((unroll, 2 * docs, blocks + deep - 1, TILE), f32),
            pltpu.VMEM((unroll, 2 * docs * blocks, deep * TILE), bf16),
            pltpu.VMEM((ROWS, blocks, TILE), f32),
        ],
        compiler_params=params(),
        cost_estimate=cost(3),
    )(seg, rows, lanes, x, tt)


def taps_grad_kernel(docs, seg_ref, flip_ref, x_ref, g_ref, dt_ref, gs_ref, gw_ref, xst_ref, wide_ref):
    wide_ref[...] = jnp.zeros(wide_ref.shape, f32)
    blocks = x_ref.shape[1]
    deep = gw_ref.shape[2] // TILE
    lead = deep - 1
    cuts = TILE // PART
    seg = seg_ref[...]
    lane = lax.broadcasted_iota(jnp.int32, (blocks, TILE), 1)
    for u in range(gs_ref.shape[0]):
        for k in range(docs * cuts):
            gs_ref[u, k, blocks:, :] = jnp.zeros((lead, TILE), f32)

    def one(c, u):
        g = g_ref[c].astype(f32)
        x = x_ref[c].astype(f32)
        for k in range(docs):
            own = jnp.where(seg == k, g, 0.0)
            gs_ref[u, k * cuts, :blocks, :] = own
            after = jnp.concatenate([own[1:], jnp.zeros((1, TILE), f32)], axis=0)
            for p in range(1, cuts):
                gs_ref[u, k * cuts + p, :blocks, :] = pltpu.roll(
                    jnp.where(lane < p * PART, after, own), TILE - p * PART, 1
                )
            mine = jnp.where(seg == k, x, 0.0).astype(bf16)
            mine = jnp.dot(mine, flip_ref[...], preferred_element_type=f32).astype(bf16)
            for p in range(cuts):
                at = (k * cuts + p) * blocks
                xst_ref[u, at : at + blocks, :] = mine[:, p * PART : (p + 1) * PART]
        for k in range(docs * cuts):
            for d in range(deep):
                gw_ref[u, k * blocks : (k + 1) * blocks, d * TILE : (d + 1) * TILE] = gs_ref[
                    u, k, d : d + blocks, :
                ].astype(bf16)
        wide_ref[u, :, : deep * TILE] = lax.dot_general(xst_ref[u], gw_ref[u], TN, preferred_element_type=f32)
        total = jnp.zeros((8, LAGS), f32)
        for r in range(0, PART, 8):
            rows = wide_ref[u, r : r + 8, :]
            total += pltpu.roll(rows, rows.shape[1] - (PART - 1) + r, 1, stride=1, stride_axis=0)[:, :LAGS]
        dt_ref[pl.ds(c, 1), :] = jnp.sum(total, axis=0, keepdims=True)

    def pair(i, _):
        for u in range(gs_ref.shape[0]):
            one(i * gs_ref.shape[0] + u, u)
        return 0

    lax.fori_loop(0, ROWS // gs_ref.shape[0], pair, 0)


def taps_grad(seg, x, g, unroll=4):
    channels, blocks, _ = x.shape
    deep = lag_blocks(blocks * TILE)
    docs = doc_count(blocks * TILE)
    cuts = TILE // PART
    place = jnp.arange(TILE)
    flip = (place[:, None] == (place // PART * PART + PART - 1 - place % PART)[None, :]).astype(bf16)
    rows = pl.BlockSpec((ROWS, blocks, TILE), lambda i: (i, 0, 0))
    return pl.pallas_call(
        functools.partial(taps_grad_kernel, docs),
        grid=(channels // ROWS,),
        in_specs=[
            pl.BlockSpec((blocks, TILE), lambda i: (0, 0)),
            pl.BlockSpec((TILE, TILE), lambda i: (0, 0)),
            rows,
            rows,
        ],
        out_specs=pl.BlockSpec((ROWS, LAGS), lambda i: (i, 0)),
        out_shape=jax.ShapeDtypeStruct((channels, LAGS), f32),
        scratch_shapes=[
            pltpu.VMEM((unroll, docs * cuts, blocks + deep - 1, TILE), f32),
            pltpu.VMEM((unroll, docs * cuts * blocks, deep * TILE), bf16),
            pltpu.VMEM((unroll, docs * cuts * blocks, PART), bf16),
            pltpu.VMEM((unroll, PART, (deep + 1) * TILE), f32),
        ],
        compiler_params=params(),
        cost_estimate=cost(4),
    )(seg, flip, x, g)


def lone(length):
    return MOST < length <= MOST + PART and 2 * doc_count(length) <= EXTRA


def lone_masks(seg, docs):
    blocks = seg.shape[0]
    long = jnp.zeros(seg.shape, f32)
    row = lax.broadcasted_iota(jnp.int32, (EXTRA, PART), 0)
    ends = jnp.where(row % 2 == 0, seg[:1, :PART], seg[blocks - 1 :, TILE - PART :])
    extra = jnp.zeros((EXTRA, PART), f32)
    for k in range(docs):
        here = (seg == k).astype(f32)
        count = jnp.sum(jnp.sum(here, axis=0, keepdims=True), axis=1, keepdims=True)
        long += jnp.where(count >= MOST, here, 0.0)
        extra += jnp.where((row // 2 == k) & (ends == k) & (count[:, :1] < MOST), 1.0, 0.0)
    return long, extra


def end_rows(z, extra):
    even = lax.broadcasted_iota(jnp.int32, extra.shape, 0) % 2 == 0
    return jnp.where(even, z[:1, :PART], z[z.shape[0] - 1 :, TILE - PART :]) * extra


def store_windows(z, long, extra, zs_ref, zw_ref, u, deep):
    blocks = z.shape[0]
    own = z * long
    after = jnp.concatenate([own[1:], jnp.zeros((1, TILE), f32)], axis=0)
    lane = lax.broadcasted_iota(jnp.int32, own.shape, 1)
    zs_ref[u, 0, :blocks, :] = own
    zs_ref[u, 1, :blocks, :] = pltpu.roll(jnp.where(lane < PART, after, own), TILE - PART, 1)
    for p in range(2):
        for d in range(deep):
            zw_ref[u, p * blocks : (p + 1) * blocks, d * TILE : (d + 1) * TILE] = zs_ref[
                u, p, d : d + blocks, :
            ].astype(bf16)
    ends = end_rows(z, extra)
    zw_ref[u, 2 * blocks :, :TILE] = jnp.concatenate([ends, jnp.zeros_like(ends)], axis=1).astype(bf16)


def turn(x, rows, lanes):
    x = jnp.dot(rows, x, preferred_element_type=f32).astype(bf16)
    return jnp.dot(x, lanes, preferred_element_type=f32)


def lone_conv_kernel(docs, back, seg_ref, rows_ref, lanes_ref, x_ref, tt_ref, y_ref, zs_ref, zw_ref, xr_ref):
    blocks, deep = x_ref.shape[1], tt_ref.shape[2] // TILE
    zw_ref[...] = jnp.zeros(zw_ref.shape, bf16)
    zs_ref[...] = jnp.zeros(zs_ref.shape, f32)
    seg = seg_ref[...].astype(f32)
    if not back:
        rows, lanes = rows_ref[...], lanes_ref[...]
        seg = turn(seg.astype(bf16), rows[:blocks, :blocks], lanes)
        xr_ref[...] = turn(x_ref[...].reshape(ROWS * blocks, TILE), rows, lanes).reshape(xr_ref.shape)
    long, extra = lone_masks(seg, docs)
    even = lax.broadcasted_iota(jnp.int32, extra.shape, 0) % 2 == 0
    place = lax.broadcasted_iota(jnp.int32, (blocks, PART), 0)

    def channel(c, u):
        z = x_ref[c].astype(f32) if back else xr_ref[c]
        store_windows(z, long, extra, zs_ref, zw_ref, u, deep)
        y = lax.dot_general(zw_ref[u], tt_ref[c], NT, preferred_element_type=f32)
        ends = y[2 * blocks :] * extra
        first = jnp.sum(jnp.where(even, ends, 0.0), axis=0, keepdims=True)
        last = jnp.sum(jnp.where(even, 0.0, ends), axis=0, keepdims=True)
        ends = jnp.concatenate([jnp.where(place == 0, first, 0.0), jnp.where(place == blocks - 1, last, 0.0)], axis=1)
        y = jnp.concatenate([y[:blocks], y[blocks : 2 * blocks]], axis=1) * long + ends
        if back:
            y_ref[c] = y.astype(bf16)
        else:
            xr_ref[c] = y

    over_channels(channel, zw_ref.shape[0])
    if not back:
        y = turn(xr_ref[...].astype(bf16).reshape(ROWS * blocks, TILE), rows, lanes)
        y_ref[...] = y.astype(bf16).reshape(y_ref.shape)


def reverse_maps(blocks):
    row = jnp.arange(ROWS * blocks)
    lane = jnp.arange(TILE)
    rows = row[:, None] == (row // blocks * blocks + blocks - 1 - row % blocks)[None, :]
    return rows.astype(bf16), (lane[:, None] == TILE - 1 - lane[None, :]).astype(bf16)


def whole(a):
    return pl.BlockSpec(a.shape, lambda i: (0,) * a.ndim)


def lone_conv(seg, x, tt, back, unroll=4):
    channels, blocks, _ = x.shape
    deep = tt.shape[2] // TILE
    rows, lanes = reverse_maps(blocks)
    cut = pl.BlockSpec((ROWS, blocks, TILE), lambda i: (i, 0, 0))
    return pl.pallas_call(
        functools.partial(lone_conv_kernel, doc_count(blocks * TILE), back),
        grid=(channels // ROWS,),
        in_specs=[
            whole(seg),
            whole(rows),
            whole(lanes),
            cut,
            pl.BlockSpec((ROWS, PART, deep * TILE), lambda i: (i, 0, 0)),
        ],
        out_specs=cut,
        out_shape=jax.ShapeDtypeStruct(x.shape, bf16),
        scratch_shapes=[
            pltpu.VMEM((unroll, 2, blocks + deep - 1, TILE), f32),
            pltpu.VMEM((unroll, 2 * blocks + EXTRA, deep * TILE), bf16),
            pltpu.VMEM((ROWS, blocks, TILE), f32),
        ],
        compiler_params=params(),
        cost_estimate=cost(3),
    )(seg, rows, lanes, x, tt)


def lone_taps_kernel(docs, seg_ref, lanes_ref, x_ref, g_ref, dt_ref, zs_ref, zw_ref, xs_ref, xr_ref):
    blocks = x_ref.shape[1]
    deep = zw_ref.shape[2] // TILE
    zw_ref[...] = jnp.zeros(zw_ref.shape, bf16)
    zs_ref[...] = jnp.zeros(zs_ref.shape, f32)
    lanes = lanes_ref[...]
    seg = seg_ref[...].astype(f32)
    long, extra = lone_masks(seg, docs)
    turned_long, turned_extra = lone_masks(jnp.dot(seg.astype(bf16), lanes, preferred_element_type=f32), docs)
    flat = x_ref[...].reshape(ROWS * blocks, TILE)
    xr_ref[...] = jnp.dot(flat, lanes, preferred_element_type=f32).reshape(xr_ref.shape)

    def channel(c, u):
        store_windows(g_ref[c].astype(f32), long, extra, zs_ref, zw_ref, u, deep)
        x = xr_ref[c]
        own = (x * turned_long).astype(bf16)
        for p in range(2):
            xs_ref[u, p * blocks : (p + 1) * blocks, :] = own[:, p * PART : (p + 1) * PART]
        xs_ref[u, 2 * blocks :, :] = end_rows(x, turned_extra).astype(bf16)
        wide = lax.dot_general(xs_ref[u], zw_ref[u], TN, preferred_element_type=f32)
        wide = jnp.concatenate([wide, jnp.zeros((PART, TILE), f32)], axis=1)
        total = jnp.zeros((8, LAGS), f32)
        for r in range(0, PART, 8):
            total += pltpu.roll(
                wide[r : r + 8], wide.shape[1] - (PART - 1) + r, 1, stride=1, stride_axis=0
            )[:, :LAGS]
        dt_ref[pl.ds(c, 1), :] = jnp.sum(total, axis=0, keepdims=True)

    over_channels(channel, zw_ref.shape[0])


def lone_taps(seg, x, g, unroll=4):
    channels, blocks, _ = x.shape
    deep = lag_blocks(blocks * TILE)
    place = jnp.arange(TILE)
    lanes = (place[:, None] == (place // PART * PART + PART - 1 - place % PART)[None, :]).astype(bf16)
    cut = pl.BlockSpec((ROWS, blocks, TILE), lambda i: (i, 0, 0))
    return pl.pallas_call(
        functools.partial(lone_taps_kernel, doc_count(blocks * TILE)),
        grid=(channels // ROWS,),
        in_specs=[whole(seg), whole(lanes), cut, cut],
        out_specs=pl.BlockSpec((ROWS, LAGS), lambda i: (i, 0)),
        out_shape=jax.ShapeDtypeStruct((channels, LAGS), f32),
        scratch_shapes=[
            pltpu.VMEM((unroll, 2, blocks + deep - 1, TILE), f32),
            pltpu.VMEM((unroll, 2 * blocks + EXTRA, deep * TILE), bf16),
            pltpu.VMEM((unroll, 2 * blocks + EXTRA, PART), bf16),
            pltpu.VMEM((ROWS, blocks, TILE), f32),
        ],
        compiler_params=params(),
        cost_estimate=cost(4),
    )(seg, lanes, x, g)


def mode_grad_kernel(
    lam_log_ref, lam_freq_ref, w_ref, step_ref, dt_ref, qh_ref, gw_ref, gstep_ref, glam_ref, sq_ref, s_ref
):
    lam_re, lam_im, delta = mode_rates(lam_log_ref, lam_freq_ref, step_ref)
    one = first_power(lam_re, lam_im, delta)
    store_squares(one, sq_ref)
    width = sq_ref.shape[-1]
    coarse = LAGS // FINE

    def channel(c, u):
        dt = dt_ref[c]
        dt = jnp.concatenate([dt[:, :FINE], dt[:, FINE:]], axis=0)
        lane = lax.broadcasted_iota(jnp.int32, (coarse, FINE), 1).astype(f32)
        hi, lo = split(jnp.concatenate([dt, dt * lane], axis=0))
        both = jnp.dot(jnp.concatenate([hi, lo], axis=0), qh_ref[c], preferred_element_type=f32)
        v = both[: 2 * coarse] + both[2 * coarse :]
        tiles = coarse_tiles(sq_ref, c)
        power = tuple(jnp.concatenate([t[part] for t in tiles], axis=0) for part in range(2))
        v0 = v[:coarse, :width], v[:coarse, width:]
        row = lax.broadcasted_iota(jnp.int32, (coarse, width), 0)
        far = (row % (coarse // 2)) * (2 * FINE) + (row // (coarse // 2)) * FINE
        far = far.astype(f32)
        v1 = tuple(far * v0[part] + v[coarse:, part * width : (part + 1) * width] for part in range(2))
        for n, pair in enumerate((v0, v1)):
            prod = cmul(power, pair)
            for part in range(2):
                s_ref[2 * n + part, pl.ds(c, 1), :] = jnp.sum(prod[part], axis=0, keepdims=True)

    over_channels(channel, 4)
    modulus = lam_re * lam_re + lam_im * lam_im
    inv = lam_re / modulus, -lam_im / modulus
    shift = one[0] - 1.0, one[1]
    ratio = cmul(shift, inv)
    w = w_ref[0], w_ref[1]
    s0 = s_ref[0], s_ref[1]
    s1 = s_ref[2], s_ref[3]
    coeff = cmul(w, ratio)
    gw = cmul(s0, ratio)
    gw_ref[0], gw_ref[1] = gw[0], -gw[1]
    near = cmul(s0, cmul(w, cmul(one, inv)))
    far = cmul(coeff, s1)
    z = near[0] + far[0], near[1] + far[1]
    back = cmul(s0, cmul(coeff, inv))
    big = delta * z[0] - back[0], delta * z[1] - back[1]
    step = jnp.sum((z[0] * lam_re - z[1] * lam_im) * delta, axis=1, keepdims=True)
    gstep_ref[...] = jnp.broadcast_to(step, gstep_ref.shape)

    @pl.when(pl.program_id(0) == 0)
    def _():
        glam_ref[...] = jnp.zeros(glam_ref.shape, f32)

    glam_ref[0] += big[0] * lam_re
    glam_ref[1] -= big[1]


def mode_grads(lam_log, lam_freq, weights, log_step, dt, fine):
    channels, modes = weights.shape[1:]
    rows = LAGS // TILE
    table = pl.BlockSpec((ROWS, FINE, 2 * modes), lambda i: (i, 0, 0))
    gw, gstep, glam = pl.pallas_call(
        mode_grad_kernel,
        grid=(channels // ROWS,),
        in_specs=[
            pl.BlockSpec((1, modes), lambda i: (0, 0)),
            pl.BlockSpec((1, modes), lambda i: (0, 0)),
            pl.BlockSpec((2, ROWS, modes), lambda i: (0, i, 0)),
            pl.BlockSpec((ROWS, 1), lambda i: (i, 0)),
            pl.BlockSpec((ROWS, rows, TILE), lambda i: (i, 0, 0)),
            table,
        ],
        out_specs=[
            pl.BlockSpec((2, ROWS, modes), lambda i: (0, i, 0)),
            pl.BlockSpec((ROWS, TILE), lambda i: (i, 0)),
            pl.BlockSpec((2, ROWS, modes), lambda i: (0, 0, 0)),
        ],
        out_shape=[
            jax.ShapeDtypeStruct((2, channels, modes), f32),
            jax.ShapeDtypeStruct((channels, TILE), f32),
            jax.ShapeDtypeStruct((2, ROWS, modes), f32),
        ],
        scratch_shapes=[
            pltpu.VMEM((2, 11, ROWS, modes), f32),
            pltpu.VMEM((4, ROWS, modes), f32),
        ],
        compiler_params=params(),
        cost_estimate=cost(2),
    )(lam_log[None], lam_freq[None], weights, log_step[:, None], dt.reshape(channels, rows, TILE), fine)
    return gw, gstep[:, 0], jnp.sum(glam, axis=1)


epsilon = 1e-05
contract_last = (((1,), (1,)), ((), ()))
contract_first = (((0,), (0,)), ((), ()))


def swap(x, k, n_grp):
    return x if k == 0 else lax.ppermute(x, "grp", [(i, i ^ k) for i in range(n_grp)])


def gather_small(x, n_seq):
    held = lax.dynamic_update_index_in_dim(jnp.zeros((n_seq, *x.shape), x.dtype), x, lax.axis_index("seq"), 0)
    for k in range(n_seq.bit_length() - 1):
        held = held + lax.ppermute(held, "seq", [(i, i ^ (1 << k)) for i in range(n_seq)])
    return held


def gelu_parts(v):
    t = jnp.tanh(0.7978845608028654 * (v + 0.044715 * (v * v * v)))
    half = 0.5 * (1.0 + t)
    return v * half, half + 0.5 * v * (1.0 - t * t) * 0.7978845608028654 * (1.0 + 0.134145 * (v * v))


def gather_grp(x, n_grp):
    return [swap(x, k, n_grp) for k in range(n_grp)]


def gather_two(a, b, n_grp):
    if n_grp != 4:
        return [jnp.concatenate(gather_grp(x, n_grp), axis=0) for x in (a, b)]
    rows = a.shape[0]
    a_near, b_near = swap(a, 1, n_grp), swap(b, 2, n_grp)
    a = jnp.concatenate([a, a_near], axis=0)
    b = jnp.concatenate([b, b_near], axis=0)
    a_far, b_far = swap(a, 2, n_grp), swap(b, 1, n_grp)
    return jnp.concatenate([a, a_far], axis=0), jnp.concatenate([b[:rows], b_far[:rows], b[rows:], b_far[rows:]], axis=0)


def sum_scatter_two(a, b, n_grp):
    a, b = (x.reshape(n_grp, -1, x.shape[1]) for x in (a, b))
    if n_grp != 4:
        return [sum_scatter_grp([x[k] for k in range(n_grp)], n_grp) for x in (a, b)]
    a = a.reshape(2, 2, *a.shape[1:])
    sent = a[:, 1].astype(bf16), b[2:].astype(bf16)
    a = a[:, 0].astype(f32) + swap(sent[0], 1, n_grp).astype(f32)
    b = b[:2].astype(f32) + swap(sent[1], 2, n_grp).astype(f32)
    sent = a[1].astype(bf16), b[1].astype(bf16)
    return a[0] + swap(sent[0], 2, n_grp).astype(f32), b[0] + swap(sent[1], 1, n_grp).astype(f32)


def sum_scatter_grp(pieces, n_grp):
    total = pieces[0].astype(f32)
    for k in range(1, n_grp):
        total = total + swap(pieces[k].astype(bf16), k, n_grp).astype(f32)
    return total


def tree_sum(terms):
    while len(terms) > 1:
        terms = [terms[i] + terms[i + 1] for i in range(0, len(terms), 2)]
    return terms[0]


def sum_grp(x, n_grp):
    return tree_sum([y.astype(f32) for y in gather_grp(x.astype(bf16), n_grp)])


def place_grp(x, n_grp, me, axis):
    held = jnp.stack(gather_grp(x, n_grp))
    rows = [lax.dynamic_index_in_dim(held, (me ^ j).astype(jnp.uint32), 0, keepdims=False) for j in range(n_grp)]
    return jnp.stack(rows, axis=axis)


def body(
    n_grp,
    n_seq,
    layer_input,
    segments,
    ln_gain,
    ln_bias,
    w_value,
    b_value,
    w_reduce,
    b_reduce,
    lam_log,
    lam_freq,
    dss_w,
    log_step,
    w_up,
    b_up,
    w_out,
    b_out,
    out_cotangent,
):
    me = lax.axis_index("grp")
    tokens, wide = layer_input.shape
    part = w_value.shape[0] // n_grp
    quarter = n_seq * part
    reduced_width = w_reduce.shape[0] * n_seq

    small = (ln_gain, ln_bias, b_value, b_reduce, lam_log, lam_freq, b_up, b_out, segments[0].astype(bf16))
    packed = jnp.concatenate([jnp.pad(v, (0, -v.shape[0] % 128)).reshape(-1, 128) for v in small], axis=0)
    packed = jnp.pad(packed, ((0, -packed.shape[0] % 16), (0, 0)))
    packed = gather_small(packed, n_seq)
    spots, fulls = 0, []
    for array in small:
        deep = -(-array.shape[0] // 128)
        fulls.append(packed[:, spots : spots + deep].reshape(n_seq, -1)[:, : array.shape[0]])
        spots += deep
    gain_full, bias_full, value_bias, reduce_bias, decay_full, freq_full, up_bias, out_bias, doc_row = fulls
    gain_wide = gain_full.reshape(-1).astype(f32)
    bias_wide = bias_full.reshape(-1).astype(f32)
    value_bias = lax.dynamic_slice_in_dim(value_bias, me * part, part, 1).reshape(-1).astype(f32)
    up_bias = lax.dynamic_slice_in_dim(up_bias, me * part, part, 1).reshape(-1).astype(f32)

    reduce_full = lax.all_gather(w_reduce, "seq", axis=0, tiled=True)
    pieces = [lax.dynamic_slice_in_dim(w, me * part, part, 0) for w in (w_value, w_up)]
    both_part = lax.all_gather(jnp.concatenate(pieces, axis=1), "seq", axis=0, tiled=True)
    value_part, up_part = both_part[:, :wide], both_part[:, wide:]
    out_cols = lax.dynamic_index_in_dim(w_out.reshape(-1, n_seq, n_grp, part), me, 2, keepdims=False)
    out_part = lax.all_gather(out_cols.reshape(-1, quarter), "seq", axis=0, tiled=True)

    length = tokens * n_seq
    blocks = length // TILE
    deep = lag_blocks(length)
    decay = decay_full.reshape(-1).astype(f32)
    freq = freq_full.reshape(-1).astype(f32)
    weights = dss_w.astype(f32)
    steps = log_step.astype(f32)
    half = steps.shape[0] // 2
    modes = [
        (decay, freq, weights[:, :half], steps[:half]),
        (decay, freq, weights[:, half:], steps[half:]),
    ]
    tables = [make_toeplitz(*modes[0], deep)]

    x_wide = layer_input.astype(f32)
    center = x_wide - jnp.mean(x_wide, axis=1, keepdims=True)
    inverse = lax.rsqrt(jnp.mean(center * center, axis=1, keepdims=True) + epsilon)
    unit = center * inverse
    normed = (unit * gain_wide + bias_wide).astype(bf16)

    pre_reduce = (
        lax.dot_general(reduce_full, normed, contract_last, preferred_element_type=f32)
        + reduce_bias.reshape(-1).astype(f32)[:, None]
    )
    reduced, reduce_slope = gelu_parts(pre_reduce)
    reduced = reduced.astype(bf16)
    reduced, later, cot_own, normed_own, last = lax.optimization_barrier(
        (reduced, modes[1][0], out_cotangent, normed, tables[0])
    )
    tables[0] = last
    tables.append(make_toeplitz(later, *modes[1][1:], deep))
    cot_all, normed_all = gather_two(cot_own, normed_own, n_grp)
    channel_in = lax.all_to_all(reduced, "seq", split_axis=0, concat_axis=1, tiled=True)
    seg = doc_row.astype(jnp.int32).reshape(blocks, TILE)
    signal = channel_in.reshape(-1, blocks, TILE)
    halves = [slice(0, half), slice(half, 2 * half)]
    convolve, sum_lags = (lone_conv, lone_taps) if lone(length) else (any_conv, taps_grad)
    channel_out = jnp.concatenate(
        [convolve(seg, signal[h], t[0], False) for h, t in zip(halves, tables)], axis=0
    ).reshape(-1, length)
    mixed = lax.all_to_all(channel_out, "seq", split_axis=1, concat_axis=0, tiled=True)
    mixed_all = jnp.concatenate(gather_grp(mixed, n_grp), axis=1)

    pre_value = lax.dot_general(normed_all, value_part, contract_last, preferred_element_type=f32) + value_bias
    activated, slope = lax.optimization_barrier(gelu_parts(pre_value))
    g_gated = jnp.dot(cot_all, out_part, preferred_element_type=f32)
    pre_up = lax.dot_general(mixed_all, up_part, (((0,), (1,)), ((), ())), preferred_element_type=f32) + up_bias
    gated = (activated * pre_up).astype(bf16)
    g_activated = g_gated * pre_up
    g_pre_up = (g_gated * activated).astype(bf16)
    g_pre_value = (g_activated * slope).astype(bf16)

    g_mixed = lax.dot_general(up_part, g_pre_up, (((0,), (1,)), ((), ())), preferred_element_type=f32)
    g_mixed = sum_scatter_grp([g_mixed[:, k * tokens : (k + 1) * tokens] for k in range(n_grp)], n_grp)
    added = lax.dot_general(gated, out_part, contract_last, preferred_element_type=f32)
    g_normed = jnp.dot(g_pre_value, value_part, preferred_element_type=f32)
    added, g_normed = added.astype(bf16), g_normed.astype(bf16)
    g_mixed, gated, g_pre_up, g_pre_value, added, g_normed = lax.optimization_barrier(
        (g_mixed.astype(bf16), gated, g_pre_up, g_pre_value, added, g_normed)
    )
    g_channel = lax.all_to_all(g_mixed, "seq", split_axis=0, concat_axis=1, tiled=True)
    g_channel = g_channel.reshape(-1, blocks, TILE)
    g_out = lax.dot_general(cot_all, gated, contract_first, preferred_element_type=f32).astype(bf16)
    g_up = lax.dot_general(g_pre_up, mixed_all, (((0,), (1,)), ((), ())), preferred_element_type=f32)
    g_value = lax.dot_general(g_pre_value, normed_all, contract_first, preferred_element_type=f32)
    left = (jnp.arange(TILE) < TILE // 2).astype(bf16)
    ones = [jnp.broadcast_to(m, (g_pre_value.shape[0], TILE)) for m in (left, 1 - left)]
    g_biases = lax.dot_general(g_pre_value, ones[0], contract_first, preferred_element_type=f32)
    g_biases += lax.dot_general(g_pre_up, ones[1], contract_first, preferred_element_type=f32)
    g_both = jnp.concatenate([y.astype(bf16) for y in (g_value, g_up, g_biases)], axis=1)
    g_channel, g_out, g_both, added, g_normed = lax.optimization_barrier(
        (g_channel, g_out, g_both, added, g_normed)
    )
    g_out = lax.psum_scatter(g_out, "seq", scatter_dimension=0, tiled=True)
    g_both = lax.psum_scatter(g_both, "seq", scatter_dimension=0, tiled=True)
    g_signal = jnp.concatenate([convolve(seg, g_channel[h], t[0], True) for h, t in zip(halves, tables)], axis=0)
    g_signal, g_channel = lax.optimization_barrier((g_signal, g_channel))
    g_reduced = lax.all_to_all(g_signal.reshape(-1, length), "seq", split_axis=1, concat_axis=0, tiled=True)
    g_taps = sum_lags(seg, signal, g_channel)
    g_taps, g_reduced = lax.optimization_barrier((g_taps, g_reduced))
    found = [mode_grads(*m, g_taps[h], *t[1:]) for h, m, t in zip(halves, modes, tables)]
    g_lam = found[0][2] + found[1][2]
    states = g_lam.shape[1]
    added, g_normed = sum_scatter_two(added, g_normed, n_grp)
    output = (x_wide + added + out_bias.reshape(-1).astype(f32)).astype(bf16)

    g_pre_reduce = (g_reduced.astype(f32) * reduce_slope).astype(bf16)
    g_reduce = jnp.dot(g_pre_reduce, normed, preferred_element_type=f32)
    g_normed = g_normed + lax.dot_general(g_pre_reduce, reduce_full, contract_first, preferred_element_type=f32)
    g_unit = g_normed * gain_wide
    g_input = inverse * (
        g_unit
        - jnp.mean(g_unit, axis=1, keepdims=True)
        - unit * jnp.mean(g_unit * unit, axis=1, keepdims=True)
    ) + out_cotangent.astype(f32)

    vectors = (
        jnp.sum(g_normed * unit, axis=0).reshape(n_seq, -1),
        jnp.sum(g_normed, axis=0).reshape(n_seq, -1),
        jnp.sum(g_pre_reduce.astype(f32), axis=1).reshape(n_seq, -1),
        g_lam[0].reshape(n_seq, -1),
        g_lam[1].reshape(n_seq, -1),
        jnp.sum(out_cotangent.astype(f32), axis=0).reshape(n_seq, -1),
    )
    flat = jnp.concatenate(vectors, axis=1)
    flat = jnp.pad(flat, ((0, 0), (0, -flat.shape[1] % wide))).reshape(n_seq, -1, wide)
    own = jnp.concatenate([g_reduce.reshape(n_seq, -1, wide).astype(bf16), flat.astype(bf16)], axis=1)
    own, g_out, g_both = lax.optimization_barrier((own, g_out, g_both))
    own = lax.psum_scatter(own, "seq", scatter_dimension=0, tiled=False)
    packed = [f[0][i].reshape(-1) for i in range(2) for f in found] + [f[1] for f in found]
    packed.append(jnp.zeros((-2 * half % wide,), f32))
    packed = jnp.concatenate(packed).reshape(-1, wide).astype(bf16)
    packed = sum_grp(packed, n_grp)
    own = sum_grp(own, n_grp)
    g_reduce, shard = own[: w_reduce.shape[0]], own[w_reduce.shape[0] :].reshape(-1)
    g_weights = packed[:-1].reshape(2, -1, states)
    g_step = packed[-1][: 2 * half]
    placed = place_grp(g_out, n_grp, me, 0)
    g_out = placed.reshape(n_grp, -1, n_seq, part).transpose(1, 2, 0, 3).reshape(w_out.shape).astype(f32)
    placed = place_grp(g_both, n_grp, me, 0).reshape(w_value.shape[0], -1).astype(f32)
    g_value, g_up = placed[:, :wide], placed[:, wide : wide + w_up.shape[1]]
    g_value_bias, g_up_bias = placed[:, wide + w_up.shape[1]], placed[:, -1]
    sums, spots = [], 0
    for array in vectors:
        sums.append(shard[spots : spots + array.shape[1]])
        spots += array.shape[1]
    g_gain, g_bias, g_reduce_bias, g_decay, g_freq, g_out_bias = sums
    return (
        output,
        g_input,
        g_gain,
        g_bias,
        g_value,
        g_value_bias,
        g_reduce,
        g_reduce_bias,
        g_decay,
        g_freq,
        g_weights,
        g_step,
        g_up,
        g_up_bias,
        g_out,
        g_out_bias,
    )


def solution(mesh):
    by_token = P(("grp", "seq"), None)
    row, matrix, cube = P("seq"), P("seq", None), P(None, "seq", None)
    layer = (row, row, matrix, row, matrix, row, row, row, cube, row, matrix, row, matrix, row)
    return jax.shard_map(
        functools.partial(body, mesh.shape["grp"], mesh.shape["seq"]),
        mesh=mesh,
        in_specs=(by_token, P("grp", "seq"), *layer, by_token),
        out_specs=(by_token, by_token, *layer),
        check_vma=False,
    )
```

```python
import functools

import jax
import jax.numpy as jnp
from jax import lax
from jax.experimental import pallas as pl
from jax.experimental.pallas import tpu as pltpu
from jax.sharding import PartitionSpec as P

f32, bf16 = jnp.float32, jnp.bfloat16
TILE = 128
MOST = 2000
LAGS = 2048
FINE = 64
EXTRA = 16
PART = 64
ROWS = 8
NT = (((1,), (1,)), ((), ()))
TN = (((0,), (0,)), ((), ()))


def params(mb=48):
    return pltpu.CompilerParams(vmem_limit_bytes=mb << 20)


def cost(us):
    return pl.CostEstimate(flops=us * 10**9, bytes_accessed=us * 10**6, transcendentals=0)


def lag_blocks(length):
    return min(length // TILE, (MOST + TILE - 2) // TILE + 1)


def doc_count(length):
    return length // 1024 + 1


def over_channels(step, unroll):
    def some(i, _):
        for u in range(unroll):
            step(i * unroll + u, u)
        return 0

    lax.fori_loop(0, ROWS // unroll, some, 0)


def cmul(a, b):
    return (a[0] * b[0] - a[1] * b[1], a[0] * b[1] + a[1] * b[0])


def mode_rates(lam_log_ref, lam_freq_ref, step_ref):
    lam_re = -jnp.exp(lam_log_ref[...])
    lam_im = lam_freq_ref[...]
    delta = jnp.exp(step_ref[...])
    return lam_re, lam_im, delta


def first_power(lam_re, lam_im, delta):
    growth = jnp.exp(delta * lam_re)
    phase = delta * lam_im
    return growth * jnp.cos(phase), growth * jnp.sin(phase)


def store_squares(one, sq_ref):
    cur = one
    for k in range(11):
        sq_ref[0, k], sq_ref[1, k] = cur
        if k < 10:
            cur = cmul(cur, cur)


def power_tiles(sq_ref, c, first, count):
    def sq(k):
        return sq_ref[0, k, pl.ds(c, 1), :], sq_ref[1, k, pl.ds(c, 1), :]

    width = sq_ref.shape[-1]
    row = lax.broadcasted_iota(jnp.int32, (8, width), 0)
    tile = None
    for k in range(3):
        re, im = sq(first + k)
        on = (row & (1 << k)) != 0
        term = jnp.where(on, re, 1.0), jnp.where(on, im, 0.0)
        tile = term if tile is None else cmul(tile, term)
    tiles, k = [tile], 3
    while len(tiles) < count:
        step = sq(first + k)
        tiles = tiles + [cmul(t, step) for t in tiles]
        k += 1
    return tiles


def split(x):
    hi = x.astype(bf16)
    return hi, (x - hi.astype(f32)).astype(bf16)


def coarse_tiles(sq_ref, c):
    even = power_tiles(sq_ref, c, 7, LAGS // TILE // 8)
    half = sq_ref[0, 6, pl.ds(c, 1), :], sq_ref[1, 6, pl.ds(c, 1), :]
    return even + [cmul(t, half) for t in even]


def taps_kernel(
    lam_log_ref, lam_freq_ref, w_ref, step_ref, tt_ref, qh_ref, sq_ref, cf_ref, p_ref, ql_ref
):
    lam_re, lam_im, delta = mode_rates(lam_log_ref, lam_freq_ref, step_ref)
    one = first_power(lam_re, lam_im, delta)
    store_squares(one, sq_ref)
    modulus = lam_re * lam_re + lam_im * lam_im
    shift_re, shift_im = one[0] - 1.0, one[1]
    ratio = (
        (shift_re * lam_re + shift_im * lam_im) / modulus,
        (shift_im * lam_re - shift_re * lam_im) / modulus,
    )
    cf_ref[0], cf_ref[1] = cmul((w_ref[0], w_ref[1]), ratio)
    width = sq_ref.shape[-1]
    deep = tt_ref.shape[2] // TILE
    coarse = LAGS // FINE

    def channel(c, u):
        for t, pair in enumerate(power_tiles(sq_ref, c, 0, FINE // 8)):
            if t % 2 == 0:
                held = pair
                continue
            for part in range(2):
                hi, lo = split(jnp.concatenate([held[part], pair[part]], axis=0))
                qh_ref[c, 8 * t - 8 : 8 * t + 8, part * width : (part + 1) * width] = hi
                ql_ref[u, 8 * t - 8 : 8 * t + 8, part * width : (part + 1) * width] = lo
        coeff = cf_ref[0, pl.ds(c, 1), :], cf_ref[1, pl.ds(c, 1), :]
        tiles = [cmul(t, coeff) for t in coarse_tiles(sq_ref, c)]
        for part, sign in ((0, 1.0), (1, -1.0)):
            hi, lo = split(sign * jnp.concatenate([t[part] for t in tiles], axis=0))
            p_ref[u, :coarse, part * width : (part + 1) * width] = hi
            p_ref[u, coarse:, part * width : (part + 1) * width] = lo
        both = lax.dot_general(qh_ref[c], p_ref[u], NT, preferred_element_type=f32)
        low = lax.dot_general(ql_ref[u], p_ref[u, :coarse], NT, preferred_element_type=f32)
        taps = (both[:, :coarse] + both[:, coarse:] + low).T
        taps = jnp.concatenate([taps[: coarse // 2], taps[coarse // 2 :]], axis=1)
        rows = [jnp.broadcast_to(taps[d : d + 1], (8, TILE)) for d in range(min(deep, LAGS // TILE))]
        gap = jnp.zeros((8, TILE), f32)
        source = jnp.concatenate([gap] + rows + [gap] * (deep - len(rows)), axis=1)
        for r in range(PART // 16):
            pair = [pltpu.roll(source, 16 * r + s, 1, stride=1, stride_axis=0)[:, TILE:] for s in (0, 8)]
            tt_ref[c, 16 * r : 16 * r + 16, :] = jnp.concatenate(pair, axis=0).astype(bf16)

    over_channels(channel, p_ref.shape[0])


def make_toeplitz(lam_log, lam_freq, weights, log_step, deep):
    channels, modes = weights.shape[1:]
    table = pl.BlockSpec((ROWS, FINE, 2 * modes), lambda i: (i, 0, 0))
    return pl.pallas_call(
        taps_kernel,
        grid=(channels // ROWS,),
        in_specs=[
            pl.BlockSpec((1, modes), lambda i: (0, 0)),
            pl.BlockSpec((1, modes), lambda i: (0, 0)),
            pl.BlockSpec((2, ROWS, modes), lambda i: (0, i, 0)),
            pl.BlockSpec((ROWS, 1), lambda i: (i, 0)),
        ],
        out_specs=[pl.BlockSpec((ROWS, PART, deep * TILE), lambda i: (i, 0, 0)), table],
        out_shape=[
            jax.ShapeDtypeStruct((channels, PART, deep * TILE), bf16),
            jax.ShapeDtypeStruct((channels, FINE, 2 * modes), bf16),
        ],
        scratch_shapes=[
            pltpu.VMEM((2, 11, ROWS, modes), f32),
            pltpu.VMEM((2, ROWS, modes), f32),
            pltpu.VMEM((4, 2 * LAGS // FINE, 2 * modes), bf16),
            pltpu.VMEM((4, FINE, 2 * modes), bf16),
        ],
        compiler_params=params(57),
        cost_estimate=cost(3),
    )(lam_log[None], lam_freq[None], weights, log_step[:, None])


def doc_windows(z, seg, docs, zs_ref, zw_ref, u, deep):
    blocks = z.shape[0]
    lane = lax.broadcasted_iota(jnp.int32, z.shape, 1)
    for k in range(docs):
        own = jnp.where(seg == k, z, 0.0)
        after = jnp.concatenate([own[1:], jnp.zeros((1, TILE), f32)], axis=0)
        zs_ref[u, 2 * k, :blocks, :] = own
        zs_ref[u, 2 * k + 1, :blocks, :] = pltpu.roll(jnp.where(lane < PART, after, own), TILE - PART, 1)
    for k in range(2 * docs):
        for d in range(deep):
            zw_ref[u, k * blocks : (k + 1) * blocks, d * TILE : (d + 1) * TILE] = zs_ref[
                u, k, d : d + blocks, :
            ].astype(bf16)


def conv_kernel(docs, back, seg_ref, rows_ref, lanes_ref, x_ref, tt_ref, y_ref, zs_ref, zw_ref, xr_ref):
    blocks, deep = x_ref.shape[1], tt_ref.shape[2] // TILE
    zs_ref[...] = jnp.zeros(zs_ref.shape, f32)
    seg = seg_ref[...].astype(f32)
    if not back:
        rows, lanes = rows_ref[...], lanes_ref[...]
        seg = turn(seg.astype(bf16), rows[:blocks, :blocks], lanes)
        xr_ref[...] = turn(x_ref[...].reshape(ROWS * blocks, TILE), rows, lanes).reshape(xr_ref.shape)

    def channel(c, u):
        z = x_ref[c].astype(f32) if back else xr_ref[c]
        doc_windows(z, seg, docs, zs_ref, zw_ref, u, deep)
        y = lax.dot_general(zw_ref[u], tt_ref[c], NT, preferred_element_type=f32)
        out = jnp.zeros((blocks, TILE), f32)
        for k in range(docs):
            at = 2 * k * blocks
            mine = jnp.concatenate([y[at : at + blocks], y[at + blocks : at + 2 * blocks]], axis=1)
            out = jnp.where(seg == k, mine, out)
        if back:
            y_ref[c] = out.astype(bf16)
        else:
            xr_ref[c] = out

    over_channels(channel, zw_ref.shape[0])
    if not back:
        y = turn(xr_ref[...].astype(bf16).reshape(ROWS * blocks, TILE), rows, lanes)
        y_ref[...] = y.astype(bf16).reshape(y_ref.shape)


def any_conv(seg, x, tt, back, unroll=2):
    channels, blocks, _ = x.shape
    deep = tt.shape[2] // TILE
    docs = doc_count(blocks * TILE)
    rows, lanes = reverse_maps(blocks)
    cut = pl.BlockSpec((ROWS, blocks, TILE), lambda i: (i, 0, 0))
    return pl.pallas_call(
        functools.partial(conv_kernel, docs, back),
        grid=(channels // ROWS,),
        in_specs=[
            whole(seg),
            whole(rows),
            whole(lanes),
            cut,
            pl.BlockSpec((ROWS, PART, deep * TILE), lambda i: (i, 0, 0)),
        ],
        out_specs=cut,
        out_shape=jax.ShapeDtypeStruct(x.shape, bf16),
        scratch_shapes=[
            pltpu.VMEM((unroll, 2 * docs, blocks + deep - 1, TILE), f32),
            pltpu.VMEM((unroll, 2 * docs * blocks, deep * TILE), bf16),
            pltpu.VMEM((ROWS, blocks, TILE), f32),
        ],
        compiler_params=params(),
        cost_estimate=cost(3),
    )(seg, rows, lanes, x, tt)


def taps_grad_kernel(docs, seg_ref, flip_ref, x_ref, g_ref, dt_ref, gs_ref, gw_ref, xst_ref, wide_ref):
    wide_ref[...] = jnp.zeros(wide_ref.shape, f32)
    blocks = x_ref.shape[1]
    deep = gw_ref.shape[2] // TILE
    lead = deep - 1
    cuts = TILE // PART
    seg = seg_ref[...]
    lane = lax.broadcasted_iota(jnp.int32, (blocks, TILE), 1)
    for u in range(gs_ref.shape[0]):
        for k in range(docs * cuts):
            gs_ref[u, k, blocks:, :] = jnp.zeros((lead, TILE), f32)

    def one(c, u):
        g = g_ref[c].astype(f32)
        x = x_ref[c].astype(f32)
        for k in range(docs):
            own = jnp.where(seg == k, g, 0.0)
            gs_ref[u, k * cuts, :blocks, :] = own
            after = jnp.concatenate([own[1:], jnp.zeros((1, TILE), f32)], axis=0)
            for p in range(1, cuts):
                gs_ref[u, k * cuts + p, :blocks, :] = pltpu.roll(
                    jnp.where(lane < p * PART, after, own), TILE - p * PART, 1
                )
            mine = jnp.where(seg == k, x, 0.0).astype(bf16)
            mine = jnp.dot(mine, flip_ref[...], preferred_element_type=f32).astype(bf16)
            for p in range(cuts):
                at = (k * cuts + p) * blocks
                xst_ref[u, at : at + blocks, :] = mine[:, p * PART : (p + 1) * PART]
        for k in range(docs * cuts):
            for d in range(deep):
                gw_ref[u, k * blocks : (k + 1) * blocks, d * TILE : (d + 1) * TILE] = gs_ref[
                    u, k, d : d + blocks, :
                ].astype(bf16)
        wide_ref[u, :, : deep * TILE] = lax.dot_general(xst_ref[u], gw_ref[u], TN, preferred_element_type=f32)
        total = jnp.zeros((8, LAGS), f32)
        for r in range(0, PART, 8):
            rows = wide_ref[u, r : r + 8, :]
            total += pltpu.roll(rows, rows.shape[1] - (PART - 1) + r, 1, stride=1, stride_axis=0)[:, :LAGS]
        dt_ref[pl.ds(c, 1), :] = jnp.sum(total, axis=0, keepdims=True)

    def pair(i, _):
        for u in range(gs_ref.shape[0]):
            one(i * gs_ref.shape[0] + u, u)
        return 0

    lax.fori_loop(0, ROWS // gs_ref.shape[0], pair, 0)


def taps_grad(seg, x, g, unroll=4):
    channels, blocks, _ = x.shape
    deep = lag_blocks(blocks * TILE)
    docs = doc_count(blocks * TILE)
    cuts = TILE // PART
    place = jnp.arange(TILE)
    flip = (place[:, None] == (place // PART * PART + PART - 1 - place % PART)[None, :]).astype(bf16)
    rows = pl.BlockSpec((ROWS, blocks, TILE), lambda i: (i, 0, 0))
    return pl.pallas_call(
        functools.partial(taps_grad_kernel, docs),
        grid=(channels // ROWS,),
        in_specs=[
            pl.BlockSpec((blocks, TILE), lambda i: (0, 0)),
            pl.BlockSpec((TILE, TILE), lambda i: (0, 0)),
            rows,
            rows,
        ],
        out_specs=pl.BlockSpec((ROWS, LAGS), lambda i: (i, 0)),
        out_shape=jax.ShapeDtypeStruct((channels, LAGS), f32),
        scratch_shapes=[
            pltpu.VMEM((unroll, docs * cuts, blocks + deep - 1, TILE), f32),
            pltpu.VMEM((unroll, docs * cuts * blocks, deep * TILE), bf16),
            pltpu.VMEM((unroll, docs * cuts * blocks, PART), bf16),
            pltpu.VMEM((unroll, PART, (deep + 1) * TILE), f32),
        ],
        compiler_params=params(),
        cost_estimate=cost(4),
    )(seg, flip, x, g)


def lone(length):
    return MOST < length <= MOST + PART and 2 * doc_count(length) <= EXTRA


def lone_masks(seg, docs):
    blocks = seg.shape[0]
    long = jnp.zeros(seg.shape, f32)
    row = lax.broadcasted_iota(jnp.int32, (EXTRA, PART), 0)
    ends = jnp.where(row % 2 == 0, seg[:1, :PART], seg[blocks - 1 :, TILE - PART :])
    extra = jnp.zeros((EXTRA, PART), f32)
    for k in range(docs):
        here = (seg == k).astype(f32)
        count = jnp.sum(jnp.sum(here, axis=0, keepdims=True), axis=1, keepdims=True)
        long += jnp.where(count >= MOST, here, 0.0)
        extra += jnp.where((row // 2 == k) & (ends == k) & (count[:, :1] < MOST), 1.0, 0.0)
    return long, extra


def end_rows(z, extra):
    even = lax.broadcasted_iota(jnp.int32, extra.shape, 0) % 2 == 0
    return jnp.where(even, z[:1, :PART], z[z.shape[0] - 1 :, TILE - PART :]) * extra


def store_windows(z, long, extra, zs_ref, zw_ref, u, deep):
    blocks = z.shape[0]
    own = z * long
    after = jnp.concatenate([own[1:], jnp.zeros((1, TILE), f32)], axis=0)
    lane = lax.broadcasted_iota(jnp.int32, own.shape, 1)
    zs_ref[u, 0, :blocks, :] = own
    zs_ref[u, 1, :blocks, :] = pltpu.roll(jnp.where(lane < PART, after, own), TILE - PART, 1)
    for p in range(2):
        for d in range(deep):
            zw_ref[u, p * blocks : (p + 1) * blocks, d * TILE : (d + 1) * TILE] = zs_ref[
                u, p, d : d + blocks, :
            ].astype(bf16)
    ends = end_rows(z, extra)
    zw_ref[u, 2 * blocks :, :TILE] = jnp.concatenate([ends, jnp.zeros_like(ends)], axis=1).astype(bf16)


def turn(x, rows, lanes):
    x = jnp.dot(rows, x, preferred_element_type=f32).astype(bf16)
    return jnp.dot(x, lanes, preferred_element_type=f32)


def lone_conv_kernel(docs, back, seg_ref, rows_ref, lanes_ref, x_ref, tt_ref, y_ref, zs_ref, zw_ref, xr_ref):
    blocks, deep = x_ref.shape[1], tt_ref.shape[2] // TILE
    zw_ref[...] = jnp.zeros(zw_ref.shape, bf16)
    zs_ref[...] = jnp.zeros(zs_ref.shape, f32)
    seg = seg_ref[...].astype(f32)
    if not back:
        rows, lanes = rows_ref[...], lanes_ref[...]
        seg = turn(seg.astype(bf16), rows[:blocks, :blocks], lanes)
        xr_ref[...] = turn(x_ref[...].reshape(ROWS * blocks, TILE), rows, lanes).reshape(xr_ref.shape)
    long, extra = lone_masks(seg, docs)
    even = lax.broadcasted_iota(jnp.int32, extra.shape, 0) % 2 == 0
    place = lax.broadcasted_iota(jnp.int32, (blocks, PART), 0)

    def channel(c, u):
        z = x_ref[c].astype(f32) if back else xr_ref[c]
        store_windows(z, long, extra, zs_ref, zw_ref, u, deep)
        y = lax.dot_general(zw_ref[u], tt_ref[c], NT, preferred_element_type=f32)
        ends = y[2 * blocks :] * extra
        first = jnp.sum(jnp.where(even, ends, 0.0), axis=0, keepdims=True)
        last = jnp.sum(jnp.where(even, 0.0, ends), axis=0, keepdims=True)
        ends = jnp.concatenate([jnp.where(place == 0, first, 0.0), jnp.where(place == blocks - 1, last, 0.0)], axis=1)
        y = jnp.concatenate([y[:blocks], y[blocks : 2 * blocks]], axis=1) * long + ends
        if back:
            y_ref[c] = y.astype(bf16)
        else:
            xr_ref[c] = y

    over_channels(channel, zw_ref.shape[0])
    if not back:
        y = turn(xr_ref[...].astype(bf16).reshape(ROWS * blocks, TILE), rows, lanes)
        y_ref[...] = y.astype(bf16).reshape(y_ref.shape)


def reverse_maps(blocks):
    row = jnp.arange(ROWS * blocks)
    lane = jnp.arange(TILE)
    rows = row[:, None] == (row // blocks * blocks + blocks - 1 - row % blocks)[None, :]
    return rows.astype(bf16), (lane[:, None] == TILE - 1 - lane[None, :]).astype(bf16)


def whole(a):
    return pl.BlockSpec(a.shape, lambda i: (0,) * a.ndim)


def lone_conv(seg, x, tt, back, unroll=4):
    channels, blocks, _ = x.shape
    deep = tt.shape[2] // TILE
    rows, lanes = reverse_maps(blocks)
    cut = pl.BlockSpec((ROWS, blocks, TILE), lambda i: (i, 0, 0))
    return pl.pallas_call(
        functools.partial(lone_conv_kernel, doc_count(blocks * TILE), back),
        grid=(channels // ROWS,),
        in_specs=[
            whole(seg),
            whole(rows),
            whole(lanes),
            cut,
            pl.BlockSpec((ROWS, PART, deep * TILE), lambda i: (i, 0, 0)),
        ],
        out_specs=cut,
        out_shape=jax.ShapeDtypeStruct(x.shape, bf16),
        scratch_shapes=[
            pltpu.VMEM((unroll, 2, blocks + deep - 1, TILE), f32),
            pltpu.VMEM((unroll, 2 * blocks + EXTRA, deep * TILE), bf16),
            pltpu.VMEM((ROWS, blocks, TILE), f32),
        ],
        compiler_params=params(),
        cost_estimate=cost(3),
    )(seg, rows, lanes, x, tt)


def lone_taps_kernel(docs, seg_ref, lanes_ref, x_ref, g_ref, dt_ref, zs_ref, zw_ref, xs_ref, xr_ref):
    blocks = x_ref.shape[1]
    deep = zw_ref.shape[2] // TILE
    zw_ref[...] = jnp.zeros(zw_ref.shape, bf16)
    zs_ref[...] = jnp.zeros(zs_ref.shape, f32)
    lanes = lanes_ref[...]
    seg = seg_ref[...].astype(f32)
    long, extra = lone_masks(seg, docs)
    turned_long, turned_extra = lone_masks(jnp.dot(seg.astype(bf16), lanes, preferred_element_type=f32), docs)
    flat = x_ref[...].reshape(ROWS * blocks, TILE)
    xr_ref[...] = jnp.dot(flat, lanes, preferred_element_type=f32).reshape(xr_ref.shape)

    def channel(c, u):
        store_windows(g_ref[c].astype(f32), long, extra, zs_ref, zw_ref, u, deep)
        x = xr_ref[c]
        own = (x * turned_long).astype(bf16)
        for p in range(2):
            xs_ref[u, p * blocks : (p + 1) * blocks, :] = own[:, p * PART : (p + 1) * PART]
        xs_ref[u, 2 * blocks :, :] = end_rows(x, turned_extra).astype(bf16)
        wide = lax.dot_general(xs_ref[u], zw_ref[u], TN, preferred_element_type=f32)
        wide = jnp.concatenate([wide, jnp.zeros((PART, TILE), f32)], axis=1)
        total = jnp.zeros((8, LAGS), f32)
        for r in range(0, PART, 8):
            total += pltpu.roll(
                wide[r : r + 8], wide.shape[1] - (PART - 1) + r, 1, stride=1, stride_axis=0
            )[:, :LAGS]
        dt_ref[pl.ds(c, 1), :] = jnp.sum(total, axis=0, keepdims=True)

    over_channels(channel, zw_ref.shape[0])


def lone_taps(seg, x, g, unroll=4):
    channels, blocks, _ = x.shape
    deep = lag_blocks(blocks * TILE)
    place = jnp.arange(TILE)
    lanes = (place[:, None] == (place // PART * PART + PART - 1 - place % PART)[None, :]).astype(bf16)
    cut = pl.BlockSpec((ROWS, blocks, TILE), lambda i: (i, 0, 0))
    return pl.pallas_call(
        functools.partial(lone_taps_kernel, doc_count(blocks * TILE)),
        grid=(channels // ROWS,),
        in_specs=[whole(seg), whole(lanes), cut, cut],
        out_specs=pl.BlockSpec((ROWS, LAGS), lambda i: (i, 0)),
        out_shape=jax.ShapeDtypeStruct((channels, LAGS), f32),
        scratch_shapes=[
            pltpu.VMEM((unroll, 2, blocks + deep - 1, TILE), f32),
            pltpu.VMEM((unroll, 2 * blocks + EXTRA, deep * TILE), bf16),
            pltpu.VMEM((unroll, 2 * blocks + EXTRA, PART), bf16),
            pltpu.VMEM((ROWS, blocks, TILE), f32),
        ],
        compiler_params=params(),
        cost_estimate=cost(4),
    )(seg, lanes, x, g)


def mode_grad_kernel(
    lam_log_ref, lam_freq_ref, w_ref, step_ref, dt_ref, qh_ref, gw_ref, gstep_ref, glam_ref, sq_ref, s_ref
):
    lam_re, lam_im, delta = mode_rates(lam_log_ref, lam_freq_ref, step_ref)
    one = first_power(lam_re, lam_im, delta)
    store_squares(one, sq_ref)
    width = sq_ref.shape[-1]
    coarse = LAGS // FINE

    def channel(c, u):
        dt = dt_ref[c]
        dt = jnp.concatenate([dt[:, :FINE], dt[:, FINE:]], axis=0)
        lane = lax.broadcasted_iota(jnp.int32, (coarse, FINE), 1).astype(f32)
        hi, lo = split(jnp.concatenate([dt, dt * lane], axis=0))
        both = jnp.dot(jnp.concatenate([hi, lo], axis=0), qh_ref[c], preferred_element_type=f32)
        v = both[: 2 * coarse] + both[2 * coarse :]
        tiles = coarse_tiles(sq_ref, c)
        power = tuple(jnp.concatenate([t[part] for t in tiles], axis=0) for part in range(2))
        v0 = v[:coarse, :width], v[:coarse, width:]
        row = lax.broadcasted_iota(jnp.int32, (coarse, width), 0)
        far = (row % (coarse // 2)) * (2 * FINE) + (row // (coarse // 2)) * FINE
        far = far.astype(f32)
        v1 = tuple(far * v0[part] + v[coarse:, part * width : (part + 1) * width] for part in range(2))
        for n, pair in enumerate((v0, v1)):
            prod = cmul(power, pair)
            for part in range(2):
                s_ref[2 * n + part, pl.ds(c, 1), :] = jnp.sum(prod[part], axis=0, keepdims=True)

    over_channels(channel, 4)
    modulus = lam_re * lam_re + lam_im * lam_im
    inv = lam_re / modulus, -lam_im / modulus
    shift = one[0] - 1.0, one[1]
    ratio = cmul(shift, inv)
    w = w_ref[0], w_ref[1]
    s0 = s_ref[0], s_ref[1]
    s1 = s_ref[2], s_ref[3]
    coeff = cmul(w, ratio)
    gw = cmul(s0, ratio)
    gw_ref[0], gw_ref[1] = gw[0], -gw[1]
    near = cmul(s0, cmul(w, cmul(one, inv)))
    far = cmul(coeff, s1)
    z = near[0] + far[0], near[1] + far[1]
    back = cmul(s0, cmul(coeff, inv))
    big = delta * z[0] - back[0], delta * z[1] - back[1]
    step = jnp.sum((z[0] * lam_re - z[1] * lam_im) * delta, axis=1, keepdims=True)
    gstep_ref[...] = jnp.broadcast_to(step, gstep_ref.shape)

    @pl.when(pl.program_id(0) == 0)
    def _():
        glam_ref[...] = jnp.zeros(glam_ref.shape, f32)

    glam_ref[0] += big[0] * lam_re
    glam_ref[1] -= big[1]


def mode_grads(lam_log, lam_freq, weights, log_step, dt, fine):
    channels, modes = weights.shape[1:]
    rows = LAGS // TILE
    table = pl.BlockSpec((ROWS, FINE, 2 * modes), lambda i: (i, 0, 0))
    gw, gstep, glam = pl.pallas_call(
        mode_grad_kernel,
        grid=(channels // ROWS,),
        in_specs=[
            pl.BlockSpec((1, modes), lambda i: (0, 0)),
            pl.BlockSpec((1, modes), lambda i: (0, 0)),
            pl.BlockSpec((2, ROWS, modes), lambda i: (0, i, 0)),
            pl.BlockSpec((ROWS, 1), lambda i: (i, 0)),
            pl.BlockSpec((ROWS, rows, TILE), lambda i: (i, 0, 0)),
            table,
        ],
        out_specs=[
            pl.BlockSpec((2, ROWS, modes), lambda i: (0, i, 0)),
            pl.BlockSpec((ROWS, TILE), lambda i: (i, 0)),
            pl.BlockSpec((2, ROWS, modes), lambda i: (0, 0, 0)),
        ],
        out_shape=[
            jax.ShapeDtypeStruct((2, channels, modes), f32),
            jax.ShapeDtypeStruct((channels, TILE), f32),
            jax.ShapeDtypeStruct((2, ROWS, modes), f32),
        ],
        scratch_shapes=[
            pltpu.VMEM((2, 11, ROWS, modes), f32),
            pltpu.VMEM((4, ROWS, modes), f32),
        ],
        compiler_params=params(),
        cost_estimate=cost(2),
    )(lam_log[None], lam_freq[None], weights, log_step[:, None], dt.reshape(channels, rows, TILE), fine)
    return gw, gstep[:, 0], jnp.sum(glam, axis=1)


epsilon = 1e-05
contract_last = (((1,), (1,)), ((), ()))
contract_first = (((0,), (0,)), ((), ()))


def swap(x, k, n_grp):
    return x if k == 0 else lax.ppermute(x, "grp", [(i, i ^ k) for i in range(n_grp)])


def gather_small(x, n_seq):
    held = lax.dynamic_update_index_in_dim(jnp.zeros((n_seq, *x.shape), x.dtype), x, lax.axis_index("seq"), 0)
    for k in range(n_seq.bit_length() - 1):
        held = held + lax.ppermute(held, "seq", [(i, i ^ (1 << k)) for i in range(n_seq)])
    return held


def gelu_parts(v):
    t = jnp.tanh(0.7978845608028654 * (v + 0.044715 * (v * v * v)))
    half = 0.5 * (1.0 + t)
    return v * half, half + 0.5 * v * (1.0 - t * t) * 0.7978845608028654 * (1.0 + 0.134145 * (v * v))


def gather_grp(x, n_grp):
    return [swap(x, k, n_grp) for k in range(n_grp)]


def gather_two(a, b, n_grp):
    if n_grp != 4:
        return [jnp.concatenate(gather_grp(x, n_grp), axis=0) for x in (a, b)]
    rows = a.shape[0]
    a_near, b_near = swap(a, 1, n_grp), swap(b, 2, n_grp)
    a = jnp.concatenate([a, a_near], axis=0)
    b = jnp.concatenate([b, b_near], axis=0)
    a_far, b_far = swap(a, 2, n_grp), swap(b, 1, n_grp)
    return jnp.concatenate([a, a_far], axis=0), jnp.concatenate([b[:rows], b_far[:rows], b[rows:], b_far[rows:]], axis=0)


def sum_scatter_first(a, b, n_grp):
    a, b = (x.reshape(n_grp, -1, x.shape[1]) for x in (a, b))
    if n_grp != 4:
        return a, b
    a = a.reshape(2, 2, *a.shape[1:])
    sent = a[:, 1].astype(bf16), b[2:].astype(bf16)
    a = a[:, 0].astype(f32) + swap(sent[0], 1, n_grp).astype(f32)
    return a, b[:2].astype(f32) + swap(sent[1], 2, n_grp).astype(f32)


def sum_scatter_second(a, b, n_grp):
    if n_grp != 4:
        return [sum_scatter_grp([x[k] for k in range(n_grp)], n_grp) for x in (a, b)]
    sent = a[1].astype(bf16), b[1].astype(bf16)
    return a[0] + swap(sent[0], 2, n_grp).astype(f32), b[0] + swap(sent[1], 1, n_grp).astype(f32)


def sum_scatter_grp(pieces, n_grp):
    total = pieces[0].astype(f32)
    for k in range(1, n_grp):
        total = total + swap(pieces[k].astype(bf16), k, n_grp).astype(f32)
    return total


def tree_sum(terms):
    while len(terms) > 1:
        terms = [terms[i] + terms[i + 1] for i in range(0, len(terms), 2)]
    return terms[0]


def sum_grp(x, n_grp):
    return tree_sum([y.astype(f32) for y in gather_grp(x.astype(bf16), n_grp)])


def place_grp(x, n_grp, me, axis):
    held = jnp.stack(gather_grp(x, n_grp))
    rows = [lax.dynamic_index_in_dim(held, (me ^ j).astype(jnp.uint32), 0, keepdims=False) for j in range(n_grp)]
    return jnp.stack(rows, axis=axis)


def body(
    n_grp,
    n_seq,
    layer_input,
    segments,
    ln_gain,
    ln_bias,
    w_value,
    b_value,
    w_reduce,
    b_reduce,
    lam_log,
    lam_freq,
    dss_w,
    log_step,
    w_up,
    b_up,
    w_out,
    b_out,
    out_cotangent,
):
    me = lax.axis_index("grp")
    tokens, wide = layer_input.shape
    part = w_value.shape[0] // n_grp
    quarter = n_seq * part
    reduced_width = w_reduce.shape[0] * n_seq

    small = (ln_gain, ln_bias, b_value, b_reduce, lam_log, lam_freq, b_up, b_out, segments[0].astype(bf16))
    packed = jnp.concatenate([jnp.pad(v, (0, -v.shape[0] % 128)).reshape(-1, 128) for v in small], axis=0)
    packed = jnp.pad(packed, ((0, -packed.shape[0] % 16), (0, 0)))
    packed = gather_small(packed, n_seq)
    spots, fulls = 0, []
    for array in small:
        deep = -(-array.shape[0] // 128)
        fulls.append(packed[:, spots : spots + deep].reshape(n_seq, -1)[:, : array.shape[0]])
        spots += deep
    gain_full, bias_full, value_bias, reduce_bias, decay_full, freq_full, up_bias, out_bias, doc_row = fulls
    gain_wide = gain_full.reshape(-1).astype(f32)
    bias_wide = bias_full.reshape(-1).astype(f32)
    value_bias = lax.dynamic_slice_in_dim(value_bias, me * part, part, 1).reshape(-1).astype(f32)
    up_bias = lax.dynamic_slice_in_dim(up_bias, me * part, part, 1).reshape(-1).astype(f32)

    reduce_full = lax.all_gather(w_reduce, "seq", axis=0, tiled=True)
    pieces = [lax.dynamic_slice_in_dim(w, me * part, part, 0) for w in (w_value, w_up)]
    both_part = lax.all_gather(jnp.concatenate(pieces, axis=1), "seq", axis=0, tiled=True)
    value_part, up_part = both_part[:, :wide], both_part[:, wide:]
    out_cols = lax.dynamic_index_in_dim(w_out.reshape(-1, n_seq, n_grp, part), me, 2, keepdims=False)
    out_part = lax.all_gather(out_cols.reshape(-1, quarter), "seq", axis=0, tiled=True)

    length = tokens * n_seq
    blocks = length // TILE
    deep = lag_blocks(length)
    decay = decay_full.reshape(-1).astype(f32)
    freq = freq_full.reshape(-1).astype(f32)
    weights = dss_w.astype(f32)
    steps = log_step.astype(f32)
    half = steps.shape[0] // 2
    modes = [
        (decay, freq, weights[:, :half], steps[:half]),
        (decay, freq, weights[:, half:], steps[half:]),
    ]
    tables = [make_toeplitz(*modes[0], deep)]

    x_wide = layer_input.astype(f32)
    center = x_wide - jnp.mean(x_wide, axis=1, keepdims=True)
    inverse = lax.rsqrt(jnp.mean(center * center, axis=1, keepdims=True) + epsilon)
    unit = center * inverse
    normed = (unit * gain_wide + bias_wide).astype(bf16)

    pre_reduce = (
        lax.dot_general(reduce_full, normed, contract_last, preferred_element_type=f32)
        + reduce_bias.reshape(-1).astype(f32)[:, None]
    )
    reduced, reduce_slope = gelu_parts(pre_reduce)
    reduced = reduced.astype(bf16)
    reduced, later, cot_own, normed_own, last = lax.optimization_barrier(
        (reduced, modes[1][0], out_cotangent, normed, tables[0])
    )
    tables[0] = last
    tables.append(make_toeplitz(later, *modes[1][1:], deep))
    cot_all, normed_all = gather_two(cot_own, normed_own, n_grp)
    channel_in = lax.all_to_all(reduced, "seq", split_axis=0, concat_axis=1, tiled=True)
    seg = doc_row.astype(jnp.int32).reshape(blocks, TILE)
    signal = channel_in.reshape(-1, blocks, TILE)
    halves = [slice(0, half), slice(half, 2 * half)]
    convolve, sum_lags = (lone_conv, lone_taps) if lone(length) else (any_conv, taps_grad)
    channel_out = jnp.concatenate(
        [convolve(seg, signal[h], t[0], False) for h, t in zip(halves, tables)], axis=0
    ).reshape(-1, length)
    mixed = lax.all_to_all(channel_out, "seq", split_axis=1, concat_axis=0, tiled=True)
    pre_value = lax.dot_general(normed_all, value_part, contract_last, preferred_element_type=f32) + value_bias
    mixed, activated, slope = lax.optimization_barrier((mixed, *gelu_parts(pre_value)))
    mixed_all = jnp.concatenate(gather_grp(mixed, n_grp), axis=1)
    g_gated = jnp.dot(cot_all, out_part, preferred_element_type=f32)
    activated, slope, g_gated = lax.optimization_barrier((activated, slope, g_gated))
    pre_up = lax.dot_general(mixed_all, up_part, (((0,), (1,)), ((), ())), preferred_element_type=f32) + up_bias
    gated = (activated * pre_up).astype(bf16)
    g_activated = g_gated * pre_up
    g_pre_up = (g_gated * activated).astype(bf16)
    g_pre_value = (g_activated * slope).astype(bf16)

    g_mixed = lax.dot_general(up_part, g_pre_up, (((0,), (1,)), ((), ())), preferred_element_type=f32)
    g_mixed = sum_scatter_grp([g_mixed[:, k * tokens : (k + 1) * tokens] for k in range(n_grp)], n_grp)
    added = lax.dot_general(gated, out_part, contract_last, preferred_element_type=f32)
    g_normed = jnp.dot(g_pre_value, value_part, preferred_element_type=f32)
    added, g_normed = added.astype(bf16), g_normed.astype(bf16)
    g_mixed, gated, g_pre_up, g_pre_value, added, g_normed = lax.optimization_barrier(
        (g_mixed.astype(bf16), gated, g_pre_up, g_pre_value, added, g_normed)
    )
    g_channel = lax.all_to_all(g_mixed, "seq", split_axis=0, concat_axis=1, tiled=True)
    g_channel = g_channel.reshape(-1, blocks, TILE)
    g_out = lax.dot_general(cot_all, gated, contract_first, preferred_element_type=f32).astype(bf16)
    g_up = lax.dot_general(g_pre_up, mixed_all, (((0,), (1,)), ((), ())), preferred_element_type=f32)
    g_value = lax.dot_general(g_pre_value, normed_all, contract_first, preferred_element_type=f32)
    left = (jnp.arange(TILE) < TILE // 2).astype(bf16)
    ones = [jnp.broadcast_to(m, (g_pre_value.shape[0], TILE)) for m in (left, 1 - left)]
    g_biases = lax.dot_general(g_pre_value, ones[0], contract_first, preferred_element_type=f32)
    g_biases += lax.dot_general(g_pre_up, ones[1], contract_first, preferred_element_type=f32)
    g_both = jnp.concatenate([y.astype(bf16) for y in (g_value, g_up, g_biases)], axis=1)
    g_channel, g_out, g_both, added, g_normed = lax.optimization_barrier(
        (g_channel, g_out, g_both, added, g_normed)
    )
    g_out = lax.psum_scatter(g_out, "seq", scatter_dimension=0, tiled=True)
    g_both = lax.psum_scatter(g_both, "seq", scatter_dimension=0, tiled=True)
    g_signal = jnp.concatenate([convolve(seg, g_channel[h], t[0], True) for h, t in zip(halves, tables)], axis=0)
    g_signal, g_channel = lax.optimization_barrier((g_signal, g_channel))
    g_reduced = lax.all_to_all(g_signal.reshape(-1, length), "seq", split_axis=1, concat_axis=0, tiled=True)
    added, g_normed = sum_scatter_first(added, g_normed, n_grp)
    g_channel, added, g_normed = lax.optimization_barrier((g_channel, added, g_normed))
    g_taps = sum_lags(seg, signal, g_channel)
    added, g_normed = sum_scatter_second(added, g_normed, n_grp)
    g_taps, g_reduced, added, g_normed = lax.optimization_barrier((g_taps, g_reduced, added, g_normed))
    found = [mode_grads(*m, g_taps[h], *t[1:]) for h, m, t in zip(halves, modes, tables)]
    g_lam = found[0][2] + found[1][2]
    states = g_lam.shape[1]
    output = (x_wide + added + out_bias.reshape(-1).astype(f32)).astype(bf16)

    g_pre_reduce = (g_reduced.astype(f32) * reduce_slope).astype(bf16)
    g_reduce = jnp.dot(g_pre_reduce, normed, preferred_element_type=f32)
    g_normed = g_normed + lax.dot_general(g_pre_reduce, reduce_full, contract_first, preferred_element_type=f32)
    g_unit = g_normed * gain_wide
    g_input = inverse * (
        g_unit
        - jnp.mean(g_unit, axis=1, keepdims=True)
        - unit * jnp.mean(g_unit * unit, axis=1, keepdims=True)
    ) + out_cotangent.astype(f32)

    vectors = (
        jnp.sum(g_normed * unit, axis=0).reshape(n_seq, -1),
        jnp.sum(g_normed, axis=0).reshape(n_seq, -1),
        jnp.sum(g_pre_reduce.astype(f32), axis=1).reshape(n_seq, -1),
        g_lam[0].reshape(n_seq, -1),
        g_lam[1].reshape(n_seq, -1),
        jnp.sum(out_cotangent.astype(f32), axis=0).reshape(n_seq, -1),
    )
    flat = jnp.concatenate(vectors, axis=1)
    flat = jnp.pad(flat, ((0, 0), (0, -flat.shape[1] % wide))).reshape(n_seq, -1, wide)
    own = jnp.concatenate([g_reduce.reshape(n_seq, -1, wide).astype(bf16), flat.astype(bf16)], axis=1)
    own, g_out, g_both = lax.optimization_barrier((own, g_out, g_both))
    own = lax.psum_scatter(own, "seq", scatter_dimension=0, tiled=False)
    packed = [f[0][i].reshape(-1) for i in range(2) for f in found] + [f[1] for f in found]
    packed.append(jnp.zeros((-2 * half % wide,), f32))
    packed = jnp.concatenate(packed).reshape(-1, wide).astype(bf16)
    packed = sum_grp(packed, n_grp)
    own = sum_grp(own, n_grp)
    g_reduce, shard = own[: w_reduce.shape[0]], own[w_reduce.shape[0] :].reshape(-1)
    g_weights = packed[:-1].reshape(2, -1, states)
    g_step = packed[-1][: 2 * half]
    placed = place_grp(g_out, n_grp, me, 0)
    g_out = placed.reshape(n_grp, -1, n_seq, part).transpose(1, 2, 0, 3).reshape(w_out.shape).astype(f32)
    placed = place_grp(g_both, n_grp, me, 0).reshape(w_value.shape[0], -1).astype(f32)
    g_value, g_up = placed[:, :wide], placed[:, wide : wide + w_up.shape[1]]
    g_value_bias, g_up_bias = placed[:, wide + w_up.shape[1]], placed[:, -1]
    sums, spots = [], 0
    for array in vectors:
        sums.append(shard[spots : spots + array.shape[1]])
        spots += array.shape[1]
    g_gain, g_bias, g_reduce_bias, g_decay, g_freq, g_out_bias = sums
    return (
        output,
        g_input,
        g_gain,
        g_bias,
        g_value,
        g_value_bias,
        g_reduce,
        g_reduce_bias,
        g_decay,
        g_freq,
        g_weights,
        g_step,
        g_up,
        g_up_bias,
        g_out,
        g_out_bias,
    )


def solution(mesh):
    by_token = P(("grp", "seq"), None)
    row, matrix, cube = P("seq"), P("seq", None), P(None, "seq", None)
    layer = (row, row, matrix, row, matrix, row, row, row, cube, row, matrix, row, matrix, row)
    return jax.shard_map(
        functools.partial(body, mesh.shape["grp"], mesh.shape["seq"]),
        mesh=mesh,
        in_specs=(by_token, P("grp", "seq"), *layer, by_token),
        out_specs=(by_token, by_token, *layer),
        check_vma=False,
    )
```

```python
import functools

import jax
import jax.numpy as jnp
from jax import lax
from jax.experimental import pallas as pl
from jax.experimental.pallas import tpu as pltpu
from jax.sharding import PartitionSpec as P

f32, bf16 = jnp.float32, jnp.bfloat16
TILE = 128
MOST = 2000
LAGS = 2048
FINE = 64
EXTRA = 16
PART = 64
ROWS = 8
NT = (((1,), (1,)), ((), ()))
TN = (((0,), (0,)), ((), ()))


def params(mb=48):
    return pltpu.CompilerParams(vmem_limit_bytes=mb << 20)


def cost(us):
    return pl.CostEstimate(flops=us * 10**9, bytes_accessed=us * 10**6, transcendentals=0)


def lag_blocks(length):
    return min(length // TILE, (MOST + TILE - 2) // TILE + 1)


def doc_count(length):
    return length // 1024 + 1


def over_channels(step, unroll):
    def some(i, _):
        for u in range(unroll):
            step(i * unroll + u, u)
        return 0

    lax.fori_loop(0, ROWS // unroll, some, 0)


def cmul(a, b):
    return (a[0] * b[0] - a[1] * b[1], a[0] * b[1] + a[1] * b[0])


def mode_rates(lam_log_ref, lam_freq_ref, step_ref):
    lam_re = -jnp.exp(lam_log_ref[...])
    lam_im = lam_freq_ref[...]
    delta = jnp.exp(step_ref[...])
    return lam_re, lam_im, delta


def first_power(lam_re, lam_im, delta):
    growth = jnp.exp(delta * lam_re)
    phase = delta * lam_im
    return growth * jnp.cos(phase), growth * jnp.sin(phase)


def store_squares(one, sq_ref):
    cur = one
    for k in range(11):
        sq_ref[0, k], sq_ref[1, k] = cur
        if k < 10:
            cur = cmul(cur, cur)


def power_tiles(sq_ref, c, first, count):
    def sq(k):
        return sq_ref[0, k, pl.ds(c, 1), :], sq_ref[1, k, pl.ds(c, 1), :]

    width = sq_ref.shape[-1]
    row = lax.broadcasted_iota(jnp.int32, (8, width), 0)
    tile = None
    for k in range(3):
        re, im = sq(first + k)
        on = (row & (1 << k)) != 0
        term = jnp.where(on, re, 1.0), jnp.where(on, im, 0.0)
        tile = term if tile is None else cmul(tile, term)
    tiles, k = [tile], 3
    while len(tiles) < count:
        step = sq(first + k)
        tiles = tiles + [cmul(t, step) for t in tiles]
        k += 1
    return tiles


def split(x):
    hi = x.astype(bf16)
    return hi, (x - hi.astype(f32)).astype(bf16)


def coarse_tiles(sq_ref, c):
    even = power_tiles(sq_ref, c, 7, LAGS // TILE // 8)
    half = sq_ref[0, 6, pl.ds(c, 1), :], sq_ref[1, 6, pl.ds(c, 1), :]
    return even + [cmul(t, half) for t in even]


def taps_kernel(
    lam_log_ref, lam_freq_ref, w_ref, step_ref, tt_ref, qh_ref, sq_ref, cf_ref, p_ref, ql_ref
):
    lam_re, lam_im, delta = mode_rates(lam_log_ref, lam_freq_ref, step_ref)
    one = first_power(lam_re, lam_im, delta)
    store_squares(one, sq_ref)
    modulus = lam_re * lam_re + lam_im * lam_im
    shift_re, shift_im = one[0] - 1.0, one[1]
    ratio = (
        (shift_re * lam_re + shift_im * lam_im) / modulus,
        (shift_im * lam_re - shift_re * lam_im) / modulus,
    )
    cf_ref[0], cf_ref[1] = cmul((w_ref[0], w_ref[1]), ratio)
    width = sq_ref.shape[-1]
    deep = tt_ref.shape[2] // TILE
    coarse = LAGS // FINE

    def channel(c, u):
        for t, pair in enumerate(power_tiles(sq_ref, c, 0, FINE // 8)):
            if t % 2 == 0:
                held = pair
                continue
            for part in range(2):
                hi, lo = split(jnp.concatenate([held[part], pair[part]], axis=0))
                qh_ref[c, 8 * t - 8 : 8 * t + 8, part * width : (part + 1) * width] = hi
                ql_ref[u, 8 * t - 8 : 8 * t + 8, part * width : (part + 1) * width] = lo
        coeff = cf_ref[0, pl.ds(c, 1), :], cf_ref[1, pl.ds(c, 1), :]
        tiles = [cmul(t, coeff) for t in coarse_tiles(sq_ref, c)]
        for part, sign in ((0, 1.0), (1, -1.0)):
            hi, lo = split(sign * jnp.concatenate([t[part] for t in tiles], axis=0))
            p_ref[u, :coarse, part * width : (part + 1) * width] = hi
            p_ref[u, coarse:, part * width : (part + 1) * width] = lo
        both = lax.dot_general(qh_ref[c], p_ref[u], NT, preferred_element_type=f32)
        low = lax.dot_general(ql_ref[u], p_ref[u, :coarse], NT, preferred_element_type=f32)
        taps = (both[:, :coarse] + both[:, coarse:] + low).T
        taps = jnp.concatenate([taps[: coarse // 2], taps[coarse // 2 :]], axis=1)
        rows = [jnp.broadcast_to(taps[d : d + 1], (8, TILE)) for d in range(min(deep, LAGS // TILE))]
        gap = jnp.zeros((8, TILE), f32)
        source = jnp.concatenate([gap] + rows + [gap] * (deep - len(rows)), axis=1)
        for r in range(PART // 16):
            pair = [pltpu.roll(source, 16 * r + s, 1, stride=1, stride_axis=0)[:, TILE:] for s in (0, 8)]
            tt_ref[c, 16 * r : 16 * r + 16, :] = jnp.concatenate(pair, axis=0).astype(bf16)

    over_channels(channel, p_ref.shape[0])


def make_toeplitz(lam_log, lam_freq, weights, log_step, deep):
    channels, modes = weights.shape[1:]
    table = pl.BlockSpec((ROWS, FINE, 2 * modes), lambda i: (i, 0, 0))
    return pl.pallas_call(
        taps_kernel,
        grid=(channels // ROWS,),
        in_specs=[
            pl.BlockSpec((1, modes), lambda i: (0, 0)),
            pl.BlockSpec((1, modes), lambda i: (0, 0)),
            pl.BlockSpec((2, ROWS, modes), lambda i: (0, i, 0)),
            pl.BlockSpec((ROWS, 1), lambda i: (i, 0)),
        ],
        out_specs=[pl.BlockSpec((ROWS, PART, deep * TILE), lambda i: (i, 0, 0)), table],
        out_shape=[
            jax.ShapeDtypeStruct((channels, PART, deep * TILE), bf16),
            jax.ShapeDtypeStruct((channels, FINE, 2 * modes), bf16),
        ],
        scratch_shapes=[
            pltpu.VMEM((2, 11, ROWS, modes), f32),
            pltpu.VMEM((2, ROWS, modes), f32),
            pltpu.VMEM((4, 2 * LAGS // FINE, 2 * modes), bf16),
            pltpu.VMEM((4, FINE, 2 * modes), bf16),
        ],
        compiler_params=params(57),
        cost_estimate=cost(3),
    )(lam_log[None], lam_freq[None], weights, log_step[:, None])


def doc_windows(z, seg, docs, zs_ref, zw_ref, u, deep):
    blocks = z.shape[0]
    lane = lax.broadcasted_iota(jnp.int32, z.shape, 1)
    for k in range(docs):
        own = jnp.where(seg == k, z, 0.0)
        after = jnp.concatenate([own[1:], jnp.zeros((1, TILE), f32)], axis=0)
        zs_ref[u, 2 * k, :blocks, :] = own
        zs_ref[u, 2 * k + 1, :blocks, :] = pltpu.roll(jnp.where(lane < PART, after, own), TILE - PART, 1)
    for k in range(2 * docs):
        for d in range(deep):
            zw_ref[u, k * blocks : (k + 1) * blocks, d * TILE : (d + 1) * TILE] = zs_ref[
                u, k, d : d + blocks, :
            ].astype(bf16)


def conv_kernel(docs, back, seg_ref, rows_ref, lanes_ref, x_ref, tt_ref, y_ref, zs_ref, zw_ref, xr_ref):
    blocks, deep = x_ref.shape[1], tt_ref.shape[2] // TILE
    zs_ref[...] = jnp.zeros(zs_ref.shape, f32)
    seg = seg_ref[...].astype(f32)
    if not back:
        rows, lanes = rows_ref[...], lanes_ref[...]
        seg = turn(seg.astype(bf16), rows[:blocks, :blocks], lanes)
        xr_ref[...] = turn(x_ref[...].reshape(ROWS * blocks, TILE), rows, lanes).reshape(xr_ref.shape)

    def channel(c, u):
        z = x_ref[c].astype(f32) if back else xr_ref[c]
        doc_windows(z, seg, docs, zs_ref, zw_ref, u, deep)
        y = lax.dot_general(zw_ref[u], tt_ref[c], NT, preferred_element_type=f32)
        out = jnp.zeros((blocks, TILE), f32)
        for k in range(docs):
            at = 2 * k * blocks
            mine = jnp.concatenate([y[at : at + blocks], y[at + blocks : at + 2 * blocks]], axis=1)
            out = jnp.where(seg == k, mine, out)
        if back:
            y_ref[c] = out.astype(bf16)
        else:
            xr_ref[c] = out

    over_channels(channel, zw_ref.shape[0])
    if not back:
        y = turn(xr_ref[...].astype(bf16).reshape(ROWS * blocks, TILE), rows, lanes)
        y_ref[...] = y.astype(bf16).reshape(y_ref.shape)


def any_conv(seg, x, tt, back, unroll=2):
    channels, blocks, _ = x.shape
    deep = tt.shape[2] // TILE
    docs = doc_count(blocks * TILE)
    rows, lanes = reverse_maps(blocks)
    cut = pl.BlockSpec((ROWS, blocks, TILE), lambda i: (i, 0, 0))
    return pl.pallas_call(
        functools.partial(conv_kernel, docs, back),
        grid=(channels // ROWS,),
        in_specs=[
            whole(seg),
            whole(rows),
            whole(lanes),
            cut,
            pl.BlockSpec((ROWS, PART, deep * TILE), lambda i: (i, 0, 0)),
        ],
        out_specs=cut,
        out_shape=jax.ShapeDtypeStruct(x.shape, bf16),
        scratch_shapes=[
            pltpu.VMEM((unroll, 2 * docs, blocks + deep - 1, TILE), f32),
            pltpu.VMEM((unroll, 2 * docs * blocks, deep * TILE), bf16),
            pltpu.VMEM((ROWS, blocks, TILE), f32),
        ],
        compiler_params=params(),
        cost_estimate=cost(3),
    )(seg, rows, lanes, x, tt)


def taps_grad_kernel(docs, seg_ref, flip_ref, x_ref, g_ref, dt_ref, gs_ref, gw_ref, xst_ref, wide_ref):
    wide_ref[...] = jnp.zeros(wide_ref.shape, f32)
    blocks = x_ref.shape[1]
    deep = gw_ref.shape[2] // TILE
    lead = deep - 1
    cuts = TILE // PART
    seg = seg_ref[...]
    lane = lax.broadcasted_iota(jnp.int32, (blocks, TILE), 1)
    for u in range(gs_ref.shape[0]):
        for k in range(docs * cuts):
            gs_ref[u, k, blocks:, :] = jnp.zeros((lead, TILE), f32)

    def one(c, u):
        g = g_ref[c].astype(f32)
        x = x_ref[c].astype(f32)
        for k in range(docs):
            own = jnp.where(seg == k, g, 0.0)
            gs_ref[u, k * cuts, :blocks, :] = own
            after = jnp.concatenate([own[1:], jnp.zeros((1, TILE), f32)], axis=0)
            for p in range(1, cuts):
                gs_ref[u, k * cuts + p, :blocks, :] = pltpu.roll(
                    jnp.where(lane < p * PART, after, own), TILE - p * PART, 1
                )
            mine = jnp.where(seg == k, x, 0.0).astype(bf16)
            mine = jnp.dot(mine, flip_ref[...], preferred_element_type=f32).astype(bf16)
            for p in range(cuts):
                at = (k * cuts + p) * blocks
                xst_ref[u, at : at + blocks, :] = mine[:, p * PART : (p + 1) * PART]
        for k in range(docs * cuts):
            for d in range(deep):
                gw_ref[u, k * blocks : (k + 1) * blocks, d * TILE : (d + 1) * TILE] = gs_ref[
                    u, k, d : d + blocks, :
                ].astype(bf16)
        wide_ref[u, :, : deep * TILE] = lax.dot_general(xst_ref[u], gw_ref[u], TN, preferred_element_type=f32)
        total = jnp.zeros((8, LAGS), f32)
        for r in range(0, PART, 8):
            rows = wide_ref[u, r : r + 8, :]
            total += pltpu.roll(rows, rows.shape[1] - (PART - 1) + r, 1, stride=1, stride_axis=0)[:, :LAGS]
        dt_ref[pl.ds(c, 1), :] = jnp.sum(total, axis=0, keepdims=True)

    def pair(i, _):
        for u in range(gs_ref.shape[0]):
            one(i * gs_ref.shape[0] + u, u)
        return 0

    lax.fori_loop(0, ROWS // gs_ref.shape[0], pair, 0)


def taps_grad(seg, x, g, unroll=4):
    channels, blocks, _ = x.shape
    deep = lag_blocks(blocks * TILE)
    docs = doc_count(blocks * TILE)
    cuts = TILE // PART
    place = jnp.arange(TILE)
    flip = (place[:, None] == (place // PART * PART + PART - 1 - place % PART)[None, :]).astype(bf16)
    rows = pl.BlockSpec((ROWS, blocks, TILE), lambda i: (i, 0, 0))
    return pl.pallas_call(
        functools.partial(taps_grad_kernel, docs),
        grid=(channels // ROWS,),
        in_specs=[
            pl.BlockSpec((blocks, TILE), lambda i: (0, 0)),
            pl.BlockSpec((TILE, TILE), lambda i: (0, 0)),
            rows,
            rows,
        ],
        out_specs=pl.BlockSpec((ROWS, LAGS), lambda i: (i, 0)),
        out_shape=jax.ShapeDtypeStruct((channels, LAGS), f32),
        scratch_shapes=[
            pltpu.VMEM((unroll, docs * cuts, blocks + deep - 1, TILE), f32),
            pltpu.VMEM((unroll, docs * cuts * blocks, deep * TILE), bf16),
            pltpu.VMEM((unroll, docs * cuts * blocks, PART), bf16),
            pltpu.VMEM((unroll, PART, (deep + 1) * TILE), f32),
        ],
        compiler_params=params(),
        cost_estimate=cost(4),
    )(seg, flip, x, g)


def lone(length):
    return MOST < length <= MOST + PART and 2 * doc_count(length) <= EXTRA


def lone_masks(seg, docs):
    blocks = seg.shape[0]
    long = jnp.zeros(seg.shape, f32)
    row = lax.broadcasted_iota(jnp.int32, (EXTRA, PART), 0)
    ends = jnp.where(row % 2 == 0, seg[:1, :PART], seg[blocks - 1 :, TILE - PART :])
    extra = jnp.zeros((EXTRA, PART), f32)
    for k in range(docs):
        here = (seg == k).astype(f32)
        count = jnp.sum(jnp.sum(here, axis=0, keepdims=True), axis=1, keepdims=True)
        long += jnp.where(count >= MOST, here, 0.0)
        extra += jnp.where((row // 2 == k) & (ends == k) & (count[:, :1] < MOST), 1.0, 0.0)
    return long, extra


def end_rows(z, extra):
    even = lax.broadcasted_iota(jnp.int32, extra.shape, 0) % 2 == 0
    return jnp.where(even, z[:1, :PART], z[z.shape[0] - 1 :, TILE - PART :]) * extra


def store_windows(z, long, extra, zs_ref, zw_ref, u, deep):
    blocks = z.shape[0]
    own = z * long
    after = jnp.concatenate([own[1:], jnp.zeros((1, TILE), f32)], axis=0)
    lane = lax.broadcasted_iota(jnp.int32, own.shape, 1)
    zs_ref[u, 0, :blocks, :] = own
    zs_ref[u, 1, :blocks, :] = pltpu.roll(jnp.where(lane < PART, after, own), TILE - PART, 1)
    for p in range(2):
        for d in range(deep):
            zw_ref[u, p * blocks : (p + 1) * blocks, d * TILE : (d + 1) * TILE] = zs_ref[
                u, p, d : d + blocks, :
            ].astype(bf16)
    ends = end_rows(z, extra)
    zw_ref[u, 2 * blocks :, :TILE] = jnp.concatenate([ends, jnp.zeros_like(ends)], axis=1).astype(bf16)


def turn(x, rows, lanes):
    x = jnp.dot(rows, x, preferred_element_type=f32).astype(bf16)
    return jnp.dot(x, lanes, preferred_element_type=f32)


def lone_conv_kernel(docs, back, seg_ref, rows_ref, lanes_ref, x_ref, tt_ref, y_ref, zs_ref, zw_ref, xr_ref):
    blocks, deep = x_ref.shape[1], tt_ref.shape[2] // TILE
    zw_ref[...] = jnp.zeros(zw_ref.shape, bf16)
    zs_ref[...] = jnp.zeros(zs_ref.shape, f32)
    seg = seg_ref[...].astype(f32)
    if not back:
        rows, lanes = rows_ref[...], lanes_ref[...]
        seg = turn(seg.astype(bf16), rows[:blocks, :blocks], lanes)
        xr_ref[...] = turn(x_ref[...].reshape(ROWS * blocks, TILE), rows, lanes).reshape(xr_ref.shape)
    long, extra = lone_masks(seg, docs)
    even = lax.broadcasted_iota(jnp.int32, extra.shape, 0) % 2 == 0
    place = lax.broadcasted_iota(jnp.int32, (blocks, PART), 0)

    def channel(c, u):
        z = x_ref[c].astype(f32) if back else xr_ref[c]
        store_windows(z, long, extra, zs_ref, zw_ref, u, deep)
        y = lax.dot_general(zw_ref[u], tt_ref[c], NT, preferred_element_type=f32)
        ends = y[2 * blocks :] * extra
        first = jnp.sum(jnp.where(even, ends, 0.0), axis=0, keepdims=True)
        last = jnp.sum(jnp.where(even, 0.0, ends), axis=0, keepdims=True)
        ends = jnp.concatenate([jnp.where(place == 0, first, 0.0), jnp.where(place == blocks - 1, last, 0.0)], axis=1)
        y = jnp.concatenate([y[:blocks], y[blocks : 2 * blocks]], axis=1) * long + ends
        if back:
            y_ref[c] = y.astype(bf16)
        else:
            xr_ref[c] = y

    over_channels(channel, zw_ref.shape[0])
    if not back:
        y = turn(xr_ref[...].astype(bf16).reshape(ROWS * blocks, TILE), rows, lanes)
        y_ref[...] = y.astype(bf16).reshape(y_ref.shape)


def reverse_maps(blocks):
    row = jnp.arange(ROWS * blocks)
    lane = jnp.arange(TILE)
    rows = row[:, None] == (row // blocks * blocks + blocks - 1 - row % blocks)[None, :]
    return rows.astype(bf16), (lane[:, None] == TILE - 1 - lane[None, :]).astype(bf16)


def whole(a):
    return pl.BlockSpec(a.shape, lambda i: (0,) * a.ndim)


def lone_conv(seg, x, tt, back, unroll=8):
    channels, blocks, _ = x.shape
    deep = tt.shape[2] // TILE
    rows, lanes = reverse_maps(blocks)
    cut = pl.BlockSpec((ROWS, blocks, TILE), lambda i: (i, 0, 0))
    return pl.pallas_call(
        functools.partial(lone_conv_kernel, doc_count(blocks * TILE), back),
        grid=(channels // ROWS,),
        in_specs=[
            whole(seg),
            whole(rows),
            whole(lanes),
            cut,
            pl.BlockSpec((ROWS, PART, deep * TILE), lambda i: (i, 0, 0)),
        ],
        out_specs=cut,
        out_shape=jax.ShapeDtypeStruct(x.shape, bf16),
        scratch_shapes=[
            pltpu.VMEM((unroll, 2, blocks + deep - 1, TILE), f32),
            pltpu.VMEM((unroll, 2 * blocks + EXTRA, deep * TILE), bf16),
            pltpu.VMEM((ROWS, blocks, TILE), f32),
        ],
        compiler_params=params(),
        cost_estimate=cost(3),
    )(seg, rows, lanes, x, tt)


def lone_taps_kernel(docs, seg_ref, lanes_ref, x_ref, g_ref, dt_ref, zs_ref, zw_ref, xs_ref, xr_ref):
    blocks = x_ref.shape[1]
    deep = zw_ref.shape[2] // TILE
    zw_ref[...] = jnp.zeros(zw_ref.shape, bf16)
    zs_ref[...] = jnp.zeros(zs_ref.shape, f32)
    lanes = lanes_ref[...]
    seg = seg_ref[...].astype(f32)
    long, extra = lone_masks(seg, docs)
    turned_long, turned_extra = lone_masks(jnp.dot(seg.astype(bf16), lanes, preferred_element_type=f32), docs)
    flat = x_ref[...].reshape(ROWS * blocks, TILE)
    xr_ref[...] = jnp.dot(flat, lanes, preferred_element_type=f32).reshape(xr_ref.shape)

    def channel(c, u):
        store_windows(g_ref[c].astype(f32), long, extra, zs_ref, zw_ref, u, deep)
        x = xr_ref[c]
        own = (x * turned_long).astype(bf16)
        for p in range(2):
            xs_ref[u, p * blocks : (p + 1) * blocks, :] = own[:, p * PART : (p + 1) * PART]
        xs_ref[u, 2 * blocks :, :] = end_rows(x, turned_extra).astype(bf16)
        wide = lax.dot_general(xs_ref[u], zw_ref[u], TN, preferred_element_type=f32)
        wide = jnp.concatenate([wide, jnp.zeros((PART, TILE), f32)], axis=1)
        total = jnp.zeros((8, LAGS), f32)
        for r in range(0, PART, 8):
            total += pltpu.roll(
                wide[r : r + 8], wide.shape[1] - (PART - 1) + r, 1, stride=1, stride_axis=0
            )[:, :LAGS]
        dt_ref[pl.ds(c, 1), :] = jnp.sum(total, axis=0, keepdims=True)

    over_channels(channel, zw_ref.shape[0])


def lone_taps(seg, x, g, unroll=4):
    channels, blocks, _ = x.shape
    deep = lag_blocks(blocks * TILE)
    place = jnp.arange(TILE)
    lanes = (place[:, None] == (place // PART * PART + PART - 1 - place % PART)[None, :]).astype(bf16)
    cut = pl.BlockSpec((ROWS, blocks, TILE), lambda i: (i, 0, 0))
    return pl.pallas_call(
        functools.partial(lone_taps_kernel, doc_count(blocks * TILE)),
        grid=(channels // ROWS,),
        in_specs=[whole(seg), whole(lanes), cut, cut],
        out_specs=pl.BlockSpec((ROWS, LAGS), lambda i: (i, 0)),
        out_shape=jax.ShapeDtypeStruct((channels, LAGS), f32),
        scratch_shapes=[
            pltpu.VMEM((unroll, 2, blocks + deep - 1, TILE), f32),
            pltpu.VMEM((unroll, 2 * blocks + EXTRA, deep * TILE), bf16),
            pltpu.VMEM((unroll, 2 * blocks + EXTRA, PART), bf16),
            pltpu.VMEM((ROWS, blocks, TILE), f32),
        ],
        compiler_params=params(),
        cost_estimate=cost(4),
    )(seg, lanes, x, g)


def mode_grad_kernel(
    lam_log_ref, lam_freq_ref, w_ref, step_ref, dt_ref, qh_ref, gw_ref, gstep_ref, glam_ref, sq_ref, s_ref
):
    lam_re, lam_im, delta = mode_rates(lam_log_ref, lam_freq_ref, step_ref)
    one = first_power(lam_re, lam_im, delta)
    store_squares(one, sq_ref)
    width = sq_ref.shape[-1]
    coarse = LAGS // FINE

    def channel(c, u):
        dt = dt_ref[c]
        dt = jnp.concatenate([dt[:, :FINE], dt[:, FINE:]], axis=0)
        lane = lax.broadcasted_iota(jnp.int32, (coarse, FINE), 1).astype(f32)
        hi, lo = split(jnp.concatenate([dt, dt * lane], axis=0))
        both = jnp.dot(jnp.concatenate([hi, lo], axis=0), qh_ref[c], preferred_element_type=f32)
        v = both[: 2 * coarse] + both[2 * coarse :]
        tiles = coarse_tiles(sq_ref, c)
        power = tuple(jnp.concatenate([t[part] for t in tiles], axis=0) for part in range(2))
        v0 = v[:coarse, :width], v[:coarse, width:]
        row = lax.broadcasted_iota(jnp.int32, (coarse, width), 0)
        far = (row % (coarse // 2)) * (2 * FINE) + (row // (coarse // 2)) * FINE
        far = far.astype(f32)
        v1 = tuple(far * v0[part] + v[coarse:, part * width : (part + 1) * width] for part in range(2))
        for n, pair in enumerate((v0, v1)):
            prod = cmul(power, pair)
            for part in range(2):
                s_ref[2 * n + part, pl.ds(c, 1), :] = jnp.sum(prod[part], axis=0, keepdims=True)

    over_channels(channel, 8)
    modulus = lam_re * lam_re + lam_im * lam_im
    inv = lam_re / modulus, -lam_im / modulus
    shift = one[0] - 1.0, one[1]
    ratio = cmul(shift, inv)
    w = w_ref[0], w_ref[1]
    s0 = s_ref[0], s_ref[1]
    s1 = s_ref[2], s_ref[3]
    coeff = cmul(w, ratio)
    gw = cmul(s0, ratio)
    gw_ref[0], gw_ref[1] = gw[0], -gw[1]
    near = cmul(s0, cmul(w, cmul(one, inv)))
    far = cmul(coeff, s1)
    z = near[0] + far[0], near[1] + far[1]
    back = cmul(s0, cmul(coeff, inv))
    big = delta * z[0] - back[0], delta * z[1] - back[1]
    step = jnp.sum((z[0] * lam_re - z[1] * lam_im) * delta, axis=1, keepdims=True)
    gstep_ref[...] = jnp.broadcast_to(step, gstep_ref.shape)

    @pl.when(pl.program_id(0) == 0)
    def _():
        glam_ref[...] = jnp.zeros(glam_ref.shape, f32)

    glam_ref[0] += big[0] * lam_re
    glam_ref[1] -= big[1]


def mode_grads(lam_log, lam_freq, weights, log_step, dt, fine):
    channels, modes = weights.shape[1:]
    rows = LAGS // TILE
    table = pl.BlockSpec((ROWS, FINE, 2 * modes), lambda i: (i, 0, 0))
    gw, gstep, glam = pl.pallas_call(
        mode_grad_kernel,
        grid=(channels // ROWS,),
        in_specs=[
            pl.BlockSpec((1, modes), lambda i: (0, 0)),
            pl.BlockSpec((1, modes), lambda i: (0, 0)),
            pl.BlockSpec((2, ROWS, modes), lambda i: (0, i, 0)),
            pl.BlockSpec((ROWS, 1), lambda i: (i, 0)),
            pl.BlockSpec((ROWS, rows, TILE), lambda i: (i, 0, 0)),
            table,
        ],
        out_specs=[
            pl.BlockSpec((2, ROWS, modes), lambda i: (0, i, 0)),
            pl.BlockSpec((ROWS, TILE), lambda i: (i, 0)),
            pl.BlockSpec((2, ROWS, modes), lambda i: (0, 0, 0)),
        ],
        out_shape=[
            jax.ShapeDtypeStruct((2, channels, modes), f32),
            jax.ShapeDtypeStruct((channels, TILE), f32),
            jax.ShapeDtypeStruct((2, ROWS, modes), f32),
        ],
        scratch_shapes=[
            pltpu.VMEM((2, 11, ROWS, modes), f32),
            pltpu.VMEM((4, ROWS, modes), f32),
        ],
        compiler_params=params(),
        cost_estimate=cost(2),
    )(lam_log[None], lam_freq[None], weights, log_step[:, None], dt.reshape(channels, rows, TILE), fine)
    return gw, gstep[:, 0], jnp.sum(glam, axis=1)


epsilon = 1e-05
contract_last = (((1,), (1,)), ((), ()))
contract_first = (((0,), (0,)), ((), ()))


def swap(x, k, n_grp):
    return x if k == 0 else lax.ppermute(x, "grp", [(i, i ^ k) for i in range(n_grp)])


def gather_small(x, n_seq):
    held = lax.dynamic_update_index_in_dim(jnp.zeros((n_seq, *x.shape), x.dtype), x, lax.axis_index("seq"), 0)
    for k in range(n_seq.bit_length() - 1):
        held = held + lax.ppermute(held, "seq", [(i, i ^ (1 << k)) for i in range(n_seq)])
    return held


def gelu_parts(v):
    t = jnp.tanh(0.7978845608028654 * (v + 0.044715 * (v * v * v)))
    half = 0.5 * (1.0 + t)
    return v * half, half + 0.5 * v * (1.0 - t * t) * 0.7978845608028654 * (1.0 + 0.134145 * (v * v))


def gather_grp(x, n_grp):
    return [swap(x, k, n_grp) for k in range(n_grp)]


def gather_two(a, b, n_grp):
    if n_grp != 4:
        return [jnp.concatenate(gather_grp(x, n_grp), axis=0) for x in (a, b)]
    rows = a.shape[0]
    a_near, b_near = swap(a, 1, n_grp), swap(b, 2, n_grp)
    a = jnp.concatenate([a, a_near], axis=0)
    b = jnp.concatenate([b, b_near], axis=0)
    a_far, b_far = swap(a, 2, n_grp), swap(b, 1, n_grp)
    return jnp.concatenate([a, a_far], axis=0), jnp.concatenate([b[:rows], b_far[:rows], b[rows:], b_far[rows:]], axis=0)


def sum_scatter_first(a, b, n_grp):
    a, b = (x.reshape(n_grp, -1, x.shape[1]) for x in (a, b))
    if n_grp != 4:
        return a, b
    a = a.reshape(2, 2, *a.shape[1:])
    sent = a[:, 1].astype(bf16), b[2:].astype(bf16)
    a = a[:, 0].astype(f32) + swap(sent[0], 1, n_grp).astype(f32)
    return a, b[:2].astype(f32) + swap(sent[1], 2, n_grp).astype(f32)


def sum_scatter_second(a, b, n_grp):
    if n_grp != 4:
        return [sum_scatter_grp([x[k] for k in range(n_grp)], n_grp) for x in (a, b)]
    sent = a[1].astype(bf16), b[1].astype(bf16)
    return a[0] + swap(sent[0], 2, n_grp).astype(f32), b[0] + swap(sent[1], 1, n_grp).astype(f32)


def sum_scatter_grp(pieces, n_grp):
    total = pieces[0].astype(f32)
    for k in range(1, n_grp):
        total = total + swap(pieces[k].astype(bf16), k, n_grp).astype(f32)
    return total


def tree_sum(terms):
    while len(terms) > 1:
        terms = [terms[i] + terms[i + 1] for i in range(0, len(terms), 2)]
    return terms[0]


def sum_grp(x, n_grp):
    return tree_sum([y.astype(f32) for y in gather_grp(x.astype(bf16), n_grp)])


def place_grp(x, n_grp, me, axis):
    held = jnp.stack(gather_grp(x, n_grp))
    rows = [lax.dynamic_index_in_dim(held, (me ^ j).astype(jnp.uint32), 0, keepdims=False) for j in range(n_grp)]
    return jnp.stack(rows, axis=axis)


def body(
    n_grp,
    n_seq,
    layer_input,
    segments,
    ln_gain,
    ln_bias,
    w_value,
    b_value,
    w_reduce,
    b_reduce,
    lam_log,
    lam_freq,
    dss_w,
    log_step,
    w_up,
    b_up,
    w_out,
    b_out,
    out_cotangent,
):
    me = lax.axis_index("grp")
    tokens, wide = layer_input.shape
    part = w_value.shape[0] // n_grp
    quarter = n_seq * part
    reduced_width = w_reduce.shape[0] * n_seq

    small = (ln_gain, ln_bias, b_value, b_reduce, lam_log, lam_freq, b_up, b_out, segments[0].astype(bf16))
    packed = jnp.concatenate([jnp.pad(v, (0, -v.shape[0] % 128)).reshape(-1, 128) for v in small], axis=0)
    packed = jnp.pad(packed, ((0, -packed.shape[0] % 16), (0, 0)))
    packed = gather_small(packed, n_seq)
    spots, fulls = 0, []
    for array in small:
        deep = -(-array.shape[0] // 128)
        fulls.append(packed[:, spots : spots + deep].reshape(n_seq, -1)[:, : array.shape[0]])
        spots += deep
    gain_full, bias_full, value_bias, reduce_bias, decay_full, freq_full, up_bias, out_bias, doc_row = fulls
    gain_wide = gain_full.reshape(-1).astype(f32)
    bias_wide = bias_full.reshape(-1).astype(f32)
    value_bias = lax.dynamic_slice_in_dim(value_bias, me * part, part, 1).reshape(-1).astype(f32)
    up_bias = lax.dynamic_slice_in_dim(up_bias, me * part, part, 1).reshape(-1).astype(f32)

    reduce_full = lax.all_gather(w_reduce, "seq", axis=0, tiled=True)
    pieces = [lax.dynamic_slice_in_dim(w, me * part, part, 0) for w in (w_value, w_up)]
    both_part = lax.all_gather(jnp.concatenate(pieces, axis=1), "seq", axis=0, tiled=True)
    value_part, up_part = both_part[:, :wide], both_part[:, wide:]
    out_cols = lax.dynamic_index_in_dim(w_out.reshape(-1, n_seq, n_grp, part), me, 2, keepdims=False)
    out_part = lax.all_gather(out_cols.reshape(-1, quarter), "seq", axis=0, tiled=True)

    length = tokens * n_seq
    blocks = length // TILE
    deep = lag_blocks(length)
    decay = decay_full.reshape(-1).astype(f32)
    freq = freq_full.reshape(-1).astype(f32)
    weights = dss_w.astype(f32)
    steps = log_step.astype(f32)
    half = steps.shape[0] // 2
    modes = [
        (decay, freq, weights[:, :half], steps[:half]),
        (decay, freq, weights[:, half:], steps[half:]),
    ]
    tables = [make_toeplitz(*modes[0], deep)]

    x_wide = layer_input.astype(f32)
    center = x_wide - jnp.mean(x_wide, axis=1, keepdims=True)
    inverse = lax.rsqrt(jnp.mean(center * center, axis=1, keepdims=True) + epsilon)
    unit = center * inverse
    normed = (unit * gain_wide + bias_wide).astype(bf16)

    pre_reduce = (
        lax.dot_general(reduce_full, normed, contract_last, preferred_element_type=f32)
        + reduce_bias.reshape(-1).astype(f32)[:, None]
    )
    reduced, reduce_slope = gelu_parts(pre_reduce)
    reduced = reduced.astype(bf16)
    reduced, later, cot_own, normed_own, last = lax.optimization_barrier(
        (reduced, modes[1][0], out_cotangent, normed, tables[0])
    )
    tables[0] = last
    tables.append(make_toeplitz(later, *modes[1][1:], deep))
    cot_all, normed_all = gather_two(cot_own, normed_own, n_grp)
    channel_in = lax.all_to_all(reduced, "seq", split_axis=0, concat_axis=1, tiled=True)
    seg = doc_row.astype(jnp.int32).reshape(blocks, TILE)
    signal = channel_in.reshape(-1, blocks, TILE)
    halves = [slice(0, half), slice(half, 2 * half)]
    convolve, sum_lags = (lone_conv, lone_taps) if lone(length) else (any_conv, taps_grad)
    channel_out = jnp.concatenate(
        [convolve(seg, signal[h], t[0], False) for h, t in zip(halves, tables)], axis=0
    ).reshape(-1, length)
    mixed = lax.all_to_all(channel_out, "seq", split_axis=1, concat_axis=0, tiled=True)
    pre_value = lax.dot_general(normed_all, value_part, contract_last, preferred_element_type=f32) + value_bias
    mixed, activated, slope = lax.optimization_barrier((mixed, *gelu_parts(pre_value)))
    mixed_all = jnp.concatenate(gather_grp(mixed, n_grp), axis=1)
    g_gated = jnp.dot(cot_all, out_part, preferred_element_type=f32)
    activated, slope, g_gated = lax.optimization_barrier((activated, slope, g_gated))
    pre_up = lax.dot_general(mixed_all, up_part, (((0,), (1,)), ((), ())), preferred_element_type=f32) + up_bias
    gated = (activated * pre_up).astype(bf16)
    g_activated = g_gated * pre_up
    g_pre_up = (g_gated * activated).astype(bf16)
    g_pre_value = (g_activated * slope).astype(bf16)

    g_mixed = lax.dot_general(up_part, g_pre_up, (((0,), (1,)), ((), ())), preferred_element_type=f32)
    g_mixed = sum_scatter_grp([g_mixed[:, k * tokens : (k + 1) * tokens] for k in range(n_grp)], n_grp)
    added = lax.dot_general(gated, out_part, contract_last, preferred_element_type=f32)
    g_normed = jnp.dot(g_pre_value, value_part, preferred_element_type=f32)
    added, g_normed = added.astype(bf16), g_normed.astype(bf16)
    g_mixed, gated, g_pre_up, g_pre_value, added, g_normed = lax.optimization_barrier(
        (g_mixed.astype(bf16), gated, g_pre_up, g_pre_value, added, g_normed)
    )
    g_channel = lax.all_to_all(g_mixed, "seq", split_axis=0, concat_axis=1, tiled=True)
    g_channel = g_channel.reshape(-1, blocks, TILE)
    g_out = lax.dot_general(cot_all, gated, contract_first, preferred_element_type=f32).astype(bf16)
    g_up = lax.dot_general(g_pre_up, mixed_all, (((0,), (1,)), ((), ())), preferred_element_type=f32)
    g_value = lax.dot_general(g_pre_value, normed_all, contract_first, preferred_element_type=f32)
    left = (jnp.arange(TILE) < TILE // 2).astype(bf16)
    ones = [jnp.broadcast_to(m, (g_pre_value.shape[0], TILE)) for m in (left, 1 - left)]
    g_biases = lax.dot_general(g_pre_value, ones[0], contract_first, preferred_element_type=f32)
    g_biases += lax.dot_general(g_pre_up, ones[1], contract_first, preferred_element_type=f32)
    g_both = jnp.concatenate([y.astype(bf16) for y in (g_value, g_up, g_biases)], axis=1)
    g_channel, g_out, g_both, added, g_normed = lax.optimization_barrier(
        (g_channel, g_out, g_both, added, g_normed)
    )
    g_out = lax.psum_scatter(g_out, "seq", scatter_dimension=0, tiled=True)
    g_both = lax.psum_scatter(g_both, "seq", scatter_dimension=0, tiled=True)
    g_signal = jnp.concatenate([convolve(seg, g_channel[h], t[0], True) for h, t in zip(halves, tables)], axis=0)
    g_signal, g_channel = lax.optimization_barrier((g_signal, g_channel))
    g_reduced = lax.all_to_all(g_signal.reshape(-1, length), "seq", split_axis=1, concat_axis=0, tiled=True)
    added, g_normed = sum_scatter_first(added, g_normed, n_grp)
    g_channel, added, g_normed = lax.optimization_barrier((g_channel, added, g_normed))
    g_taps = sum_lags(seg, signal, g_channel)
    added, g_normed = sum_scatter_second(added, g_normed, n_grp)
    g_taps, g_reduced, added, g_normed = lax.optimization_barrier((g_taps, g_reduced, added, g_normed))
    found = [mode_grads(*m, g_taps[h], *t[1:]) for h, m, t in zip(halves, modes, tables)]
    g_lam = found[0][2] + found[1][2]
    states = g_lam.shape[1]
    output = (x_wide + added + out_bias.reshape(-1).astype(f32)).astype(bf16)

    g_pre_reduce = (g_reduced.astype(f32) * reduce_slope).astype(bf16)
    g_reduce = jnp.dot(g_pre_reduce, normed, preferred_element_type=f32)
    g_normed = g_normed + lax.dot_general(g_pre_reduce, reduce_full, contract_first, preferred_element_type=f32)
    g_unit = g_normed * gain_wide
    g_input = inverse * (
        g_unit
        - jnp.mean(g_unit, axis=1, keepdims=True)
        - unit * jnp.mean(g_unit * unit, axis=1, keepdims=True)
    ) + out_cotangent.astype(f32)

    vectors = (
        jnp.sum(g_normed * unit, axis=0).reshape(n_seq, -1),
        jnp.sum(g_normed, axis=0).reshape(n_seq, -1),
        jnp.sum(g_pre_reduce.astype(f32), axis=1).reshape(n_seq, -1),
        g_lam[0].reshape(n_seq, -1),
        g_lam[1].reshape(n_seq, -1),
        jnp.sum(out_cotangent.astype(f32), axis=0).reshape(n_seq, -1),
    )
    flat = jnp.concatenate(vectors, axis=1)
    flat = jnp.pad(flat, ((0, 0), (0, -flat.shape[1] % wide))).reshape(n_seq, -1, wide)
    own = jnp.concatenate([g_reduce.reshape(n_seq, -1, wide).astype(bf16), flat.astype(bf16)], axis=1)
    own, g_out, g_both = lax.optimization_barrier((own, g_out, g_both))
    own = lax.psum_scatter(own, "seq", scatter_dimension=0, tiled=False)
    packed = [f[0][i].reshape(-1) for i in range(2) for f in found] + [f[1] for f in found]
    packed.append(jnp.zeros((-2 * half % wide,), f32))
    packed = jnp.concatenate(packed).reshape(-1, wide).astype(bf16)
    packed = sum_grp(packed, n_grp)
    own = sum_grp(own, n_grp)
    g_reduce, shard = own[: w_reduce.shape[0]], own[w_reduce.shape[0] :].reshape(-1)
    g_weights = packed[:-1].reshape(2, -1, states)
    g_step = packed[-1][: 2 * half]
    placed = place_grp(g_out, n_grp, me, 0)
    g_out = placed.reshape(n_grp, -1, n_seq, part).transpose(1, 2, 0, 3).reshape(w_out.shape).astype(f32)
    placed = place_grp(g_both, n_grp, me, 0).reshape(w_value.shape[0], -1).astype(f32)
    g_value, g_up = placed[:, :wide], placed[:, wide : wide + w_up.shape[1]]
    g_value_bias, g_up_bias = placed[:, wide + w_up.shape[1]], placed[:, -1]
    sums, spots = [], 0
    for array in vectors:
        sums.append(shard[spots : spots + array.shape[1]])
        spots += array.shape[1]
    g_gain, g_bias, g_reduce_bias, g_decay, g_freq, g_out_bias = sums
    return (
        output,
        g_input,
        g_gain,
        g_bias,
        g_value,
        g_value_bias,
        g_reduce,
        g_reduce_bias,
        g_decay,
        g_freq,
        g_weights,
        g_step,
        g_up,
        g_up_bias,
        g_out,
        g_out_bias,
    )


def solution(mesh):
    by_token = P(("grp", "seq"), None)
    row, matrix, cube = P("seq"), P("seq", None), P(None, "seq", None)
    layer = (row, row, matrix, row, matrix, row, row, row, cube, row, matrix, row, matrix, row)
    return jax.shard_map(
        functools.partial(body, mesh.shape["grp"], mesh.shape["seq"]),
        mesh=mesh,
        in_specs=(by_token, P("grp", "seq"), *layer, by_token),
        out_specs=(by_token, by_token, *layer),
        check_vma=False,
    )
```
